32 devices in a mesh: dp: 8 (over z, y), mp: 4 (over x, core).
Axes of the slice: x: 2, y: 2, z: 4, core: 2. Of those that a mesh axis runs over, the one named last changes fastest.
Arguments:
- tokens: bfloat16 [768, 64, 768], P('dp'), may hold values from -6 to 6
- visible_mask: int32 [768, 64], P('dp'), may hold values from 0 to 1, as said below
- cotangent: bfloat16 [768, 32, 768], P('dp', 'mp'), may hold values from -6 to 6
- qkv_weight: float32 [3, 768, 768], P(None, 'dp', 'mp'), may hold values from -0.21875 to 0.21875
- qkv_momentum: float32 [3, 768, 768], P(None, 'dp', 'mp'), may hold values from -384 to 384
- qkv_average: float32 [3, 768, 768], P(None, 'dp', 'mp'), may hold values from -0.21875 to 0.21875
- out_weight: float32 [768, 768], P('mp', 'dp'), may hold values from -0.875 to 0.875
- out_momentum: float32 [768, 768], P('mp', 'dp'), may hold values from -320 to 320
- out_average: float32 [768, 768], P('mp', 'dp'), may hold values from -0.875 to 0.875
- up_weight: float32 [768, 3072], P('dp', 'mp'), may hold values from -0.21875 to 0.21875
- up_momentum: float32 [768, 3072], P('dp', 'mp'), may hold values from -320 to 320
- up_average: float32 [768, 3072], P('dp', 'mp'), may hold values from -0.21875 to 0.21875
- down_weight: float32 [3072, 768], P('mp', 'dp'), may hold values from -0.15625 to 0.15625
- down_momentum: float32 [3072, 768], P('mp', 'dp'), may hold values from -448 to 448
- down_average: float32 [3072, 768], P('mp', 'dp'), may hold values from -0.15625 to 0.15625
- norm_params: float32 [4, 768], replicated, may hold values from -0.6 to 1.4
- norm_momentum: float32 [4, 768], replicated, may hold values from -768 to 768
- norm_average: float32 [4, 768], replicated, may hold values from -0.6 to 1.4
Outputs:
- block_out: float32 [768, 32, 768], P('dp', 'mp')
- input_grad: float32 [768, 32, 768], P('dp', 'mp')
- branch_rms: float32 [3], replicated
- qkv_moment: float32 [3, 768, 768], P(None, 'dp', 'mp')
- qkv_updated: float32 [3, 768, 768], P(None, 'dp', 'mp')
- qkv_smooth: float32 [3, 768, 768], P(None, 'dp', 'mp')
- qkv_copy: bfloat16 [3, 768, 768], P(None, 'dp', 'mp')
- out_moment: float32 [768, 768], P('mp', 'dp')
- out_updated: float32 [768, 768], P('mp', 'dp')
- out_smooth: float32 [768, 768], P('mp', 'dp')
- out_copy: bfloat16 [768, 768], P('mp', 'dp')
- up_moment: float32 [768, 3072], P('dp', 'mp')
- up_updated: float32 [768, 3072], P('dp', 'mp')
- up_smooth: float32 [768, 3072], P('dp', 'mp')
- up_copy: bfloat16 [768, 3072], P('dp', 'mp')
- down_moment: float32 [3072, 768], P('mp', 'dp')
- down_updated: float32 [3072, 768], P('mp', 'dp')
- down_smooth: float32 [3072, 768], P('mp', 'dp')
- down_copy: bfloat16 [3072, 768], P('mp', 'dp')
- norm_moment: float32 [4, 768], replicated
- norm_updated: float32 [4, 768], replicated
- norm_smooth: float32 [4, 768], replicated
- norm_copy: bfloat16 [4, 768], replicated
The draws below stay inside these ranges and needn't reach their ends.
Inputs may be any that keep to these rules, and one draw needn't show every extreme that they name: `visible_mask`: each row has exactly 32 ones or none. Within each aligned block of 96 slots the slots that hold fields come first; a block holds 32 to 96 fields, both reached, and all blocks together hold 512 fields.
All inputs are finite; a program needn't handle non-finite values.
Results may differ from the reference program's by a relative error of at most 0.018.
Values may be sent and summed in bfloat16 or wider, within the bound.
A program may use at most 192 MiB of HBM per device.

```python
import jax
import jax.numpy as jnp
from jax import lax

D = 768
HEADS = 12
HDIM = 64
FF = 3072
P_SIZE = 64
VIS = 32
FLD_DEV = 64
FMAX = 96
FIELDS = 768
N_DP = 8


def draw_visible_mask(key, part):
    key = jax.random.fold_in(key, 11)
    pair_key, perm_key = jax.random.split(key)
    device = jnp.arange(N_DP, dtype=jnp.int32)
    rising = FLD_DEV // 2 * device // (N_DP - 1)
    base_fields = FLD_DEV + rising - rising[::-1]
    pair_count = N_DP // 2 - 1
    jitter = jax.random.randint(pair_key, (pair_count,), -1, 2)
    first_side = (device % 2 == 1) & (device <= N_DP - 3)
    second_side = (device % 2 == 0) & (device >= 2) & (device <= N_DP - 2)
    first_pick = jnp.clip((device - 1) // 2, 0, pair_count - 1)
    second_pick = jnp.clip((device - 2) // 2, 0, pair_count - 1)
    fields_held = base_fields + jnp.where(first_side, jitter[first_pick], 0) - jnp.where(second_side, jitter[second_pick], 0)
    slot_ids = jnp.arange(N_DP * FMAX, dtype=jnp.int32)
    slot_live = slot_ids % FMAX < fields_held[slot_ids // FMAX]
    row_keys = jax.random.split(perm_key, N_DP * FMAX)
    patch_ranks = jax.vmap(lambda one_key: jax.random.permutation(one_key, P_SIZE))(row_keys)
    return ((patch_ranks < VIS) & slot_live[:, None]).astype(jnp.int32)


def gain_shift_rows(key):
    gain_key, shift_key = jax.random.split(key)
    gains = jax.random.uniform(gain_key, (2, D), jnp.float32, 0.6, 1.4)
    shifts = jax.random.uniform(shift_key, (2, D), jnp.float32, -0.6, 0.6)
    return jnp.stack([gains[0], shifts[0], gains[1], shifts[1]])


def draw_norm_params(key, part):
    key = jax.random.fold_in(key, 5)
    return gain_shift_rows(key)


def draw_norm_average(key, part):
    key = jax.random.fold_in(key, 7)
    return gain_shift_rows(key)


def steps_of(stream_key, extent, pieces, low, high):
    level = 1.0
    for axis_at, parts in pieces:
        draws = jax.random.uniform(jax.random.fold_in(jax.random.fold_in(stream_key, 6), axis_at), (parts,), jnp.float32, low / len(pieces), high / len(pieces))
        level = level * jnp.repeat(jnp.exp(draws), extent[axis_at] // parts).reshape((-1,) + (1,) * (len(extent) - 1 - axis_at))
    return level


def gaussian(own_key, extent, width, most, cuts=(), kind=jnp.bfloat16):
    level = steps_of(own_key, extent, cuts, -0.22, 0.18) if cuts else 1.0
    entries = jax.random.normal(own_key, extent, jnp.float32) * width * level
    return jnp.minimum(jnp.maximum(entries, -most), most).astype(kind)


def setup_inputs(seed: int = 0) -> dict:
    splits = jax.random.split(jax.random.key(seed), 19)
    tokens = gaussian(splits[0], (FIELDS, P_SIZE, D), 1.0, 6.0, ((0, 8),))
    visible_mask = draw_visible_mask(jax.random.fold_in(splits[18], 71), 0)
    cotangent = gaussian(splits[2], (FIELDS, VIS, D), 1.0, 6.0, ((0, 8), (1, 4)))
    qkv_weight = gaussian(splits[3], (3, D, D), D ** -0.5, 0.21875, ((1, 8), (2, 4)), jnp.float32)
    qkv_momentum = gaussian(splits[4], (3, D, D), (0.5 * (VIS * N_DP * FLD_DEV) ** 0.5), 384.0, ((1, 8), (2, 4)), jnp.float32)
    qkv_average = gaussian(splits[5], (3, D, D), D ** -0.5, 0.21875, ((1, 8), (2, 4)), jnp.float32)
    out_weight = gaussian(splits[6], (D, D), (D // 16) ** -0.5, 0.875, ((0, 4), (1, 8)), jnp.float32)
    out_momentum = gaussian(splits[7], (D, D), (0.4 * (VIS * N_DP * FLD_DEV) ** 0.5), 320.0, ((0, 4), (1, 8)), jnp.float32)
    out_average = gaussian(splits[8], (D, D), (D // 16) ** -0.5, 0.875, ((0, 4), (1, 8)), jnp.float32)
    up_weight = gaussian(splits[9], (D, FF), D ** -0.5, 0.21875, ((0, 8), (1, 4)), jnp.float32)
    up_momentum = gaussian(splits[10], (D, FF), (0.4 * (VIS * N_DP * FLD_DEV) ** 0.5), 320.0, ((0, 8), (1, 4)), jnp.float32)
    up_average = gaussian(splits[11], (D, FF), D ** -0.5, 0.21875, ((0, 8), (1, 4)), jnp.float32)
    down_weight = gaussian(splits[12], (FF, D), (FF // 2) ** -0.5, 0.15625, ((0, 4), (1, 8)), jnp.float32)
    down_momentum = gaussian(splits[13], (FF, D), (0.6 * (VIS * N_DP * FLD_DEV) ** 0.5), 448.0, ((0, 4), (1, 8)), jnp.float32)
    down_average = gaussian(splits[14], (FF, D), (FF // 2) ** -0.5, 0.15625, ((0, 4), (1, 8)), jnp.float32)
    norm_params = draw_norm_params(jax.random.fold_in(splits[18], 71), 0)
    norm_momentum = gaussian(splits[16], (4, D), (1.0 * (VIS * N_DP * FLD_DEV) ** 0.5), 768.0, (), jnp.float32)
    norm_average = draw_norm_average(jax.random.fold_in(splits[18], 71), 0)
    return {"tokens": tokens, "visible_mask": visible_mask, "cotangent": cotangent, "qkv_weight": qkv_weight, "qkv_momentum": qkv_momentum, "qkv_average": qkv_average, "out_weight": out_weight, "out_momentum": out_momentum, "out_average": out_average, "up_weight": up_weight, "up_momentum": up_momentum, "up_average": up_average, "down_weight": down_weight, "down_momentum": down_momentum, "down_average": down_average, "norm_params": norm_params, "norm_momentum": norm_momentum, "norm_average": norm_average}


FULL_PRECISION = lax.Precision.HIGHEST
NORM_EPS = 1e-06
MOMENTUM_RATE = 0.9
MATRIX_RATE = 4e-05
OUTPUT_RATE = 0.00025
NORM_RATE = 0.0003
AVERAGE_DECAY = 0.7

@jax.custom_vjp
def low(v):
    return lax.optimization_barrier(v.astype(jnp.bfloat16)).astype(jnp.float32)

@jax.custom_vjp
def low_back(v):
    return v

def low_keep(v):
    return (low(v), None)

def low_pass(kept, grad):
    return (grad,)

def back_keep(v):
    return (v, None)

def back_low(kept, grad):
    return (low(grad),)
low.defvjp(low_keep, low_pass)
low_back.defvjp(back_keep, back_low)

def layer_norm(row_values, norm_gain, norm_shift):
    center = row_values - lax.optimization_barrier(jnp.mean(row_values, axis=-1, keepdims=True))
    spread = lax.optimization_barrier(jnp.mean(center * center, axis=-1, keepdims=True))
    return center * lax.rsqrt(spread + NORM_EPS) * norm_gain + norm_shift

def gelu_exact(values):
    return jax.nn.gelu(values, approximate=False)

def renew_weight(weight, momentum, average, gradient, step_rate):
    moment = MOMENTUM_RATE * momentum + gradient
    updated = weight - step_rate * (gradient + MOMENTUM_RATE * moment)
    smooth = AVERAGE_DECAY * average + (1.0 - AVERAGE_DECAY) * updated
    return (moment, updated, smooth, updated.astype(jnp.bfloat16))

def attend(block_rows, w_qkv, w_out, w_up, w_down, norm_low):
    field_count = block_rows.shape[0] // VIS
    normed_in = low(layer_norm(block_rows, norm_low[0], norm_low[1]))
    qkv_rows = jnp.einsum('rd,tde->tre', normed_in, w_qkv, precision=FULL_PRECISION)
    qkv_rows = low_back(low(qkv_rows)).reshape(3, field_count, VIS, HEADS, HDIM)
    scores = jnp.einsum('fqhe,fkhe->fhqk', qkv_rows[0], qkv_rows[1], precision=FULL_PRECISION) * HDIM ** (-0.5)
    scores = low_back(scores)
    attention = low(jax.nn.softmax(scores, axis=-1))
    context = jnp.einsum('fhqk,fkhe->fqhe', attention, qkv_rows[2], precision=FULL_PRECISION).reshape(-1, D)
    context = low_back(low(context))
    attn_branch = low_back(jnp.dot(context, w_out, precision=FULL_PRECISION))
    middle = block_rows + attn_branch
    normed_mid = low(layer_norm(middle, norm_low[2], norm_low[3]))
    pre_act = low_back(jnp.dot(normed_mid, w_up, precision=FULL_PRECISION))
    gelu_out = low(gelu_exact(pre_act))
    mlp_branch = low_back(jnp.dot(gelu_out, w_down, precision=FULL_PRECISION))
    return (middle + mlp_branch, (attn_branch, mlp_branch))

def reference(tokens, visible_mask, cotangent, qkv_weight, qkv_momentum, qkv_average, out_weight, out_momentum, out_average, up_weight, up_momentum, up_average, down_weight, down_momentum, down_average, norm_params, norm_momentum, norm_average):
    patch_ids = jnp.arange(P_SIZE, dtype=jnp.int32)
    sort_keys = (1 - visible_mask) * P_SIZE + patch_ids[None, :]
    ranked = jnp.argsort(sort_keys, axis=1)[:, :VIS].astype(jnp.int32)
    visible = jnp.take_along_axis(tokens, ranked[:, :, None], axis=1).astype(jnp.float32)
    field_live = (lax.optimization_barrier(jnp.sum(visible_mask, axis=1)) > 0).astype(jnp.float32)[:, None, None]
    target = cotangent.astype(jnp.float32) * field_live
    params = (low(qkv_weight), low(out_weight), low(up_weight), low(down_weight), low(norm_params))
    live_rows = jnp.broadcast_to(field_live, (FIELDS, VIS, 1)).reshape(N_DP, FMAX * VIS, 1)
    blocks = (visible.reshape(N_DP, FMAX * VIS, D), target.reshape(N_DP, FMAX * VIS, D), live_rows)

    def one_block(carried, inputs):
        grad_sums, squares = carried
        block_rows, wanted, block_live = inputs
        result, pullback, branches = jax.vjp(attend, block_rows, *params, has_aux=True)
        pulled = pullback(wanted)
        grad_sums = tuple((running + addend for running, addend in zip(grad_sums, pulled[1:])))
        attn_branch, mlp_branch = branches
        out_rows = result * block_live
        squares = squares + jnp.stack([jnp.sum(attn_branch * attn_branch * block_live), jnp.sum(mlp_branch * mlp_branch * block_live), jnp.sum(out_rows * out_rows)])
        return ((grad_sums, squares), (out_rows, pulled[0] * block_live))
    start_sums = tuple((jnp.zeros(param.shape, jnp.float32) for param in params))
    (grad_sums, squares), (out_blocks, grad_blocks) = lax.scan(one_block, (start_sums, jnp.zeros((3,), jnp.float32)), blocks)
    block_out = out_blocks.reshape(FIELDS, VIS, D)
    input_grad = grad_blocks.reshape(FIELDS, VIS, D)
    branch_rms = jnp.sqrt(squares / (VIS * N_DP * FLD_DEV * D))
    qkv_new = renew_weight(qkv_weight, qkv_momentum, qkv_average, grad_sums[0], MATRIX_RATE)
    out_new = renew_weight(out_weight, out_momentum, out_average, grad_sums[1], OUTPUT_RATE)
    up_new = renew_weight(up_weight, up_momentum, up_average, grad_sums[2], MATRIX_RATE)
    down_new = renew_weight(down_weight, down_momentum, down_average, grad_sums[3], MATRIX_RATE)
    norm_new = renew_weight(norm_params, norm_momentum, norm_average, grad_sums[4], NORM_RATE)
    return (block_out, input_grad, branch_rms, qkv_new[0], qkv_new[1], qkv_new[2], qkv_new[3], out_new[0], out_new[1], out_new[2], out_new[3], up_new[0], up_new[1], up_new[2], up_new[3], down_new[0], down_new[1], down_new[2], down_new[3], norm_new[0], norm_new[1], norm_new[2], norm_new[3])
```

```python
import functools

import jax
import jax.numpy as jnp
from jax import lax
from jax.experimental import pallas as pl
from jax.experimental.pallas import tpu as pltpu
from jax.sharding import PartitionSpec as P

HDIM = 64
FLD_DEV = 64


NORM_EPS = 1e-06
MOMENTUM_RATE = 0.9
MATRIX_RATE = 4e-05
OUTPUT_RATE = 0.00025
NORM_RATE = 0.0003
AVERAGE_DECAY = 0.7


def layer_norm(row_values, norm_gain, norm_shift):
    center = row_values - jnp.mean(row_values, axis=-1, keepdims=True)
    spread = jnp.mean(center * center, axis=-1, keepdims=True)
    return center * lax.rsqrt(spread + NORM_EPS) * norm_gain + norm_shift


def gelu_exact(values):
    return jax.nn.gelu(values, approximate=False)


def renew_weight(weight, momentum, average, gradient, step_rate):
    moment = MOMENTUM_RATE * momentum + gradient
    updated = weight - step_rate * (gradient + MOMENTUM_RATE * moment)
    smooth = AVERAGE_DECAY * average + (1.0 - AVERAGE_DECAY) * updated
    return (moment, updated, smooth, updated.astype(jnp.bfloat16))


BF = jnp.bfloat16
F32 = jnp.float32
MESH_ID = pl.DeviceIdType.MESH
WIDE = 768
VMEM_BYTES = 63 * 1024 * 1024
ORDERS = (("zxy", 0, 64), ("zyx", 64, 96))
CHUNKS = ((0, 1, 0, 384), (0, 1, 384, 384), (1, 2, 0, 256), (1, 2, 256, 256), (1, 2, 512, 256))


def dot_nn(a, b):
    return jnp.dot(a, b, preferred_element_type=F32)


def dot_nt(a, b):
    return lax.dot_general(a, b, (((1,), (1,)), ((), ())), preferred_element_type=F32)


def dot_tn(a, b):
    return lax.dot_general(a, b, (((0,), (0,)), ((), ())), preferred_element_type=F32)


def gelu_pair(v):
    size = jnp.abs(v)
    bell = jnp.exp(v * v * -0.5)
    t = 1.0 / (1.0 + (0.3275911 * 0.7071067811865476) * size)
    poly = t * (
        0.254829592
        + t * (-0.284496736 + t * (1.421413741 + t * (-1.453152027 + t * 1.061405429)))
    )
    tail = 0.5 * poly * bell
    phi = jnp.where(v < 0.0, tail, 1.0 - tail)
    return v * phi, phi + v * bell * 0.3989422804014327


def lnorm(v, gain, shift):
    center = v - jnp.mean(v, axis=-1, keepdims=True)
    rs = lax.rsqrt(jnp.mean(center * center, axis=-1, keepdims=True) + NORM_EPS)
    return center * rs * gain + shift


def lnorm_back(v, e, gain):
    center = v - jnp.mean(v, axis=-1, keepdims=True)
    rs = lax.rsqrt(jnp.mean(center * center, axis=-1, keepdims=True) + NORM_EPS)
    xhat = center * rs
    eg = e * gain
    dv = rs * (
        eg - jnp.mean(eg, axis=-1, keepdims=True) - xhat * jnp.mean(eg * xhat, axis=-1, keepdims=True)
    )
    return dv, e * xhat


def layer_kernel(
    sizes,
    tok_hbm,
    mask_ref,
    cot_hbm,
    own_ref,
    norm_ref,
    gout_ref,
    bo_out,
    ig_out,
    stats_ref,
    G,
    PA,
    RSC,
    *rest,
):
    n_bufs = len(ORDERS) * 3
    RSB = rest[:n_bufs]
    (
        tok_s, key_s, live_s, band_s, x_s, nin_s, qkv_s, ctx_s, mid_s, nm_s, nmT_s,
        cot_s, dmT_s, g_s, d_s, mlp_s, dmn_s, dctx_s, st_send, st_recv,
        loc_sem, ag_send, ag_recv, rs_send, rs_recv, ex_send, ex_recv, st_ss, st_rs,
    ) = rest[n_bufs:]
    X, C, Z, Y = sizes
    dp = lax.axis_index("dp")
    mp = lax.axis_index("mp")
    me = {"z": lax.div(dp, Y), "y": lax.rem(dp, Y), "x": lax.div(mp, C), "c": lax.rem(mp, C)}
    size_of = {"x": X, "c": C, "z": Z, "y": Y}

    def device(**over):
        at = dict(me, **over)
        return (at["z"] * Y + at["y"], at["x"] * C + at["c"])

    def shifted(axis, delta):
        return lax.rem(me[axis] + delta, size_of[axis])

    def place(whole, **over):
        return tuple(slice(None) if a in whole else pl.ds(over.get(a, me[a]), 1) for a in "xczy")

    def remote(src, dst, ss, rs, dev):
        return pltpu.make_async_remote_copy(
            src_ref=src, dst_ref=dst, send_sem=ss, recv_sem=rs, device_id=dev, device_id_type=MESH_ID
        )

    def ag_copies(k, o, i):
        m0, nm, c0, nc = CHUNKS[k]
        if i == 3:
            part = G.at[(pl.ds(m0, nm),) + place("xzy") + (slice(None), pl.ds(c0, nc))]
            return [remote(part, part, ag_send.at[k, 0], ag_recv.at[k, 0], device(c=1 - me["c"]))]
        order, r0, r1 = ORDERS[o]
        axis = order[i]
        part = G.at[(pl.ds(m0, nm),) + place(order[:i]) + (pl.ds(r0, r1 - r0), pl.ds(c0, nc))]
        made = []
        for delta in range(1, size_of[axis]):
            at = 1 + o * 5 + sum(size_of[a] - 1 for a in order[:i]) + delta - 1
            made.append(
                remote(part, part, ag_send.at[k, at], ag_recv.at[k, at], device(**{axis: shifted(axis, delta)}))
            )
        return made

    def ag_step(k, step, orders=None):
        todo = range(len(ORDERS)) if orders is None else orders
        if step == 4:
            for c in ag_copies(k, 0, 3):
                c.wait_recv()
            return
        for o in todo:
            if step > 0:
                for c in ag_copies(k, o, step - 1):
                    c.wait_recv()
            if step < 3:
                for c in ag_copies(k, o, step):
                    c.start()
        if step == 3:
            for c in ag_copies(k, 0, 3):
                c.start()

    def ag_sent(k):
        for o in range(len(ORDERS)):
            for i in range(3):
                for c in ag_copies(k, o, i):
                    c.wait_send()
        for c in ag_copies(k, 0, 3):
            c.wait_send()

    def grads_of(k):
        return (PA, 0) if CHUNKS[k][0] == 0 else (G, CHUNKS[k][0])

    def rs_copies(k, o, i):
        m0, nm, c0, nc = CHUNKS[k]
        buf, b0 = grads_of(k)
        cols = pl.ds(c0, nc)
        if i == -1:
            src = buf.at[(pl.ds(b0, nm),) + place("xzy", c=1 - me["c"]) + (slice(None), cols)]
            dst = RSC.at[pl.ds(m0, nm), :, :, :, :, :, cols]
            return [remote(src, dst, rs_send.at[k, 0], rs_recv.at[k, 0], device(c=1 - me["c"]))]
        order, r0, r1 = ORDERS[o]
        back = order[::-1]
        axis, left = back[i], back[i + 1:]
        made = []
        for delta in range(1, size_of[axis]):
            at = 1 + o * 5 + sum(size_of[a] - 1 for a in back[:i]) + delta - 1
            to = shifted(axis, delta)
            src = buf.at[(pl.ds(b0, nm),) + place(left, **{axis: to}) + (pl.ds(r0, r1 - r0), cols)]
            dst = RSB[o * 3 + i].at[delta - 1, pl.ds(m0, nm), :, :, :, :, :, cols]
            made.append(remote(src, dst, rs_send.at[k, at], rs_recv.at[k, at], device(**{axis: to})))
        return made

    def rs_start(k, i, orders=None):
        if i == -1:
            for c in rs_copies(k, 0, -1):
                c.start()
            return
        for o in range(len(ORDERS)) if orders is None else orders:
            for c in rs_copies(k, o, i):
                c.start()

    def rs_add(k, i, orders=None):
        m0, nm, c0, nc = CHUNKS[k]
        buf, b0 = grads_of(k)
        cols = pl.ds(c0, nc)
        if i == -1:
            for c in rs_copies(k, 0, -1):
                c.wait_recv()
            jobs = [(RSC, None, "xzy", 0, 96, 1)]
        else:
            jobs = []
            for o in range(len(ORDERS)) if orders is None else orders:
                for c in rs_copies(k, o, i):
                    c.wait_recv()
                order, r0, r1 = ORDERS[o]
                back = order[::-1]
                jobs.append((RSB[o * 3 + i], o, back[i + 1:], r0, r1, size_of[back[i]] - 1))
        for came, o, left, r0, r1, deltas in jobs:
            nx, nz, ny = (size_of[a] if a in left else 1 for a in "xzy")

            def one(t, carry):
                mat = lax.div(t, nx * nz * ny)
                xi, zi, yi = lax.rem(lax.div(t, nz * ny), nx), lax.rem(lax.div(t, ny), nz), lax.rem(t, ny)
                at = (
                    b0 + mat,
                    xi if "x" in left else me["x"],
                    me["c"],
                    zi if "z" in left else me["z"],
                    yi if "y" in left else me["y"],
                    pl.ds(r0, r1 - r0),
                    cols,
                )
                total = buf[at].astype(F32)
                if o is None:
                    total = total + came[m0 + mat, xi, 0, zi, yi, :, cols].astype(F32)
                else:
                    for delta in range(deltas):
                        total = total + came[delta, m0 + mat, xi, 0, zi, yi, :, cols].astype(F32)
                if left == "":
                    gout_ref[m0 + mat, pl.ds(r0, r1 - r0), cols] = total
                else:
                    buf[at] = total.astype(BF)
                return carry

            lax.fori_loop(0, nm * nx * nz * ny, one, 0)

    def rs_sent(k):
        for c in rs_copies(k, 0, -1):
            c.wait_send()
        for o in range(len(ORDERS)):
            for i in range(3):
                for c in rs_copies(k, o, i):
                    c.wait_send()

    mates = [(0, 1), (1, 0), (1, 1)]

    def mate(j):
        dx, dc = mates[j]
        x2, c2 = lax.rem(me["x"] + dx, X), lax.rem(me["c"] + dc, C)
        return device(x=x2, c=c2), x2 * C + c2

    def exchange(which, src_of, dst):
        made = []
        for j in range(3):
            dev, index = mate(j)
            made.append(remote(src_of(index), dst, ex_send.at[which, j], ex_recv.at[which, j], dev))
        return made

    slab = pl.ds(pl.multiple_of(mp * 32, 32), 32)
    cot_copies = exchange(0, lambda t: cot_hbm.at[t], cot_s.at[:, slab, :])

    def rows_of(index):
        return pl.ds(pl.multiple_of(index * 32, 32), 32)

    bo_copies = exchange(1, lambda t: nm_s.at[:, rows_of(t), :], bo_out.at[mp])
    ig_copies = exchange(2, lambda t: cot_s.at[:, rows_of(t), :], ig_out.at[mp])
    cot_own = pltpu.make_async_copy(cot_hbm.at[mp], cot_s.at[:, slab, :], loc_sem.at[0])
    tok_copy = pltpu.make_async_copy(
        tok_hbm.at[pl.ds(pl.multiple_of(mp * 1536, 1536), 1536)], tok_s, loc_sem.at[1]
    )
    bo_own = pltpu.make_async_copy(nm_s.at[:, slab, :], bo_out.at[mp], loc_sem.at[2])
    ig_own = pltpu.make_async_copy(cot_s.at[:, slab, :], ig_out.at[mp], loc_sem.at[3])

    st_axes = "cyxz"

    def st_copies(i):
        axis = st_axes[i]
        return [
            remote(
                st_send.at[i], st_recv.at[i + delta - 1], st_ss.at[i + delta - 1], st_rs.at[i + delta - 1],
                device(**{axis: shifted(axis, delta)}),
            )
            for delta in range(1, size_of[axis])
        ]

    def st_step(i):
        if i == 0:
            total = stats_ref[...]
        else:
            copies = st_copies(i - 1)
            for c in copies:
                c.wait_recv()
            total = st_send[i - 1]
            for n in range(len(copies)):
                total = total + st_recv[i - 1 + n]
        if i < 4:
            st_send[i] = total
            for c in st_copies(i):
                c.start()
        else:
            stats_ref[...] = total

    low = norm_ref[...].astype(BF).astype(F32)
    gain_in, shift_in, gain_mid, shift_mid = (low[i:i + 1] for i in range(4))
    lane = lax.broadcasted_iota(jnp.int32, (1, 128), 1)
    lo = (lane < 64).astype(F32).astype(BF)
    hi = (lane >= 64).astype(F32).astype(BF)

    def weight(mat, m, c0, nc):
        m = jnp.int32(m)
        return G[mat, lax.div(m, C), lax.rem(m, C), :, :, :, pl.ds(c0, nc)].reshape(WIDE, nc)

    def put(buf, mat, m, c0, nc, value):
        m = jnp.int32(m)
        buf[mat, lax.div(m, C), lax.rem(m, C), :, :, :, pl.ds(c0, nc)] = value.reshape(Z, Y, 96, nc)

    def block(b):
        return pl.ds(pl.multiple_of(b * 128, 128), 128)

    def rows256(t):
        return pl.ds(pl.multiple_of(t * 256, 256), 256)

    def setup():
        col = lax.broadcasted_iota(jnp.int32, (256, 256), 1)
        row = lax.broadcasted_iota(jnp.int32, (256, 256), 0)
        tri = jnp.where((col // 64 == row // 64) & (row < col), 1.0, 0.0).astype(BF)
        marks = mask_ref[...].astype(F32)
        before = dot_nn(marks.astype(BF), tri)
        field = (lax.broadcasted_iota(jnp.int32, marks.shape, 1) // 64 * 64).astype(F32)
        key_s[...] = jnp.where(marks > 0.0, before + field, -1.0)
        ri = lax.broadcasted_iota(jnp.int32, (128, 128), 0) // 8 % 4
        ci = lax.broadcasted_iota(jnp.int32, (128, 128), 1) // 8 % 4
        band_s[...] = jnp.where(ri == ci, 0.0, -1e30)
        stats_ref[...] = jnp.zeros_like(stats_ref)

    def take_block(b, carry):
        ri = lax.broadcasted_iota(jnp.int32, (128, 256), 0)
        want = (ri // 8 % 4 * 64 + ri // 32 * 8 + ri % 8).astype(F32)
        pick = jnp.where(key_s[pl.ds(mp * 6 + b, 1), :] == want, 1.0, 0.0)
        live_s[block(b), :] = jnp.broadcast_to(jnp.sum(pick, axis=1, keepdims=True), (128, 128))
        x = dot_nn(pick.astype(BF), tok_s[pl.ds(pl.multiple_of(b * 256, 256), 256), :])
        x_s[block(b), :] = x.astype(BF)
        nin_s[block(b), :] = lnorm(x, gain_in, shift_in).astype(BF)
        return carry

    def qkv_first(m, carry):
        w = weight(0, m, 0, 384)
        for t in range(3):
            rows = pl.ds(t * 256, 256)
            qkv_s[m, rows, 0:384] = dot_nn(nin_s[rows, :], w).astype(BF)
        return carry

    def qkv_second(m, carry):
        w = weight(0, m, 384, 256)
        for t in range(3):
            rows = pl.ds(t * 256, 256)
            out = dot_nn(nin_s[rows, :], w)
            qkv_s[m, rows, 384:512] = out[:, :128].astype(BF)
            qkv_s[m, rows, 512:640] = pltpu.roll(out[:, :128], 64, 1).astype(BF)
            qkv_s[m, rows, 640:768] = pltpu.roll(out[:, 128:], 64, 1).astype(BF)
        return carry

    def keep_p(i, h, p):
        rows = pl.ds(pl.multiple_of(i * 64, 64), 64)
        tok_s[rows, h * 128:(h + 1) * 128] = p[:64]
        tok_s[rows, 384 + h * 128:512 + h * 128] = p[64:]

    def kept_p(i, h):
        rows = pl.ds(pl.multiple_of(i * 64, 64), 64)
        return jnp.concatenate(
            [tok_s[rows, h * 128:(h + 1) * 128], tok_s[rows, 384 + h * 128:512 + h * 128]], axis=0
        )

    def softmax(q, k):
        s = dot_nt(q, k) * 0.125 + band_s[...]
        e = jnp.exp(s - jnp.max(s, axis=1, keepdims=True))
        return (e / jnp.sum(e, axis=1, keepdims=True)).astype(BF)

    def attend_first(i, carry):
        m, b = lax.div(i, 6), lax.rem(i, 6)
        q, k, v = (qkv_s[m, block(b), n * 128:(n + 1) * 128] for n in range(3))
        p0 = softmax(q * lo, k)
        p1 = softmax(q * hi, k)
        keep_p(i, 0, p0)
        keep_p(i, 1, p1)
        ctx_s[m, block(b), 128:256] = (dot_nn(p0, v * lo) + dot_nn(p1, v * hi)).astype(BF)
        return carry

    def attend_second(i, carry):
        m, b = lax.div(i, 6), lax.rem(i, 6)
        q, k, v = (qkv_s[m, block(b), n * 128:(n + 1) * 128] for n in range(3, 6))
        p2 = softmax(q * lo, k)
        keep_p(i, 2, p2)
        ctx_s[m, block(b), 0:128] = dot_nn(p2, v * hi).astype(BF)
        return carry

    def mid_block(t, carry):
        rows = rows256(t)
        attn = dot_nt(ctx_s[0, rows, :], weight(0, 0, 512, 256))
        for m in range(1, X * C):
            attn = attn + dot_nt(ctx_s[m, rows, :], weight(0, m, 512, 256))
        live = live_s[rows, :][:, :1]
        stats_ref[4:5, :] += jnp.sum(attn * attn * live, axis=0, keepdims=True)
        mid = x_s[rows, :].astype(F32) + attn
        mid_s[rows, :] = mid
        nm_s[pl.ds(t * 2, 2)] = lnorm(mid, gain_mid, shift_mid).astype(BF).reshape(2, 128, WIDE)
        return carry

    def transpose_into(dst, src):
        def one(b, carry):
            part = src(b)
            for j in range(6):
                dst[pl.ds(j * 128, 128), block(b)] = part[:, j * 128:(j + 1) * 128].T
            return carry

        lax.fori_loop(0, 6, one, 0)

    def cot_block(b, carry):
        live = live_s[block(b), :][:, :1]
        cot_s[b] = (cot_s[b].astype(F32) * live).astype(BF)
        return carry

    def mlp_tile(q):
        c0 = q * 256

        def tile(m, carry):
            w_up = weight(1, m, c0, 256)
            w_down = weight(2, m, c0, 256)
            for t in range(3):
                rows = pl.ds(t * 256, 256)
                pre = dot_nn(nm_s[2 * t:2 * t + 2].reshape(256, WIDE), w_up)
                act, slope = gelu_pair(pre)
                act = act.astype(BF)
                d_pre = (dot_nn(cot_s[2 * t:2 * t + 2].reshape(256, WIDE), w_down) * slope).astype(BF)
                g_s[rows, :] = act
                d_s[rows, :] = d_pre
                mlp_s[rows, :] += dot_nt(act, w_down)
                dmn_s[rows, :] += dot_nt(d_pre, w_up)
            put(G, 2, m, c0, 256, dot_nn(dmT_s[...], g_s[...]).astype(BF))
            put(G, 1, m, c0, 256, dot_nn(nmT_s[...], d_s[...]).astype(BF))
            return carry

        return tile

    def end_block(b, carry):
        rows = block(b)
        live = live_s[rows, :][:, :1]
        mlp = mlp_s[rows, :]
        mid = mid_s[rows, :]
        out = (mid + mlp) * live
        stats_ref[5:6, :] += jnp.sum(mlp * mlp * live, axis=0, keepdims=True)
        stats_ref[6:7, :] += jnp.sum(out * out, axis=0, keepdims=True)
        nm_s[b] = out.astype(BF)
        e = dmn_s[rows, :]
        dv, ex = lnorm_back(mid, e, gain_mid)
        stats_ref[2:3, :] += jnp.sum(ex, axis=0, keepdims=True)
        stats_ref[3:4, :] += jnp.sum(e, axis=0, keepdims=True)
        d_mid = cot_s[b].astype(F32) + dv
        mlp_s[rows, :] = d_mid
        cot_s[b] = d_mid.astype(BF)
        return carry

    def dctx_tile(m, carry):
        w = weight(0, m, 512, 256)
        for t in range(3):
            rows = pl.ds(t * 256, 256)
            out = dot_nn(cot_s[2 * t:2 * t + 2].reshape(256, WIDE), w)
            dctx_s[rows, 0:256] = out.astype(BF)
            dctx_s[rows, 256:384] = pltpu.roll(out[:, :128], 64, 1).astype(BF)
        return carry

    def score_back(p, d_probs):
        pf = p.astype(F32)
        w = pf * d_probs
        return (w - pf * jnp.sum(w, axis=1, keepdims=True)).astype(BF)

    def attend_back(i, carry):
        m, b = lax.div(i, 6), lax.rem(i, 6)
        q, k, v, q2, k2, v2 = (qkv_s[m, block(b), n * 128:(n + 1) * 128] for n in range(6))
        d2, d01, d2r = (dctx_s[block(b), n * 128:(n + 1) * 128] for n in range(3))
        p0, p1, p2 = (kept_p(i, h) for h in range(3))
        s0 = score_back(p0, dot_nt(d01 * lo, v))
        s1 = score_back(p1, dot_nt(d01 * hi, v))
        s2 = score_back(p2, dot_nt(d2 * hi, v2))
        dq = dot_nn(s0, k * lo) + dot_nn(s1, k * hi)
        dk = dot_tn(s0, q * lo) + dot_tn(s1, q * hi)
        dv = dot_tn(p0, d01 * lo) + dot_tn(p1, d01 * hi)
        dqk2 = dot_nn(s2, k2 * lo) + dot_tn(s2, k2 * hi)
        dv2 = dot_tn(p2, d2r * lo)
        for n, out in enumerate((dq * 0.125, dk * 0.125, dv, dqk2 * 0.125, dv2)):
            qkv_s[m, block(b), n * 128:(n + 1) * 128] = out.astype(BF)
        return carry

    def put_all(m, c0, nc, value):
        put(PA, 0, m, c0, nc, value)

    def grad_a0(m, carry):
        put_all(m, 0, 384, dot_nn(nmT_s[...], qkv_s[m, :, 0:384]).astype(BF))
        return carry

    def grad_a1(m, carry):
        out_part = dot_nn(dmT_s[...], ctx_s[m])
        qkv_part = dot_nn(nmT_s[...], qkv_s[m, :, 384:640])
        put_all(m, 384, 128, qkv_part[:, :128].astype(BF))
        put_all(m, 512, 128, (qkv_part[:, 128:] + out_part[:, :128]).astype(BF))
        put_all(m, 640, 128, out_part[:, 128:].astype(BF))
        return carry

    def in_block(t, carry):
        rows = rows256(t)
        e = dot_nt(qkv_s[0, rows, 0:640], weight(0, 0, 0, 640))
        for m in range(1, X * C):
            e = e + dot_nt(qkv_s[m, rows, 0:640], weight(0, m, 0, 640))
        dv, ex = lnorm_back(x_s[rows, :].astype(F32), e, gain_in)
        stats_ref[0:1, :] += jnp.sum(ex, axis=0, keepdims=True)
        stats_ref[1:2, :] += jnp.sum(e, axis=0, keepdims=True)
        live = live_s[rows, :][:, :1]
        out = (mlp_s[rows, :] + dv) * live
        cot_s[pl.ds(t * 2, 2)] = out.astype(BF).reshape(2, 128, WIDE)
        return carry

    def loop(first, last, body):
        lax.fori_loop(first, last, body, 0)

    tok_copy.start()
    cot_own.start()
    G[(slice(None),) + (me["x"], me["c"], me["z"], me["y"])] = own_ref[...]
    barrier = pltpu.get_barrier_semaphore()
    greet = [device(c=1 - me["c"]), device(y=1 - me["y"]), device(x=1 - me["x"]),
             device(x=1 - me["x"], c=1 - me["c"])]
    greet += [device(z=shifted("z", n)) for n in range(1, Z)]
    for dev in greet:
        pl.semaphore_signal(barrier, inc=1, device_id=dev, device_id_type=MESH_ID)
    pl.semaphore_wait(barrier, len(greet))

    ag_step(0, 0)
    ag_step(1, 0)
    for c in cot_copies:
        c.start()
    ag_step(2, 0)
    setup()
    tok_copy.wait()
    loop(0, 6, take_block)
    ag_step(0, 1)
    ag_step(0, 2)
    ag_step(1, 1)
    ag_step(3, 0)
    ag_step(0, 3)
    ag_step(1, 2)
    ag_step(0, 4)
    loop(0, 4, qkv_first)
    ag_step(2, 1)
    ag_step(1, 3)
    loop(0, 12, attend_first)
    ag_step(2, 2)
    ag_step(4, 0)
    ag_step(3, 1)
    loop(12, 24, attend_first)
    ag_step(1, 4)
    loop(0, 4, qkv_second)
    loop(0, 24, attend_second)
    ag_step(2, 3)
    cot_own.wait()
    for c in cot_copies:
        c.wait_recv()
    loop(0, 6, cot_block)
    transpose_into(dmT_s, lambda b: cot_s[b])
    mlp_s[...] = jnp.zeros_like(mlp_s)
    dmn_s[...] = jnp.zeros_like(dmn_s)
    loop(0, 3, mid_block)
    transpose_into(nmT_s, lambda b: nm_s[b])
    ag_step(3, 2)
    ag_step(2, 4)
    ag_sent(2)

    tile = mlp_tile(0)
    loop(0, 1, tile)
    ag_step(4, 1)
    loop(1, 2, tile)
    ag_step(3, 3)
    loop(2, 4, tile)
    ag_step(3, 4)
    ag_sent(3)
    rs_start(2, -1)

    tile = mlp_tile(1)
    loop(0, 1, tile)
    ag_step(4, 2)
    rs_add(2, -1)
    rs_start(2, 0)
    loop(1, 2, tile)
    ag_step(4, 3)
    loop(2, 3, tile)
    rs_add(2, 0)
    rs_start(2, 1)
    loop(3, 4, tile)
    ag_step(4, 4)
    ag_sent(4)
    rs_start(3, -1)

    tile = mlp_tile(2)
    loop(0, 1, tile)
    rs_add(3, -1)
    rs_start(3, 0)
    loop(1, 2, tile)
    rs_add(2, 1)
    rs_start(2, 2)
    loop(2, 3, tile)
    rs_add(3, 0)
    rs_start(3, 1)
    loop(3, 4, tile)
    rs_start(4, -1)

    loop(0, 6, end_block)
    for c in bo_copies:
        c.start()
    bo_own.start()
    rs_add(4, -1)
    rs_start(4, 0)
    transpose_into(dmT_s, lambda b: cot_s[b])
    transpose_into(nmT_s, lambda b: nin_s[block(b), :])
    loop(0, 1, dctx_tile)
    loop(0, 6, attend_back)
    rs_add(3, 1)
    rs_start(3, 2)
    loop(1, 2, dctx_tile)
    loop(6, 12, attend_back)
    rs_add(2, 2)
    loop(2, 3, dctx_tile)
    loop(12, 18, attend_back)
    rs_add(4, 0)
    rs_start(4, 1)
    loop(3, 4, dctx_tile)
    loop(18, 24, attend_back)
    loop(0, 4, grad_a0)
    rs_start(0, -1)
    loop(0, 4, grad_a1)
    rs_add(0, -1)
    rs_start(0, 0)
    rs_start(1, -1)
    rs_add(4, 1)
    rs_start(4, 2)
    rs_add(3, 2)
    loop(0, 3, in_block)
    for c in ig_copies:
        c.start()
    ig_own.start()
    rs_add(1, -1)
    rs_start(1, 0)
    st_step(0)
    rs_add(0, 0)
    rs_start(0, 1)
    st_step(1)
    rs_add(4, 2)
    rs_add(1, 0)
    rs_start(1, 1)
    st_step(2)
    rs_add(0, 1)
    rs_start(0, 2)
    st_step(3)
    rs_add(1, 1)
    rs_start(1, 2)
    st_step(4)
    rs_add(0, 2)
    rs_add(1, 2)

    ag_sent(0)
    ag_sent(1)
    for k in range(len(CHUNKS)):
        rs_sent(k)
    for c in cot_copies:
        c.wait_send()
    for c in (*bo_copies, *ig_copies):
        c.wait()
    bo_own.wait()
    ig_own.wait()
    for i in range(4):
        for c in st_copies(i):
            c.wait_send()


def fits_fused(mesh):
    return mesh.shape["dp"] == 8 and mesh.shape["mp"] == 4


def local_fused(
    tokens,
    visible_mask,
    cotangent,
    qkv_weight,
    qkv_momentum,
    qkv_average,
    out_weight,
    out_momentum,
    out_average,
    up_weight,
    up_momentum,
    up_average,
    down_weight,
    down_momentum,
    down_average,
    norm_params,
    norm_momentum,
    norm_average,
):
    data_size = lax.axis_size("dp")
    model_size = lax.axis_size("mp")
    slots, patches, width = tokens.shape
    quarter = cotangent.shape[1]
    sizes = (model_size // 2, 2, data_size // 2, 2)
    X, C, Z, Y = sizes
    out_t = out_weight.T
    first = jnp.concatenate(
        [qkv_weight[0, :, :128], qkv_weight[1, :, :128], qkv_weight[2, :, :128]]
        + [qkv_weight[0, :, 128:], qkv_weight[1, :, 128:], qkv_weight[2, :, 128:]]
        + [out_t[:, 128:], out_t[:, :128]],
        axis=1,
    )
    own = jnp.stack([first, up_weight, down_weight.T]).astype(BF)
    blocks = slots // (4 * model_size)
    group = blocks * 32
    bufs = []
    for order, r0, r1 in ORDERS:
        back = order[::-1]
        for i in range(3):
            left = back[i + 1:]
            dims = tuple({"x": X, "z": Z, "y": Y}[a] if a in left else 1 for a in "xzy")
            count = {"x": X, "z": Z, "y": Y}[back[i]] - 1
            bufs.append(pltpu.VMEM((count, 3, dims[0], 1, dims[1], dims[2], r1 - r0, WIDE), BF))
    n_chunk, n_ag = len(CHUNKS), 1 + 5 * len(ORDERS)
    rows = blocks * 128
    vmem = pltpu.VMEM
    dma = pltpu.SemaphoreType.DMA
    scratch = [
        vmem((3, X, C, Z, Y, 96, WIDE), BF),
        vmem((1, X, C, Z, Y, 96, WIDE), BF),
        vmem((3, X, 1, Z, Y, 96, WIDE), BF),
        *bufs,
        vmem((24 * patches, WIDE), BF),
        vmem((24, 256), F32),
        vmem((rows, 128), F32),
        vmem((128, 128), F32),
        vmem((rows, WIDE), BF),
        vmem((rows, WIDE), BF),
        vmem((4, rows, WIDE), BF),
        vmem((4, rows, 256), BF),
        vmem((rows, WIDE), F32),
        vmem((blocks, 128, WIDE), BF),
        vmem((WIDE, rows), BF),
        vmem((blocks, 128, WIDE), BF),
        vmem((WIDE, rows), BF),
        vmem((rows, 256), BF),
        vmem((rows, 256), BF),
        vmem((rows, WIDE), F32),
        vmem((rows, WIDE), F32),
        vmem((rows, 384), BF),
        vmem((4, 8, WIDE), F32),
        vmem((6, 8, WIDE), F32),
        dma((4,)),
        dma((n_chunk, n_ag)),
        dma((n_chunk, n_ag)),
        dma((n_chunk, n_ag)),
        dma((n_chunk, n_ag)),
        dma((3, 3)),
        dma((3, 3)),
        dma((6,)),
        dma((6,)),
    ]
    in_vmem = pl.BlockSpec(memory_space=pltpu.VMEM)
    anywhere = pl.BlockSpec(memory_space=pl.ANY)
    grads, bo, ig, stats = pl.pallas_call(
        functools.partial(layer_kernel, sizes),
        out_shape=(
            jax.ShapeDtypeStruct((3, 96, WIDE), F32),
            jax.ShapeDtypeStruct((model_size, blocks, 32, WIDE), BF),
            jax.ShapeDtypeStruct((model_size, blocks, 32, WIDE), BF),
            jax.ShapeDtypeStruct((8, WIDE), F32),
        ),
        in_specs=[anywhere, in_vmem, anywhere, in_vmem, in_vmem],
        out_specs=(in_vmem, anywhere, anywhere, in_vmem),
        scratch_shapes=scratch,
        compiler_params=pltpu.CompilerParams(
            collective_id=0, has_side_effects=True, vmem_limit_bytes=VMEM_BYTES
        ),
        name="layer",
    )(
        tokens.reshape(slots * patches, width),
        visible_mask.reshape(slots // 4, 4 * patches),
        cotangent.reshape(model_size, blocks, 32, width),
        own,
        norm_params,
    )
    block_out = bo.astype(F32).reshape(slots, quarter, width)
    input_grad = ig.astype(F32).reshape(slots, quarter, width)
    totals = jnp.sum(stats[4:7], axis=1)
    visible_count = quarter * model_size
    branch_rms = jnp.sqrt(totals / (visible_count * data_size * FLD_DEV * width))
    a = grads[0]
    qkv_grad = jnp.stack(
        [jnp.concatenate([a[:, 128 * t:128 * t + 128], a[:, 384 + 64 * t:448 + 64 * t]], axis=1) for t in range(3)]
    )
    out_grad = jnp.concatenate([a[:, 640:768], a[:, 576:640]], axis=1).T
    qkv_new = renew_weight(qkv_weight, qkv_momentum, qkv_average, qkv_grad, MATRIX_RATE)
    out_new = renew_weight(out_weight, out_momentum, out_average, out_grad, OUTPUT_RATE)
    up_new = renew_weight(up_weight, up_momentum, up_average, grads[1], MATRIX_RATE)
    down_new = renew_weight(down_weight, down_momentum, down_average, grads[2].T, MATRIX_RATE)
    norm_new = renew_weight(norm_params, norm_momentum, norm_average, stats[:4], NORM_RATE)
    return (block_out, input_grad, branch_rms, *qkv_new, *out_new, *up_new, *down_new, *norm_new)


def local_general(
    tokens,
    visible_mask,
    cotangent,
    qkv_weight,
    qkv_momentum,
    qkv_average,
    out_weight,
    out_momentum,
    out_average,
    up_weight,
    up_momentum,
    up_average,
    down_weight,
    down_momentum,
    down_average,
    norm_params,
    norm_momentum,
    norm_average,
):
    data_size = lax.axis_size("dp")
    model_size = lax.axis_size("mp")
    data_rank = lax.axis_index("dp")
    model_rank = lax.axis_index("mp")
    slot_count, patch_count, feature_count = tokens.shape
    quarter = cotangent.shape[1]
    visible_count = quarter * model_size
    capacity = (slot_count + data_size - 1) // data_size
    owned_fields = FLD_DEV
    pad_total = data_size * capacity
    per_field = jnp.sum(visible_mask, axis=1)
    field_total = jnp.sum(per_field) // visible_count
    all_fields = lax.all_gather(field_total.reshape(1), "dp", axis=0, tiled=True)
    firsts = jnp.cumsum(all_fields) - all_fields
    my_first = firsts[data_rank]
    patch_ids = jnp.arange(patch_count, dtype=jnp.int32)
    sort_keys = (1 - visible_mask) * patch_count + patch_ids[None, :]
    ranked = jnp.argsort(sort_keys, axis=1)
    my_order = lax.dynamic_slice_in_dim(ranked, model_rank * quarter, quarter, 1)
    visible = jnp.take_along_axis(tokens, my_order[:, :, None], axis=1)
    owner_ids = jnp.arange(data_size, dtype=jnp.int32)[:, None]
    slot_ids = jnp.arange(capacity, dtype=jnp.int32)[None, :]
    source_field = slot_ids * data_size + (owner_ids - my_first) % data_size
    send_live = (source_field < field_total).reshape(-1)[:, None, None]
    source_pick = jnp.minimum(source_field, slot_count - 1).reshape(-1)
    sent_rows = jnp.where(send_live, visible[source_pick], jnp.zeros((), jnp.bfloat16))
    sent_grads = jnp.where(send_live, cotangent[source_pick], jnp.zeros((), jnp.bfloat16))
    got_rows, got_grads = (
        lax.all_to_all(sent_rows, "dp", split_axis=0, concat_axis=0, tiled=True),
        lax.all_to_all(sent_grads, "dp", split_axis=0, concat_axis=0, tiled=True),
    )
    arrive = slot_ids * data_size + (data_rank - firsts[:, None]) % data_size
    flat_live = (arrive < all_fields[:, None]).reshape(-1)
    order_keys = jnp.where(flat_live, 0, pad_total) + jnp.arange(pad_total, dtype=jnp.int32)
    chosen = jnp.argsort(order_keys)[:owned_fields]
    share_rows = owned_fields * quarter
    mine_rows = got_rows[chosen].reshape(share_rows, feature_count)
    mine_grads = got_grads[chosen].reshape(share_rows, feature_count)
    w_qkv, w_out, w_up, w_down = (
        lax.all_gather(qkv_weight.astype(jnp.bfloat16), "dp", axis=1, tiled=True),
        lax.all_gather(out_weight.astype(jnp.bfloat16), "dp", axis=1, tiled=True),
        lax.all_gather(up_weight.astype(jnp.bfloat16), "dp", axis=0, tiled=True),
        lax.all_gather(down_weight.astype(jnp.bfloat16), "dp", axis=1, tiled=True),
    )
    norm_low = lax.optimization_barrier(norm_params.astype(jnp.bfloat16)).astype(jnp.float32)
    total_rows = share_rows * model_size
    local_width = w_qkv.shape[2]
    head_local = local_width // HDIM
    score_scale = HDIM ** (-0.5)
    x_share = mine_rows.astype(jnp.float32)
    normed_share, norm_in_back = jax.vjp(layer_norm, x_share, norm_low[0], norm_low[1])
    normed_all = lax.all_gather(normed_share.astype(jnp.bfloat16), "mp", axis=0, tiled=True)
    qkv_rows = jnp.einsum(
        "rd,tde->tre", normed_all, w_qkv, preferred_element_type=jnp.float32
    ).astype(jnp.bfloat16)
    qkv_six = qkv_rows.reshape(3, model_size, owned_fields, quarter, head_local, HDIM)
    queries = qkv_six[0]
    key_rows = qkv_six[1]
    values = qkv_six[2]
    scores = (
        jnp.einsum("afbhe,cfdhe->fhabcd", queries, key_rows, preferred_element_type=jnp.float32)
        * score_scale
    )
    scores = scores.reshape(owned_fields, head_local, visible_count, visible_count)
    attention = jax.nn.softmax(scores, axis=-1)
    att_six = attention.astype(jnp.bfloat16).reshape(
        owned_fields, head_local, model_size, quarter, model_size, quarter
    )
    context = jnp.einsum("fhabcd,cfdhe->afbhe", att_six, values, preferred_element_type=jnp.float32)
    context = context.astype(jnp.bfloat16).reshape(total_rows, local_width)
    attn_share = lax.psum_scatter(
        jnp.dot(context, w_out, preferred_element_type=jnp.float32).astype(jnp.bfloat16),
        "mp",
        scatter_dimension=0,
        tiled=True,
    ).astype(jnp.float32)
    mid_share = x_share + attn_share
    normed_mid, norm_mid_back = jax.vjp(layer_norm, mid_share, norm_low[2], norm_low[3])
    mid_all, grad_all = (
        lax.all_gather(normed_mid.astype(jnp.bfloat16), "mp", axis=0, tiled=True),
        lax.all_gather(mine_grads, "mp", axis=0, tiled=True),
    )
    pre_act = jnp.dot(mid_all, w_up, preferred_element_type=jnp.float32)
    gelu_float, gelu_back = jax.vjp(gelu_exact, pre_act)
    gelu_out = gelu_float.astype(jnp.bfloat16)
    mlp_share = lax.psum_scatter(
        jnp.dot(gelu_out, w_down, preferred_element_type=jnp.float32).astype(jnp.bfloat16),
        "mp",
        scatter_dimension=0,
        tiled=True,
    ).astype(jnp.float32)
    out_share = mid_share + mlp_share
    squares = jnp.stack(
        [
            jnp.sum(attn_share * attn_share),
            jnp.sum(mlp_share * mlp_share),
            jnp.sum(out_share * out_share),
        ]
    )
    grad_down = jnp.einsum("rf,rd->fd", gelu_out, grad_all, preferred_element_type=jnp.float32)
    d_act = jnp.einsum("rd,fd->rf", grad_all, w_down, preferred_element_type=jnp.float32)
    d_pre = gelu_back(d_act)[0].astype(jnp.bfloat16)
    grad_up = jnp.einsum("rd,rf->df", mid_all, d_pre, preferred_element_type=jnp.float32)
    d_mid_norm = lax.psum_scatter(
        jnp.einsum("rf,df->rd", d_pre, w_up, preferred_element_type=jnp.float32).astype(
            jnp.bfloat16
        ),
        "mp",
        scatter_dimension=0,
        tiled=True,
    ).astype(jnp.float32)
    d_mid_part, grad_gain_mid, grad_shift_mid = norm_mid_back(d_mid_norm)
    d_middle = mine_grads.astype(jnp.float32) + d_mid_part
    d_att_all = lax.all_gather(d_middle.astype(jnp.bfloat16), "mp", axis=0, tiled=True)
    grad_out = jnp.einsum("rc,rd->cd", context, d_att_all, preferred_element_type=jnp.float32)
    d_context = jnp.einsum(
        "rd,cd->rc", d_att_all, w_out, preferred_element_type=jnp.float32
    ).astype(jnp.bfloat16)
    d_ctx_six = d_context.reshape(model_size, owned_fields, quarter, head_local, HDIM)
    d_probs = jnp.einsum(
        "afbhe,cfdhe->fhabcd", d_ctx_six, values, preferred_element_type=jnp.float32
    )
    d_probs = d_probs.reshape(owned_fields, head_local, visible_count, visible_count)
    d_values = jnp.einsum(
        "fhabcd,afbhe->cfdhe", att_six, d_ctx_six, preferred_element_type=jnp.float32
    )
    d_scores = (
        attention * (d_probs - jnp.sum(d_probs * attention, axis=-1, keepdims=True))
    ).astype(jnp.bfloat16)
    d_six = d_scores.reshape(owned_fields, head_local, model_size, quarter, model_size, quarter)
    d_queries = (
        jnp.einsum("fhabcd,cfdhe->afbhe", d_six, key_rows, preferred_element_type=jnp.float32)
        * score_scale
    )
    d_keys = (
        jnp.einsum("fhabcd,afbhe->cfdhe", d_six, queries, preferred_element_type=jnp.float32)
        * score_scale
    )
    d_qkv = (
        jnp.stack([d_queries, d_keys, d_values])
        .astype(jnp.bfloat16)
        .reshape(3, total_rows, local_width)
    )
    grad_qkv = jnp.einsum("rd,tre->tde", normed_all, d_qkv, preferred_element_type=jnp.float32)
    d_in_norm = lax.psum_scatter(
        jnp.einsum("tre,tde->rd", d_qkv, w_qkv, preferred_element_type=jnp.float32).astype(
            jnp.bfloat16
        ),
        "mp",
        scatter_dimension=0,
        tiled=True,
    ).astype(jnp.float32)
    d_in_part, grad_gain_in, grad_shift_in = norm_in_back(d_in_norm)
    d_input = d_middle + d_in_part
    gradients = (grad_qkv, grad_out, grad_up, grad_down)
    summed = lax.psum((gradients[0], gradients[1], gradients[2], gradients[3]), "dp")
    qkv_grad = lax.dynamic_slice_in_dim(
        summed[0], data_rank * qkv_weight.shape[1], qkv_weight.shape[1], 1
    )
    out_grad = lax.dynamic_slice_in_dim(
        summed[1], data_rank * out_weight.shape[1], out_weight.shape[1], 1
    )
    up_grad = lax.dynamic_slice_in_dim(
        summed[2], data_rank * up_weight.shape[0], up_weight.shape[0], 0
    )
    down_grad = lax.dynamic_slice_in_dim(
        summed[3], data_rank * down_weight.shape[1], down_weight.shape[1], 1
    )

    def spread_back(share_block):
        padded = jnp.zeros((pad_total, quarter, feature_count), jnp.float32)
        return padded.at[chosen].set(share_block.reshape(owned_fields, quarter, feature_count))

    back_out, back_grad = (
        lax.all_to_all(
            spread_back(out_share).astype(jnp.bfloat16),
            "dp",
            split_axis=0,
            concat_axis=0,
            tiled=True,
        ).astype(jnp.float32),
        lax.all_to_all(
            spread_back(d_input).astype(jnp.bfloat16), "dp", split_axis=0, concat_axis=0, tiled=True
        ).astype(jnp.float32),
    )
    field_ids = jnp.arange(slot_count, dtype=jnp.int32)
    home_slot = (my_first + field_ids) % data_size * capacity + field_ids // data_size
    field_live = (field_ids < field_total)[:, None, None]
    block_out = jnp.where(field_live, back_out[home_slot], 0.0)
    input_grad = jnp.where(field_live, back_grad[home_slot], 0.0)
    norm_grad = jnp.stack([grad_gain_in, grad_shift_in, grad_gain_mid, grad_shift_mid])
    totals, norm_grad = lax.psum((squares, norm_grad), ("dp", "mp"))
    branch_rms = jnp.sqrt(totals / (visible_count * data_size * FLD_DEV * feature_count))
    qkv_new = renew_weight(qkv_weight, qkv_momentum, qkv_average, qkv_grad, MATRIX_RATE)
    out_new = renew_weight(out_weight, out_momentum, out_average, out_grad, OUTPUT_RATE)
    up_new = renew_weight(up_weight, up_momentum, up_average, up_grad, MATRIX_RATE)
    down_new = renew_weight(down_weight, down_momentum, down_average, down_grad, MATRIX_RATE)
    norm_new = renew_weight(norm_params, norm_momentum, norm_average, norm_grad, NORM_RATE)
    return (
        block_out,
        input_grad,
        branch_rms,
        qkv_new[0],
        qkv_new[1],
        qkv_new[2],
        qkv_new[3],
        out_new[0],
        out_new[1],
        out_new[2],
        out_new[3],
        up_new[0],
        up_new[1],
        up_new[2],
        up_new[3],
        down_new[0],
        down_new[1],
        down_new[2],
        down_new[3],
        norm_new[0],
        norm_new[1],
        norm_new[2],
        norm_new[3],
    )


def solution(mesh):
    in_specs = (
        P("dp", None, None),
        P("dp", None),
        P("dp", "mp", None),
        P(None, "dp", "mp"),
        P(None, "dp", "mp"),
        P(None, "dp", "mp"),
        P("mp", "dp"),
        P("mp", "dp"),
        P("mp", "dp"),
        P("dp", "mp"),
        P("dp", "mp"),
        P("dp", "mp"),
        P("mp", "dp"),
        P("mp", "dp"),
        P("mp", "dp"),
        P(),
        P(),
        P(),
    )
    out_specs = (
        P("dp", "mp", None),
        P("dp", "mp", None),
        P(),
        P(None, "dp", "mp"),
        P(None, "dp", "mp"),
        P(None, "dp", "mp"),
        P(None, "dp", "mp"),
        P("mp", "dp"),
        P("mp", "dp"),
        P("mp", "dp"),
        P("mp", "dp"),
        P("dp", "mp"),
        P("dp", "mp"),
        P("dp", "mp"),
        P("dp", "mp"),
        P("mp", "dp"),
        P("mp", "dp"),
        P("mp", "dp"),
        P("mp", "dp"),
        P(),
        P(),
        P(),
        P(),
    )
    local = local_fused if fits_fused(mesh) else local_general
    return jax.shard_map(local, mesh=mesh, in_specs=in_specs, out_specs=out_specs, check_vma=False)
```

```python
import functools

import jax
import jax.numpy as jnp
from jax import lax
from jax.experimental import pallas as pl
from jax.experimental.pallas import tpu as pltpu
from jax.sharding import PartitionSpec as P

HDIM = 64
FLD_DEV = 64


NORM_EPS = 1e-06
MOMENTUM_RATE = 0.9
MATRIX_RATE = 4e-05
OUTPUT_RATE = 0.00025
NORM_RATE = 0.0003
AVERAGE_DECAY = 0.7


def layer_norm(row_values, norm_gain, norm_shift):
    center = row_values - jnp.mean(row_values, axis=-1, keepdims=True)
    spread = jnp.mean(center * center, axis=-1, keepdims=True)
    return center * lax.rsqrt(spread + NORM_EPS) * norm_gain + norm_shift


def gelu_exact(values):
    return jax.nn.gelu(values, approximate=False)


def renew_weight(weight, momentum, average, gradient, step_rate):
    moment = MOMENTUM_RATE * momentum + gradient
    updated = weight - step_rate * (gradient + MOMENTUM_RATE * moment)
    smooth = AVERAGE_DECAY * average + (1.0 - AVERAGE_DECAY) * updated
    return (moment, updated, smooth, updated.astype(jnp.bfloat16))


BF = jnp.bfloat16
F32 = jnp.float32
MESH_ID = pl.DeviceIdType.MESH
WIDE = 768
VMEM_BYTES = 63 * 1024 * 1024
CHUNKS = ((0, 1, 0, 384), (0, 1, 384, 384), (1, 2, 0, 256), (1, 2, 256, 256), (1, 2, 512, 256))
AG_ORDERS = (
    (('zxy', 0, 48), ('zyx', 48, 80), ('yxz', 80, 96)),
    (('zxy', 0, 48), ('zyx', 48, 80), ('yxz', 80, 96)),
    (('zxy', 0, 48), ('zyx', 48, 80), ('yxz', 80, 96)),
    (('zxy', 0, 48), ('zyx', 48, 80), ('yxz', 80, 96)),
    (('zxy', 0, 48), ('zyx', 48, 80), ('yxz', 80, 96)),
)
RS_ORDERS = (
    (('yxz', 0, 64), ('yzx', 64, 96)),
    (('yxz', 0, 64), ('yzx', 64, 96)),
    (('yxz', 0, 48), ('xyz', 48, 80), ('zxy', 80, 96)),
    (('yxz', 0, 48), ('xyz', 48, 80), ('zxy', 80, 96)),
    (('yxz', 0, 48), ('xyz', 48, 80), ('zxy', 80, 96)),
)


def dot_nn(a, b):
    return jnp.dot(a, b, preferred_element_type=F32)


def dot_nt(a, b):
    return lax.dot_general(a, b, (((1,), (1,)), ((), ())), preferred_element_type=F32)


def dot_tn(a, b):
    return lax.dot_general(a, b, (((0,), (0,)), ((), ())), preferred_element_type=F32)


def gelu_pair(v):
    size = jnp.abs(v)
    bell = jnp.exp(v * v * -0.5)
    t = 1.0 / (1.0 + (0.3275911 * 0.7071067811865476) * size)
    poly = t * (
        0.254829592
        + t * (-0.284496736 + t * (1.421413741 + t * (-1.453152027 + t * 1.061405429)))
    )
    tail = 0.5 * poly * bell
    phi = jnp.where(v < 0.0, tail, 1.0 - tail)
    return v * phi, phi + v * bell * 0.3989422804014327


def lnorm(v, gain, shift):
    center = v - jnp.mean(v, axis=-1, keepdims=True)
    rs = lax.rsqrt(jnp.mean(center * center, axis=-1, keepdims=True) + NORM_EPS)
    return center * rs * gain + shift


def lnorm_back(v, e, gain):
    center = v - jnp.mean(v, axis=-1, keepdims=True)
    rs = lax.rsqrt(jnp.mean(center * center, axis=-1, keepdims=True) + NORM_EPS)
    xhat = center * rs
    eg = e * gain
    dv = rs * (
        eg - jnp.mean(eg, axis=-1, keepdims=True) - xhat * jnp.mean(eg * xhat, axis=-1, keepdims=True)
    )
    return dv, e * xhat


def layer_kernel(
    sizes,
    tok_hbm,
    mask_ref,
    cot_hbm,
    qkv_ref,
    out_ref,
    up_ref,
    down_ref,
    norm_ref,
    gout_ref,
    bo_out,
    ig_out,
    stats_ref,
    G,
    PA,
    RSC,
    *rest,
):
    places = [(k, o, i) for k in range(len(CHUNKS)) for o in range(len(RS_ORDERS[k])) for i in range(3)]
    n_bufs = len(places)
    RSB = dict(zip(places, rest[:n_bufs]))
    (
        tok_s, key_s, live_s, band_s, x_s, nin_s, qkv_s, ctx_s, mid_s, nm_s, nmT_s,
        cot_s, dmT_s, g_s, d_s, mlp_s, dmn_s, dctx_s, st_send, st_recv,
        loc_sem, ag_send, ag_recv, rs_send, rs_recv, ex_send, ex_recv, st_ss, st_rs,
    ) = rest[n_bufs:]
    X, C, Z, Y = sizes
    dp = lax.axis_index("dp")
    mp = lax.axis_index("mp")
    me = {"z": lax.div(dp, Y), "y": lax.rem(dp, Y), "x": lax.div(mp, C), "c": lax.rem(mp, C)}
    size_of = {"x": X, "c": C, "z": Z, "y": Y}

    def device(**over):
        at = dict(me, **over)
        return (at["z"] * Y + at["y"], at["x"] * C + at["c"])

    def shifted(axis, delta):
        return lax.rem(me[axis] + delta, size_of[axis])

    def place(whole, **over):
        return tuple(slice(None) if a in whole else pl.ds(over.get(a, me[a]), 1) for a in "xczy")

    def remote(src, dst, ss, rs, dev):
        return pltpu.make_async_remote_copy(
            src_ref=src, dst_ref=dst, send_sem=ss, recv_sem=rs, device_id=dev, device_id_type=MESH_ID
        )

    def ag_copies(k, o, i):
        m0, nm, c0, nc = CHUNKS[k]
        if i == 3:
            part = G.at[(pl.ds(m0, nm),) + place("xzy") + (slice(None), pl.ds(c0, nc))]
            return [remote(part, part, ag_send.at[k, 0], ag_recv.at[k, 0], device(c=1 - me["c"]))]
        order, r0, r1 = AG_ORDERS[k][o]
        axis = order[i]
        part = G.at[(pl.ds(m0, nm),) + place(order[:i]) + (pl.ds(r0, r1 - r0), pl.ds(c0, nc))]
        made = []
        for delta in range(1, size_of[axis]):
            at = 1 + o * 5 + sum(size_of[a] - 1 for a in order[:i]) + delta - 1
            made.append(
                remote(part, part, ag_send.at[k, at], ag_recv.at[k, at], device(**{axis: shifted(axis, delta)}))
            )
        return made

    def ag_go(k, o, i):
        if i > 0:
            for c in ag_copies(k, o, i - 1):
                c.wait_recv()
        for c in ag_copies(k, o, i):
            c.start()

    def ag_core(k):
        for o in range(len(AG_ORDERS[k])):
            for c in ag_copies(k, o, 2):
                c.wait_recv()
        for c in ag_copies(k, 0, 3):
            c.start()

    def ag_ready(k):
        for c in ag_copies(k, 0, 3):
            c.wait_recv()

    def ag_sent(k):
        for o in range(len(AG_ORDERS[k])):
            for i in range(3):
                for c in ag_copies(k, o, i):
                    c.wait_send()
        for c in ag_copies(k, 0, 3):
            c.wait_send()

    def grads_of(k):
        return (PA, 0) if CHUNKS[k][0] == 0 else (G, CHUNKS[k][0])

    def rs_copies(k, o, i):
        m0, nm, c0, nc = CHUNKS[k]
        buf, b0 = grads_of(k)
        cols = pl.ds(c0, nc)
        if i == -1:
            src = buf.at[(pl.ds(b0, nm),) + place("xzy", c=1 - me["c"]) + (slice(None), cols)]
            dst = RSC.at[pl.ds(m0, nm), :, :, :, :, :, cols]
            return [remote(src, dst, rs_send.at[k, 0], rs_recv.at[k, 0], device(c=1 - me["c"]))]
        order, r0, r1 = RS_ORDERS[k][o]
        axis, left = order[i], order[i + 1:]
        made = []
        for delta in range(1, size_of[axis]):
            at = 1 + o * 5 + sum(size_of[a] - 1 for a in order[:i]) + delta - 1
            to = shifted(axis, delta)
            src = buf.at[(pl.ds(b0, nm),) + place(left, **{axis: to}) + (pl.ds(r0, r1 - r0), cols)]
            dst = RSB[k, o, i].at[delta - 1]
            made.append(remote(src, dst, rs_send.at[k, at], rs_recv.at[k, at], device(**{axis: to})))
        return made

    def rs_go(k, o, i):
        for c in rs_copies(k, o, i):
            c.start()

    def rs_core(k):
        rs_go(k, 0, -1)

    def rs_add(k, o, i):
        m0, nm, c0, nc = CHUNKS[k]
        buf, b0 = grads_of(k)
        cols = pl.ds(c0, nc)
        for c in rs_copies(k, o, i):
            c.wait_recv()
        if i == -1:
            left, r0, r1, deltas = "xzy", 0, 96, 1
        else:
            order, r0, r1 = RS_ORDERS[k][o]
            left, deltas = order[i + 1:], size_of[order[i]] - 1
        nx, nz, ny = (size_of[a] if a in left else 1 for a in "xzy")
        here = pl.ds(r0, r1 - r0)

        def one(t, carry):
            mat = lax.div(t, nx * nz * ny)
            xi, zi, yi = lax.rem(lax.div(t, nz * ny), nx), lax.rem(lax.div(t, ny), nz), lax.rem(t, ny)
            at = (
                b0 + mat,
                xi if "x" in left else me["x"],
                me["c"],
                zi if "z" in left else me["z"],
                yi if "y" in left else me["y"],
                here,
                cols,
            )
            total = buf[at].astype(F32)
            if i == -1:
                total = total + RSC[m0 + mat, xi, 0, zi, yi, :, cols].astype(F32)
            else:
                for delta in range(deltas):
                    total = total + RSB[k, o, i][delta, mat, xi, 0, zi, yi, :, :].astype(F32)
            if left == "":
                gout_ref[m0 + mat, here, cols] = total
            else:
                buf[at] = total.astype(BF)
            return carry

        lax.fori_loop(0, nm * nx * nz * ny, one, 0)

    def rs_sent(k):
        for c in rs_copies(k, 0, -1):
            c.wait_send()
        for o in range(len(RS_ORDERS[k])):
            for i in range(3):
                for c in rs_copies(k, o, i):
                    c.wait_send()

    mates = [(0, 1), (1, 0), (1, 1)]

    def mate(j):
        dx, dc = mates[j]
        x2, c2 = lax.rem(me["x"] + dx, X), lax.rem(me["c"] + dc, C)
        return device(x=x2, c=c2), x2 * C + c2

    def exchange(which, src_of, dst):
        made = []
        for j in range(3):
            dev, index = mate(j)
            made.append(remote(src_of(index), dst, ex_send.at[which, j], ex_recv.at[which, j], dev))
        return made

    slab = pl.ds(pl.multiple_of(mp * 32, 32), 32)
    cot_copies = exchange(0, lambda t: cot_hbm.at[t], cot_s.at[:, slab, :])

    def rows_of(index):
        return pl.ds(pl.multiple_of(index * 32, 32), 32)

    bo_copies = exchange(1, lambda t: nm_s.at[:, rows_of(t), :], bo_out.at[mp])
    ig_copies = exchange(2, lambda t: cot_s.at[:, rows_of(t), :], ig_out.at[mp])
    cot_own = pltpu.make_async_copy(cot_hbm.at[mp], cot_s.at[:, slab, :], loc_sem.at[0])
    tok_copy = pltpu.make_async_copy(
        tok_hbm.at[pl.ds(pl.multiple_of(mp * 1536, 1536), 1536)], tok_s, loc_sem.at[1]
    )
    bo_own = pltpu.make_async_copy(nm_s.at[:, slab, :], bo_out.at[mp], loc_sem.at[2])
    ig_own = pltpu.make_async_copy(cot_s.at[:, slab, :], ig_out.at[mp], loc_sem.at[3])

    st_axes = "cyxz"

    def st_copies(i):
        axis = st_axes[i]
        return [
            remote(
                st_send.at[i], st_recv.at[i + delta - 1], st_ss.at[i + delta - 1], st_rs.at[i + delta - 1],
                device(**{axis: shifted(axis, delta)}),
            )
            for delta in range(1, size_of[axis])
        ]

    def st_step(i):
        if i == 0:
            total = stats_ref[...]
        else:
            copies = st_copies(i - 1)
            for c in copies:
                c.wait_recv()
            total = st_send[i - 1]
            for n in range(len(copies)):
                total = total + st_recv[i - 1 + n]
        if i < 4:
            st_send[i] = total
            for c in st_copies(i):
                c.start()
        else:
            stats_ref[...] = total

    low = norm_ref[...].astype(BF).astype(F32)
    gain_in, shift_in, gain_mid, shift_mid = (low[i:i + 1] for i in range(4))
    lane = lax.broadcasted_iota(jnp.int32, (1, 128), 1)
    lo = (lane < 64).astype(F32).astype(BF)
    hi = (lane >= 64).astype(F32).astype(BF)
    low_eighth = jnp.where(lane < 64, 0.125, 1.0)

    def weight(mat, m, c0, nc):
        m = jnp.int32(m)
        return G[mat, lax.div(m, C), lax.rem(m, C), :, :, :, pl.ds(c0, nc)].reshape(WIDE, nc)

    def put(buf, mat, m, c0, nc, value):
        m = jnp.int32(m)
        buf[mat, lax.div(m, C), lax.rem(m, C), :, :, :, pl.ds(c0, nc)] = value.reshape(Z, Y, 96, nc)

    def block(b):
        return pl.ds(pl.multiple_of(b * 128, 128), 128)

    def rows256(t):
        return pl.ds(pl.multiple_of(t * 256, 256), 256)

    def setup():
        col = lax.broadcasted_iota(jnp.int32, (64, 64), 1)
        row = lax.broadcasted_iota(jnp.int32, (64, 64), 0)
        marks = mask_ref[...].astype(F32)
        before = dot_nn(jnp.where(col < row, 1.0, 0.0).astype(BF), marks.astype(BF))
        key_s[...] = jnp.where(marks > 0.0, before, -1.0).astype(BF)
        ri = lax.broadcasted_iota(jnp.int32, (128, 128), 0) // 8 % 4
        ci = lax.broadcasted_iota(jnp.int32, (128, 128), 1) // 8 % 4
        band_s[...] = jnp.where(ri == ci, 0.0, -1e30)
        stats_ref[...] = jnp.zeros_like(stats_ref)
        mid_s[...] = jnp.zeros_like(mid_s)

    def take_block(b, carry):
        slot = lax.broadcasted_iota(jnp.int32, (key_s.shape[1], 128), 0)
        row = lax.broadcasted_iota(jnp.int32, (key_s.shape[1], 128), 1)
        owner = (mp * 6 + b) * 4 + row // 8 % 4
        rank = dot_nn(key_s[...], jnp.where(slot == owner, 1.0, 0.0).astype(BF))
        row = lax.broadcasted_iota(jnp.int32, (64, 128), 1)
        hit = jnp.where(rank == (row // 32 * 8 + row % 8).astype(F32), 1.0, 0.0)
        pick = jnp.concatenate([jnp.where(row // 8 % 4 == n, hit, 0.0) for n in range(4)], axis=0)
        live_s[block(b), :] = jnp.broadcast_to(jnp.sum(hit, axis=0, keepdims=True), (128, 128)).T
        x = dot_tn(pick.astype(BF), tok_s[pl.ds(pl.multiple_of(b * 256, 256), 256), :])
        x_s[block(b), :] = x.astype(BF)
        nin_s[block(b), :] = lnorm(x, gain_in, shift_in).astype(BF)
        return carry

    def qkv_first(m, carry):
        w = weight(0, m, 0, 384)
        for t in range(3):
            rows = pl.ds(t * 256, 256)
            out = dot_nn(nin_s[rows, :], w)
            qkv_s[m, rows, 0:128] = (out[:, :128] * 0.125).astype(BF)
            qkv_s[m, rows, 128:384] = out[:, 128:].astype(BF)
        return carry

    def qkv_second(m, carry):
        w = weight(0, m, 384, 256)
        for t in range(3):
            rows = pl.ds(t * 256, 256)
            out = dot_nn(nin_s[rows, :], w)
            first = out[:, :128] * low_eighth
            qkv_s[m, rows, 384:512] = first.astype(BF)
            qkv_s[m, rows, 512:640] = pltpu.roll(first, 64, 1).astype(BF)
            qkv_s[m, rows, 640:768] = pltpu.roll(out[:, 128:], 64, 1).astype(BF)
        return carry

    def keep_p(i, h, p):
        rows = pl.ds(pl.multiple_of(i * 64, 64), 64)
        tok_s[rows, h * 128:(h + 1) * 128] = p[:64]
        tok_s[rows, 384 + h * 128:512 + h * 128] = p[64:]

    def kept_p(i, h):
        rows = pl.ds(pl.multiple_of(i * 64, 64), 64)
        return jnp.concatenate(
            [tok_s[rows, h * 128:(h + 1) * 128], tok_s[rows, 384 + h * 128:512 + h * 128]], axis=0
        )

    def softmax(s):
        e = jnp.exp(s - jnp.max(s, axis=0, keepdims=True))
        return (e * (1.0 / jnp.sum(e, axis=0, keepdims=True))).astype(BF)

    def attend_first(j, carry):
        at = [(lax.div(j, 2), lax.rem(j, 2) * 3 + u) for u in range(3)]
        qs, ks, vs = ([qkv_s[m, block(b), n * 128:(n + 1) * 128] for m, b in at] for n in range(3))
        scores = [dot_nt(k, q * side) + band_s[...] for q, k in zip(qs, ks) for side in (lo, hi)]
        probs = [softmax(x) for x in scores]
        for u, (m, b) in enumerate(at):
            p0, p1 = probs[2 * u], probs[2 * u + 1]
            keep_p(m * 6 + b, 0, p0)
            keep_p(m * 6 + b, 1, p1)
            ctx_s[m, block(b), 128:256] = (dot_tn(p0, vs[u] * lo) + dot_tn(p1, vs[u] * hi)).astype(BF)
        return carry

    def attend_second(j, carry):
        at = [(j, u) for u in range(6)]
        qs, ks, vs = ([qkv_s[m, block(b), n * 128:(n + 1) * 128] for m, b in at] for n in range(3, 6))
        scores = [dot_nt(k, q * lo) + band_s[...] for q, k in zip(qs, ks)]
        probs = [softmax(x) for x in scores]
        for u, (m, b) in enumerate(at):
            keep_p(m * 6 + b, 2, probs[u])
            ctx_s[m, block(b), 0:128] = dot_tn(probs[u], vs[u] * hi).astype(BF)
        return carry

    def mid_tile(m, carry):
        w = weight(0, m, 512, 256)
        for t in range(3):
            rows = pl.ds(t * 256, 256)
            mid_s[rows, :] += dot_nt(ctx_s[m, rows, :], w)
        return carry

    def mid_block(b, carry):
        rows = block(b)
        attn = mid_s[rows, :]
        live = live_s[rows, :][:, :1]
        stats_ref[4:5, :] += jnp.sum(attn * attn * live, axis=0, keepdims=True)
        mid = x_s[rows, :].astype(F32) + attn
        mid_s[rows, :] = mid
        nm_s[b] = lnorm(mid, gain_mid, shift_mid).astype(BF)
        return carry

    def transpose_into(dst, src):
        def one(b, carry):
            part = src(b)
            for j in range(6):
                dst[pl.ds(j * 128, 128), block(b)] = part[:, j * 128:(j + 1) * 128].T
            return carry

        lax.fori_loop(0, 6, one, 0)

    def cot_block(b, carry):
        live = live_s[block(b), :][:, :1]
        cot_s[b] = (cot_s[b].astype(F32) * live).astype(BF)
        return carry

    def mlp_tile(c0, nc):
        def tile(m, carry):
            w_up = weight(1, m, c0, nc)
            w_down = weight(2, m, c0, nc)
            pre, d_act = [], []

            def begin(t):
                pre.append(dot_nn(nm_s[2 * t:2 * t + 2].reshape(256, WIDE), w_up))
                d_act.append(dot_nn(cot_s[2 * t:2 * t + 2].reshape(256, WIDE), w_down))

            begin(0)
            for t in range(3):
                if t < 2:
                    begin(t + 1)
                rows = pl.ds(t * 256, 256)
                act, slope = gelu_pair(pre[t])
                act = act.astype(BF)
                d_pre = (d_act[t] * slope).astype(BF)
                g_s[rows, :] = act
                d_s[rows, :] = d_pre
                mlp_s[rows, :] += dot_nt(act, w_down)
                dmn_s[rows, :] += dot_nt(d_pre, w_up)
            put(G, 2, m, c0, nc, dot_nn(dmT_s[...], g_s[...]).astype(BF))
            put(G, 1, m, c0, nc, dot_nn(nmT_s[...], d_s[...]).astype(BF))
            return carry

        return tile

    def end_block(b, carry):
        rows = block(b)
        live = live_s[rows, :][:, :1]
        mlp = mlp_s[rows, :]
        mid = mid_s[rows, :]
        out = (mid + mlp) * live
        stats_ref[5:6, :] += jnp.sum(mlp * mlp * live, axis=0, keepdims=True)
        stats_ref[6:7, :] += jnp.sum(out * out, axis=0, keepdims=True)
        nm_s[b] = out.astype(BF)
        e = dmn_s[rows, :]
        dv, ex = lnorm_back(mid, e, gain_mid)
        stats_ref[2:3, :] += jnp.sum(ex, axis=0, keepdims=True)
        stats_ref[3:4, :] += jnp.sum(e, axis=0, keepdims=True)
        d_mid = cot_s[b].astype(F32) + dv
        mlp_s[rows, :] = d_mid
        cot_s[b] = d_mid.astype(BF)
        return carry

    def dctx_tile(m, carry):
        w = weight(0, m, 512, 256)
        for t in range(3):
            rows = pl.ds(t * 256, 256)
            out = dot_nn(cot_s[2 * t:2 * t + 2].reshape(256, WIDE), w)
            dctx_s[rows, 0:256] = out.astype(BF)
            dctx_s[rows, 256:384] = pltpu.roll(out[:, :128], 64, 1).astype(BF)
        return carry

    def score_back(p, d_probs):
        pf = p.astype(F32)
        w = pf * d_probs
        return (w - pf * jnp.sum(w, axis=0, keepdims=True)).astype(BF)

    def attend_back(j, carry):
        m = lax.div(j, 2)
        at = [lax.rem(j, 2) * 3 + u for u in range(3)]
        held = [[qkv_s[m, block(b), n * 128:(n + 1) * 128] for n in range(6)] for b in at]
        came = [[dctx_s[block(b), n * 128:(n + 1) * 128] for n in range(3)] for b in at]
        probs = [[kept_p(m * 6 + b, h) for h in range(3)] for b in at]
        d_probs = [
            [dot_nt(v, d01 * lo), dot_nt(v, d01 * hi), dot_nt(v2, d2 * hi)]
            for (q, k, v, q2, k2, v2), (d2, d01, d2r) in zip(held, came)
        ]
        d_scores = [[score_back(p, d) for p, d in zip(ps, ds)] for ps, ds in zip(probs, d_probs)]
        for b, (q, k, v, q2, k2, v2), (d2, d01, d2r), (p0, p1, p2), (s0, s1, s2) in zip(
            at, held, came, probs, d_scores
        ):
            dk = dot_nn(s0, q * lo) + dot_nn(s1, q * hi)
            dv = dot_nn(p0, d01 * lo) + dot_nn(p1, d01 * hi)
            dv2 = dot_nn(p2, d2r * lo)
            dq = dot_tn(s0, k * lo) + dot_tn(s1, k * hi)
            dqk2 = dot_tn(s2, k2 * lo) * 0.125 + dot_nn(s2, k2 * hi)
            for n, out in enumerate((dq * 0.125, dk, dv, dqk2, dv2)):
                qkv_s[m, block(b), n * 128:(n + 1) * 128] = out.astype(BF)
        return carry

    def put_all(m, c0, nc, value):
        put(PA, 0, m, c0, nc, value)

    def grad_a0(m, carry):
        put_all(m, 0, 384, dot_nn(nmT_s[...], qkv_s[m, :, 0:384]).astype(BF))
        return carry

    def grad_a1(m, carry):
        out_part = dot_nn(dmT_s[...], ctx_s[m])
        qkv_part = dot_nn(nmT_s[...], qkv_s[m, :, 384:640])
        put_all(m, 384, 128, qkv_part[:, :128].astype(BF))
        put_all(m, 512, 128, (qkv_part[:, 128:] + out_part[:, :128]).astype(BF))
        put_all(m, 640, 128, out_part[:, 128:].astype(BF))
        return carry

    def in_tile(m, carry):
        w = weight(0, m, 0, 640)
        for t in range(3):
            rows = pl.ds(t * 256, 256)
            dmn_s[rows, :] += dot_nt(qkv_s[m, rows, 0:640], w)
        return carry

    def in_block(b, carry):
        rows = block(b)
        e = dmn_s[rows, :]
        dv, ex = lnorm_back(x_s[rows, :].astype(F32), e, gain_in)
        stats_ref[0:1, :] += jnp.sum(ex, axis=0, keepdims=True)
        stats_ref[1:2, :] += jnp.sum(e, axis=0, keepdims=True)
        live = live_s[rows, :][:, :1]
        cot_s[b] = ((mlp_s[rows, :] + dv) * live).astype(BF)
        return carry

    def loop(first, last, body):
        if last == first + 1:
            body(jnp.int32(first), 0)
        else:
            lax.fori_loop(first, last, body, 0)

    def take():
        tok_copy.wait()
        loop(0, 6, take_block)

    def cot_start():
        for c in cot_copies:
            c.start()

    def cot_ready():
        cot_own.wait()
        for c in cot_copies:
            c.wait_recv()
        loop(0, 6, cot_block)
        transpose_into(dmT_s, lambda b: cot_s[b])
        mlp_s[...] = jnp.zeros_like(mlp_s)
        dmn_s[...] = jnp.zeros_like(dmn_s)

    def middle():
        loop(0, 6, mid_block)
        transpose_into(nmT_s, lambda b: nm_s[b])

    def turn():
        dmn_s[...] = jnp.zeros_like(dmn_s)
        transpose_into(dmT_s, lambda b: cot_s[b])
        transpose_into(nmT_s, lambda b: nin_s[block(b), :])

    def bo_start():
        for c in bo_copies:
            c.start()
        bo_own.start()

    def ig_start():
        for c in ig_copies:
            c.start()
        ig_own.start()

    def finish():
        for k in range(len(CHUNKS)):
            if CHUNKS[k][0] == 0:
                ag_sent(k)
            rs_sent(k)
        for c in cot_copies:
            c.wait_send()
        for c in (*bo_copies, *ig_copies):
            c.wait()
        bo_own.wait()
        ig_own.wait()
        for i in range(4):
            for c in st_copies(i):
                c.wait_send()

    tok_copy.start()
    cot_own.start()
    here = (me["x"], me["c"], me["z"], me["y"], slice(None))
    out_t = out_ref[...].T
    for t in range(3):
        G[(0, *here, pl.ds(t * 128, 128))] = qkv_ref[t, :, 0:128].astype(BF)
    last = [qkv_ref[t, :, 128:192] for t in range(3)]
    G[(0, *here, pl.ds(384, 128))] = jnp.concatenate(last[:2], axis=1).astype(BF)
    G[(0, *here, pl.ds(512, 128))] = jnp.concatenate([last[2], out_t[:, 128:192]], axis=1).astype(BF)
    G[(0, *here, pl.ds(640, 128))] = out_t[:, 0:128].astype(BF)
    G[(1, *here, slice(None))] = up_ref[...].astype(BF)
    G[(2, *here, slice(None))] = down_ref[...].astype(BF)
    barrier = pltpu.get_barrier_semaphore()
    greet = [device(c=1 - me["c"]), device(y=1 - me["y"]), device(x=1 - me["x"]),
             device(x=1 - me["x"], c=1 - me["c"])]
    greet += [device(z=shifted("z", n)) for n in range(1, Z)]
    for dev in greet:
        pl.semaphore_signal(barrier, inc=1, device_id=dev, device_id_type=MESH_ID)
    pl.semaphore_wait(barrier, len(greet))

    ag_go(0, 0, 0)
    cot_start()
    ag_go(0, 2, 0)
    ag_go(0, 1, 0)
    ag_go(0, 2, 1)
    ag_go(1, 1, 0)
    ag_go(4, 2, 0)
    ag_go(1, 2, 0)
    ag_go(2, 2, 0)
    ag_go(2, 0, 0)
    ag_go(0, 0, 1)
    ag_go(0, 1, 1)
    setup()
    take()
    ag_go(1, 0, 0)
    ag_go(3, 0, 0)
    ag_go(2, 2, 1)
    ag_go(1, 1, 1)
    ag_go(1, 0, 1)
    ag_go(0, 1, 2)
    ag_go(0, 2, 2)
    ag_go(1, 2, 1)
    ag_go(4, 2, 1)
    ag_go(3, 1, 0)
    ag_go(2, 0, 1)
    cot_ready()
    ag_go(1, 1, 2)
    ag_go(2, 1, 0)
    ag_go(0, 0, 2)
    ag_go(3, 2, 0)
    ag_go(1, 2, 2)
    ag_go(1, 0, 2)
    ag_core(0)
    ag_ready(0)
    ag_go(3, 0, 1)
    ag_go(2, 1, 1)
    loop(2, 4, qkv_first)
    ag_go(2, 0, 2)
    ag_core(1)
    ag_go(4, 0, 0)
    loop(0, 2, qkv_first)
    loop(2, 4, attend_first)
    ag_go(2, 2, 2)
    ag_go(3, 1, 1)
    ag_ready(1)
    loop(1, 2, qkv_second)
    ag_go(2, 1, 2)
    loop(0, 1, qkv_second)
    loop(0, 2, attend_second)
    loop(2, 3, qkv_second)
    loop(4, 6, attend_first)
    loop(1, 2, mid_tile)
    ag_go(3, 2, 1)
    loop(2, 3, attend_second)
    loop(2, 3, mid_tile)
    ag_go(4, 1, 0)
    ag_go(4, 0, 1)
    loop(3, 4, qkv_second)
    loop(0, 2, attend_first)
    ag_go(3, 0, 2)
    ag_go(3, 1, 2)
    ag_core(2)
    loop(6, 8, attend_first)
    loop(0, 1, mid_tile)
    loop(3, 4, attend_second)
    ag_go(3, 2, 2)
    loop(3, 4, mid_tile)
    middle()
    ag_ready(2)
    ag_go(4, 1, 1)
    ag_sent(2)
    loop(0, 1, mlp_tile(0, 256))
    ag_go(4, 2, 2)
    loop(1, 2, mlp_tile(0, 256))
    ag_go(4, 0, 2)
    ag_core(3)
    loop(2, 3, mlp_tile(0, 256))
    ag_go(4, 1, 2)
    loop(3, 4, mlp_tile(0, 256))
    rs_core(2)
    ag_ready(3)
    ag_sent(3)
    loop(0, 2, mlp_tile(256, 256))
    ag_core(4)
    rs_add(2, 0, -1)
    rs_go(2, 0, 0)
    loop(2, 3, mlp_tile(256, 256))
    rs_go(2, 2, 0)
    loop(3, 4, mlp_tile(256, 256))
    rs_go(2, 1, 0)
    ag_ready(4)
    rs_core(3)
    ag_sent(4)
    loop(0, 3, mlp_tile(512, 256))
    rs_add(3, 0, -1)
    rs_go(3, 1, 0)
    rs_add(2, 0, 0)
    rs_go(3, 0, 0)
    loop(3, 4, mlp_tile(512, 256))
    rs_core(4)
    loop(0, 6, end_block)
    rs_add(2, 1, 0)
    rs_go(2, 0, 1)
    loop(0, 1, dctx_tile)
    turn()
    rs_add(3, 1, 0)
    rs_add(2, 2, 0)
    rs_go(2, 1, 1)
    rs_go(2, 2, 1)
    rs_go(3, 2, 0)
    rs_go(3, 1, 1)
    rs_add(4, 0, -1)
    rs_go(4, 1, 0)
    loop(0, 2, attend_back)
    loop(1, 2, dctx_tile)
    loop(2, 4, attend_back)
    rs_go(4, 2, 0)
    loop(2, 3, dctx_tile)
    bo_start()
    rs_go(4, 0, 0)
    loop(4, 6, attend_back)
    loop(3, 4, dctx_tile)
    rs_add(2, 1, 1)
    loop(0, 1, grad_a0)
    loop(6, 8, attend_back)
    loop(3, 4, grad_a0)
    loop(1, 2, grad_a0)
    rs_add(2, 2, 1)
    loop(2, 3, grad_a0)
    rs_core(0)
    rs_add(4, 1, 0)
    rs_go(4, 1, 1)
    rs_add(3, 1, 1)
    loop(2, 3, in_tile)
    loop(0, 1, grad_a1)
    rs_go(2, 1, 2)
    loop(2, 3, grad_a1)
    rs_add(3, 0, 0)
    rs_add(4, 0, 0)
    rs_go(4, 0, 1)
    rs_add(3, 2, 0)
    rs_add(0, 0, -1)
    rs_go(0, 0, 0)
    rs_add(2, 0, 1)
    rs_go(3, 1, 2)
    loop(1, 2, grad_a1)
    loop(3, 4, in_tile)
    rs_go(3, 2, 1)
    rs_add(4, 2, 0)
    rs_go(2, 2, 2)
    loop(3, 4, grad_a1)
    rs_core(1)
    rs_add(4, 1, 1)
    rs_go(4, 2, 1)
    rs_go(3, 0, 1)
    rs_go(4, 1, 2)
    rs_go(2, 0, 2)
    loop(0, 2, in_tile)
    rs_add(4, 0, 1)
    rs_add(1, 0, -1)
    rs_go(4, 0, 2)
    rs_add(0, 0, 0)
    rs_go(1, 1, 0)
    loop(0, 6, in_block)
    rs_go(0, 0, 1)
    rs_go(1, 0, 0)
    rs_add(1, 1, 0)
    ig_start()
    rs_add(2, 2, 2)
    rs_go(1, 1, 1)
    rs_add(3, 1, 2)
    rs_add(3, 0, 1)
    rs_add(0, 0, 1)
    rs_go(0, 1, 0)
    st_step(0)
    rs_add(4, 0, 2)
    rs_go(0, 0, 2)
    rs_add(1, 0, 0)
    rs_go(3, 0, 2)
    rs_add(4, 2, 1)
    rs_go(1, 0, 1)
    rs_add(0, 1, 0)
    rs_go(0, 1, 1)
    rs_add(4, 1, 2)
    rs_add(1, 1, 1)
    rs_go(1, 1, 2)
    st_step(1)
    rs_add(3, 2, 1)
    rs_add(1, 0, 1)
    rs_go(1, 0, 2)
    st_step(2)
    rs_add(1, 1, 2)
    rs_go(4, 2, 2)
    rs_add(4, 2, 2)
    rs_add(0, 1, 1)
    rs_go(3, 2, 2)
    rs_add(3, 0, 2)
    rs_add(2, 1, 2)
    rs_add(2, 0, 2)
    rs_add(0, 0, 2)
    st_step(3)
    rs_go(0, 1, 2)
    rs_add(0, 1, 2)
    rs_add(3, 2, 2)
    rs_add(1, 0, 2)
    st_step(4)
    finish()


def fits_fused(mesh):
    return mesh.shape["dp"] == 8 and mesh.shape["mp"] == 4


def renew_kernel(count, grads, bo, ig, stats, *rest):
    ins, (bo_new, ig_new, rms), news = rest[:15], rest[15:18], rest[18:]

    def rows(t, carry):
        for b in range(bo.shape[1]):
            bo_new[t, b] = bo[t, b].astype(F32)
            ig_new[t, b] = ig[t, b].astype(F32)
        return carry

    lax.fori_loop(0, bo.shape[0], rows, 0)
    size = jnp.sqrt(jnp.sum(stats[...], axis=1, keepdims=True) / count)
    for n in range(3):
        rms[n] = size[4 + n, 0]

    def step(n, at, gradient, rate):
        weight, momentum, average = (ref[at] for ref in ins[3 * n:3 * n + 3])
        for ref, value in zip(news[4 * n:4 * n + 4], renew_weight(weight, momentum, average, gradient, rate)):
            ref[at] = value

    whole = slice(None)
    for t in range(3):
        step(0, (t, whole, pl.ds(0, 128)), grads[0, :, 128 * t:128 * t + 128], MATRIX_RATE)
        step(0, (t, whole, pl.ds(128, 64)), grads[0, :, 384 + 64 * t:448 + 64 * t], MATRIX_RATE)
    step(1, (pl.ds(0, 128), whole), grads[0, :, 640:768].T, OUTPUT_RATE)
    step(1, (pl.ds(128, 64), whole), grads[0, :, 512:640].T[64:], OUTPUT_RATE)
    step(2, (whole, whole), grads[1], MATRIX_RATE)
    step(3, (whole, whole), grads[2], MATRIX_RATE)
    step(4, (whole, whole), stats[0:4], NORM_RATE)


def local_fused(
    tokens,
    visible_mask,
    cotangent,
    qkv_weight,
    qkv_momentum,
    qkv_average,
    out_weight,
    out_momentum,
    out_average,
    up_weight,
    up_momentum,
    up_average,
    down_weight,
    down_momentum,
    down_average,
    norm_params,
    norm_momentum,
    norm_average,
):
    data_size = lax.axis_size("dp")
    model_size = lax.axis_size("mp")
    slots, patches, width = tokens.shape
    quarter = cotangent.shape[1]
    sizes = (model_size // 2, 2, data_size // 2, 2)
    X, C, Z, Y = sizes
    blocks = slots // (4 * model_size)
    group = blocks * 32
    bufs = []
    size_of = {"x": X, "z": Z, "y": Y}
    for (_, mats, _, cols), orders in zip(CHUNKS, RS_ORDERS):
        for order, r0, r1 in orders:
            for i in range(3):
                nx, nz, ny = (size_of[a] if a in order[i + 1:] else 1 for a in "xzy")
                bufs.append(pltpu.VMEM((size_of[order[i]] - 1, mats, nx, 1, nz, ny, r1 - r0, cols), BF))
    n_chunk = len(CHUNKS)
    n_ag = 1 + 5 * max(len(orders) for orders in AG_ORDERS)
    n_rs = 1 + 5 * max(len(orders) for orders in RS_ORDERS)
    rows = blocks * 128
    vmem = pltpu.VMEM
    dma = pltpu.SemaphoreType.DMA
    scratch = [
        vmem((3, X, C, Z, Y, 96, WIDE), BF),
        vmem((1, X, C, Z, Y, 96, WIDE), BF),
        vmem((3, X, 1, Z, Y, 96, WIDE), BF),
        *bufs,
        vmem((24 * patches, WIDE), BF),
        vmem((patches, slots), BF),
        vmem((rows, 128), F32),
        vmem((128, 128), F32),
        vmem((rows, WIDE), BF),
        vmem((rows, WIDE), BF),
        vmem((4, rows, WIDE), BF),
        vmem((4, rows, 256), BF),
        vmem((rows, WIDE), F32),
        vmem((blocks, 128, WIDE), BF),
        vmem((WIDE, rows), BF),
        vmem((blocks, 128, WIDE), BF),
        vmem((WIDE, rows), BF),
        vmem((rows, 256), BF),
        vmem((rows, 256), BF),
        vmem((rows, WIDE), F32),
        vmem((rows, WIDE), F32),
        vmem((rows, 384), BF),
        vmem((4, 8, WIDE), F32),
        vmem((6, 8, WIDE), F32),
        dma((4,)),
        dma((n_chunk, n_ag)),
        dma((n_chunk, n_ag)),
        dma((n_chunk, n_rs)),
        dma((n_chunk, n_rs)),
        dma((3, 3)),
        dma((3, 3)),
        dma((6,)),
        dma((6,)),
    ]
    in_vmem = pl.BlockSpec(memory_space=pltpu.VMEM)
    anywhere = pl.BlockSpec(memory_space=pl.ANY)
    grads, bo, ig, stats = pl.pallas_call(
        functools.partial(layer_kernel, sizes),
        out_shape=(
            jax.ShapeDtypeStruct((3, 96, WIDE), F32),
            jax.ShapeDtypeStruct((model_size, blocks, 32, WIDE), BF),
            jax.ShapeDtypeStruct((model_size, blocks, 32, WIDE), BF),
            jax.ShapeDtypeStruct((8, WIDE), F32),
        ),
        in_specs=[anywhere, in_vmem, anywhere] + [in_vmem] * 5,
        out_specs=(in_vmem, anywhere, anywhere, in_vmem),
        scratch_shapes=scratch,
        compiler_params=pltpu.CompilerParams(
            collective_id=0, has_side_effects=True, vmem_limit_bytes=VMEM_BYTES
        ),
        name="layer",
    )(
        tokens.reshape(slots * patches, width),
        visible_mask.T,
        cotangent.reshape(model_size, blocks, 32, width),
        qkv_weight,
        out_weight,
        up_weight,
        down_weight.T,
        norm_params,
    )
    visible_count = quarter * model_size
    triples = (
        (qkv_weight, qkv_momentum, qkv_average),
        (out_weight, out_momentum, out_average),
        (up_weight, up_momentum, up_average),
        (down_weight.T, down_momentum.T, down_average.T),
        (norm_params, norm_momentum, norm_average),
    )
    shares = jax.ShapeDtypeStruct((model_size, blocks, 32, width), F32)
    news = []
    for weight, _, _ in triples:
        news += [jax.ShapeDtypeStruct(weight.shape, F32)] * 3 + [jax.ShapeDtypeStruct(weight.shape, BF)]
    block_out, input_grad, rms, *new = pl.pallas_call(
        functools.partial(renew_kernel, visible_count * data_size * FLD_DEV * width),
        out_shape=(shares, shares, jax.ShapeDtypeStruct((3,), F32), *news),
        in_specs=[in_vmem] * (4 + 3 * len(triples)),
        out_specs=(in_vmem, in_vmem, pl.BlockSpec(memory_space=pltpu.SMEM)) + (in_vmem,) * len(news),
        compiler_params=pltpu.CompilerParams(vmem_limit_bytes=VMEM_BYTES),
        name="renew",
    )(grads, bo, ig, stats, *(array for triple in triples for array in triple))
    block_out = block_out.reshape(slots, quarter, width)
    input_grad = input_grad.reshape(slots, quarter, width)
    new[12:16] = [array.T for array in new[12:16]]
    return (block_out, input_grad, rms, *new)


def local_general(
    tokens,
    visible_mask,
    cotangent,
    qkv_weight,
    qkv_momentum,
    qkv_average,
    out_weight,
    out_momentum,
    out_average,
    up_weight,
    up_momentum,
    up_average,
    down_weight,
    down_momentum,
    down_average,
    norm_params,
    norm_momentum,
    norm_average,
):
    data_size = lax.axis_size("dp")
    model_size = lax.axis_size("mp")
    data_rank = lax.axis_index("dp")
    model_rank = lax.axis_index("mp")
    slot_count, patch_count, feature_count = tokens.shape
    quarter = cotangent.shape[1]
    visible_count = quarter * model_size
    capacity = (slot_count + data_size - 1) // data_size
    owned_fields = FLD_DEV
    pad_total = data_size * capacity
    per_field = jnp.sum(visible_mask, axis=1)
    field_total = jnp.sum(per_field) // visible_count
    all_fields = lax.all_gather(field_total.reshape(1), "dp", axis=0, tiled=True)
    firsts = jnp.cumsum(all_fields) - all_fields
    my_first = firsts[data_rank]
    patch_ids = jnp.arange(patch_count, dtype=jnp.int32)
    sort_keys = (1 - visible_mask) * patch_count + patch_ids[None, :]
    ranked = jnp.argsort(sort_keys, axis=1)
    my_order = lax.dynamic_slice_in_dim(ranked, model_rank * quarter, quarter, 1)
    visible = jnp.take_along_axis(tokens, my_order[:, :, None], axis=1)
    owner_ids = jnp.arange(data_size, dtype=jnp.int32)[:, None]
    slot_ids = jnp.arange(capacity, dtype=jnp.int32)[None, :]
    source_field = slot_ids * data_size + (owner_ids - my_first) % data_size
    send_live = (source_field < field_total).reshape(-1)[:, None, None]
    source_pick = jnp.minimum(source_field, slot_count - 1).reshape(-1)
    sent_rows = jnp.where(send_live, visible[source_pick], jnp.zeros((), jnp.bfloat16))
    sent_grads = jnp.where(send_live, cotangent[source_pick], jnp.zeros((), jnp.bfloat16))
    got_rows, got_grads = (
        lax.all_to_all(sent_rows, "dp", split_axis=0, concat_axis=0, tiled=True),
        lax.all_to_all(sent_grads, "dp", split_axis=0, concat_axis=0, tiled=True),
    )
    arrive = slot_ids * data_size + (data_rank - firsts[:, None]) % data_size
    flat_live = (arrive < all_fields[:, None]).reshape(-1)
    order_keys = jnp.where(flat_live, 0, pad_total) + jnp.arange(pad_total, dtype=jnp.int32)
    chosen = jnp.argsort(order_keys)[:owned_fields]
    share_rows = owned_fields * quarter
    mine_rows = got_rows[chosen].reshape(share_rows, feature_count)
    mine_grads = got_grads[chosen].reshape(share_rows, feature_count)
    w_qkv, w_out, w_up, w_down = (
        lax.all_gather(qkv_weight.astype(jnp.bfloat16), "dp", axis=1, tiled=True),
        lax.all_gather(out_weight.astype(jnp.bfloat16), "dp", axis=1, tiled=True),
        lax.all_gather(up_weight.astype(jnp.bfloat16), "dp", axis=0, tiled=True),
        lax.all_gather(down_weight.astype(jnp.bfloat16), "dp", axis=1, tiled=True),
    )
    norm_low = lax.optimization_barrier(norm_params.astype(jnp.bfloat16)).astype(jnp.float32)
    total_rows = share_rows * model_size
    local_width = w_qkv.shape[2]
    head_local = local_width // HDIM
    score_scale = HDIM ** (-0.5)
    x_share = mine_rows.astype(jnp.float32)
    normed_share, norm_in_back = jax.vjp(layer_norm, x_share, norm_low[0], norm_low[1])
    normed_all = lax.all_gather(normed_share.astype(jnp.bfloat16), "mp", axis=0, tiled=True)
    qkv_rows = jnp.einsum(
        "rd,tde->tre", normed_all, w_qkv, preferred_element_type=jnp.float32
    ).astype(jnp.bfloat16)
    qkv_six = qkv_rows.reshape(3, model_size, owned_fields, quarter, head_local, HDIM)
    queries = qkv_six[0]
    key_rows = qkv_six[1]
    values = qkv_six[2]
    scores = (
        jnp.einsum("afbhe,cfdhe->fhabcd", queries, key_rows, preferred_element_type=jnp.float32)
        * score_scale
    )
    scores = scores.reshape(owned_fields, head_local, visible_count, visible_count)
    attention = jax.nn.softmax(scores, axis=-1)
    att_six = attention.astype(jnp.bfloat16).reshape(
        owned_fields, head_local, model_size, quarter, model_size, quarter
    )
    context = jnp.einsum("fhabcd,cfdhe->afbhe", att_six, values, preferred_element_type=jnp.float32)
    context = context.astype(jnp.bfloat16).reshape(total_rows, local_width)
    attn_share = lax.psum_scatter(
        jnp.dot(context, w_out, preferred_element_type=jnp.float32).astype(jnp.bfloat16),
        "mp",
        scatter_dimension=0,
        tiled=True,
    ).astype(jnp.float32)
    mid_share = x_share + attn_share
    normed_mid, norm_mid_back = jax.vjp(layer_norm, mid_share, norm_low[2], norm_low[3])
    mid_all, grad_all = (
        lax.all_gather(normed_mid.astype(jnp.bfloat16), "mp", axis=0, tiled=True),
        lax.all_gather(mine_grads, "mp", axis=0, tiled=True),
    )
    pre_act = jnp.dot(mid_all, w_up, preferred_element_type=jnp.float32)
    gelu_float, gelu_back = jax.vjp(gelu_exact, pre_act)
    gelu_out = gelu_float.astype(jnp.bfloat16)
    mlp_share = lax.psum_scatter(
        jnp.dot(gelu_out, w_down, preferred_element_type=jnp.float32).astype(jnp.bfloat16),
        "mp",
        scatter_dimension=0,
        tiled=True,
    ).astype(jnp.float32)
    out_share = mid_share + mlp_share
    squares = jnp.stack(
        [
            jnp.sum(attn_share * attn_share),
            jnp.sum(mlp_share * mlp_share),
            jnp.sum(out_share * out_share),
        ]
    )
    grad_down = jnp.einsum("rf,rd->fd", gelu_out, grad_all, preferred_element_type=jnp.float32)
    d_act = jnp.einsum("rd,fd->rf", grad_all, w_down, preferred_element_type=jnp.float32)
    d_pre = gelu_back(d_act)[0].astype(jnp.bfloat16)
    grad_up = jnp.einsum("rd,rf->df", mid_all, d_pre, preferred_element_type=jnp.float32)
    d_mid_norm = lax.psum_scatter(
        jnp.einsum("rf,df->rd", d_pre, w_up, preferred_element_type=jnp.float32).astype(
            jnp.bfloat16
        ),
        "mp",
        scatter_dimension=0,
        tiled=True,
    ).astype(jnp.float32)
    d_mid_part, grad_gain_mid, grad_shift_mid = norm_mid_back(d_mid_norm)
    d_middle = mine_grads.astype(jnp.float32) + d_mid_part
    d_att_all = lax.all_gather(d_middle.astype(jnp.bfloat16), "mp", axis=0, tiled=True)
    grad_out = jnp.einsum("rc,rd->cd", context, d_att_all, preferred_element_type=jnp.float32)
    d_context = jnp.einsum(
        "rd,cd->rc", d_att_all, w_out, preferred_element_type=jnp.float32
    ).astype(jnp.bfloat16)
    d_ctx_six = d_context.reshape(model_size, owned_fields, quarter, head_local, HDIM)
    d_probs = jnp.einsum(
        "afbhe,cfdhe->fhabcd", d_ctx_six, values, preferred_element_type=jnp.float32
    )
    d_probs = d_probs.reshape(owned_fields, head_local, visible_count, visible_count)
    d_values = jnp.einsum(
        "fhabcd,afbhe->cfdhe", att_six, d_ctx_six, preferred_element_type=jnp.float32
    )
    d_scores = (
        attention * (d_probs - jnp.sum(d_probs * attention, axis=-1, keepdims=True))
    ).astype(jnp.bfloat16)
    d_six = d_scores.reshape(owned_fields, head_local, model_size, quarter, model_size, quarter)
    d_queries = (
        jnp.einsum("fhabcd,cfdhe->afbhe", d_six, key_rows, preferred_element_type=jnp.float32)
        * score_scale
    )
    d_keys = (
        jnp.einsum("fhabcd,afbhe->cfdhe", d_six, queries, preferred_element_type=jnp.float32)
        * score_scale
    )
    d_qkv = (
        jnp.stack([d_queries, d_keys, d_values])
        .astype(jnp.bfloat16)
        .reshape(3, total_rows, local_width)
    )
    grad_qkv = jnp.einsum("rd,tre->tde", normed_all, d_qkv, preferred_element_type=jnp.float32)
    d_in_norm = lax.psum_scatter(
        jnp.einsum("tre,tde->rd", d_qkv, w_qkv, preferred_element_type=jnp.float32).astype(
            jnp.bfloat16
        ),
        "mp",
        scatter_dimension=0,
        tiled=True,
    ).astype(jnp.float32)
    d_in_part, grad_gain_in, grad_shift_in = norm_in_back(d_in_norm)
    d_input = d_middle + d_in_part
    gradients = (grad_qkv, grad_out, grad_up, grad_down)
    summed = lax.psum((gradients[0], gradients[1], gradients[2], gradients[3]), "dp")
    qkv_grad = lax.dynamic_slice_in_dim(
        summed[0], data_rank * qkv_weight.shape[1], qkv_weight.shape[1], 1
    )
    out_grad = lax.dynamic_slice_in_dim(
        summed[1], data_rank * out_weight.shape[1], out_weight.shape[1], 1
    )
    up_grad = lax.dynamic_slice_in_dim(
        summed[2], data_rank * up_weight.shape[0], up_weight.shape[0], 0
    )
    down_grad = lax.dynamic_slice_in_dim(
        summed[3], data_rank * down_weight.shape[1], down_weight.shape[1], 1
    )

    def spread_back(share_block):
        padded = jnp.zeros((pad_total, quarter, feature_count), jnp.float32)
        return padded.at[chosen].set(share_block.reshape(owned_fields, quarter, feature_count))

    back_out, back_grad = (
        lax.all_to_all(
            spread_back(out_share).astype(jnp.bfloat16),
            "dp",
            split_axis=0,
            concat_axis=0,
            tiled=True,
        ).astype(jnp.float32),
        lax.all_to_all(
            spread_back(d_input).astype(jnp.bfloat16), "dp", split_axis=0, concat_axis=0, tiled=True
        ).astype(jnp.float32),
    )
    field_ids = jnp.arange(slot_count, dtype=jnp.int32)
    home_slot = (my_first + field_ids) % data_size * capacity + field_ids // data_size
    field_live = (field_ids < field_total)[:, None, None]
    block_out = jnp.where(field_live, back_out[home_slot], 0.0)
    input_grad = jnp.where(field_live, back_grad[home_slot], 0.0)
    norm_grad = jnp.stack([grad_gain_in, grad_shift_in, grad_gain_mid, grad_shift_mid])
    totals, norm_grad = lax.psum((squares, norm_grad), ("dp", "mp"))
    branch_rms = jnp.sqrt(totals / (visible_count * data_size * FLD_DEV * feature_count))
    qkv_new = renew_weight(qkv_weight, qkv_momentum, qkv_average, qkv_grad, MATRIX_RATE)
    out_new = renew_weight(out_weight, out_momentum, out_average, out_grad, OUTPUT_RATE)
    up_new = renew_weight(up_weight, up_momentum, up_average, up_grad, MATRIX_RATE)
    down_new = renew_weight(down_weight, down_momentum, down_average, down_grad, MATRIX_RATE)
    norm_new = renew_weight(norm_params, norm_momentum, norm_average, norm_grad, NORM_RATE)
    return (
        block_out,
        input_grad,
        branch_rms,
        qkv_new[0],
        qkv_new[1],
        qkv_new[2],
        qkv_new[3],
        out_new[0],
        out_new[1],
        out_new[2],
        out_new[3],
        up_new[0],
        up_new[1],
        up_new[2],
        up_new[3],
        down_new[0],
        down_new[1],
        down_new[2],
        down_new[3],
        norm_new[0],
        norm_new[1],
        norm_new[2],
        norm_new[3],
    )


def solution(mesh):
    in_specs = (
        P("dp", None, None),
        P("dp", None),
        P("dp", "mp", None),
        P(None, "dp", "mp"),
        P(None, "dp", "mp"),
        P(None, "dp", "mp"),
        P("mp", "dp"),
        P("mp", "dp"),
        P("mp", "dp"),
        P("dp", "mp"),
        P("dp", "mp"),
        P("dp", "mp"),
        P("mp", "dp"),
        P("mp", "dp"),
        P("mp", "dp"),
        P(),
        P(),
        P(),
    )
    out_specs = (
        P("dp", "mp", None),
        P("dp", "mp", None),
        P(),
        P(None, "dp", "mp"),
        P(None, "dp", "mp"),
        P(None, "dp", "mp"),
        P(None, "dp", "mp"),
        P("mp", "dp"),
        P("mp", "dp"),
        P("mp", "dp"),
        P("mp", "dp"),
        P("dp", "mp"),
        P("dp", "mp"),
        P("dp", "mp"),
        P("dp", "mp"),
        P("mp", "dp"),
        P("mp", "dp"),
        P("mp", "dp"),
        P("mp", "dp"),
        P(),
        P(),
        P(),
        P(),
    )
    local = local_fused if fits_fused(mesh) else local_general
    return jax.shard_map(local, mesh=mesh, in_specs=in_specs, out_specs=out_specs, check_vma=False)
```

```python
import functools

import jax
import jax.numpy as jnp
from jax import lax
from jax.experimental import pallas as pl
from jax.experimental.pallas import tpu as pltpu
from jax.sharding import PartitionSpec as P

HDIM = 64
FLD_DEV = 64


NORM_EPS = 1e-06
MOMENTUM_RATE = 0.9
MATRIX_RATE = 4e-05
OUTPUT_RATE = 0.00025
NORM_RATE = 0.0003
AVERAGE_DECAY = 0.7


def layer_norm(row_values, norm_gain, norm_shift):
    center = row_values - jnp.mean(row_values, axis=-1, keepdims=True)
    spread = jnp.mean(center * center, axis=-1, keepdims=True)
    return center * lax.rsqrt(spread + NORM_EPS) * norm_gain + norm_shift


def gelu_exact(values):
    return jax.nn.gelu(values, approximate=False)


def renew_weight(weight, momentum, average, gradient, step_rate):
    moment = MOMENTUM_RATE * momentum + gradient
    updated = weight - step_rate * (gradient + MOMENTUM_RATE * moment)
    smooth = AVERAGE_DECAY * average + (1.0 - AVERAGE_DECAY) * updated
    return (moment, updated, smooth, updated.astype(jnp.bfloat16))


BF = jnp.bfloat16
F32 = jnp.float32
MESH_ID = pl.DeviceIdType.MESH
WIDE = 768
VMEM_BYTES = 63 * 1024 * 1024
AG_CHUNKS = ((0, 1, 0, 384), (0, 1, 384, 384), (1, 2, 0, 256), (1, 2, 256, 256), (1, 2, 512, 256))
CHUNKS = ((0, 1, 0, 384), (0, 1, 384, 384), (1, 2, 0, 256), (1, 2, 256, 256), (1, 2, 512, 256))
AG_ROWS = ((48, 48, 0), (48, 48, 0), (48, 48, 0), (48, 48, 0), (48, 48, 0))
RS_ROWS = ((48, 0, 48), (48, 0, 48), (48, 0, 48), (48, 0, 48), (48, 0, 48))


def dot_nn(a, b):
    return jnp.dot(a, b, preferred_element_type=F32)


def dot_nt(a, b):
    return lax.dot_general(a, b, (((1,), (1,)), ((), ())), preferred_element_type=F32)


def dot_tn(a, b):
    return lax.dot_general(a, b, (((0,), (0,)), ((), ())), preferred_element_type=F32)


def gelu_pair(v):
    size = jnp.abs(v)
    bell = jnp.exp(v * v * -0.5)
    t = 1.0 / (1.0 + (0.3275911 * 0.7071067811865476) * size)
    poly = t * (
        0.254829592
        + t * (-0.284496736 + t * (1.421413741 + t * (-1.453152027 + t * 1.061405429)))
    )
    tail = 0.5 * poly * bell
    phi = jnp.where(v < 0.0, tail, 1.0 - tail)
    return v * phi, phi + v * bell * 0.3989422804014327


def lnorm(v, gain, shift):
    center = v - jnp.mean(v, axis=-1, keepdims=True)
    rs = lax.rsqrt(jnp.mean(center * center, axis=-1, keepdims=True) + NORM_EPS)
    return center * rs * gain + shift


def lnorm_back(v, e, gain):
    center = v - jnp.mean(v, axis=-1, keepdims=True)
    rs = lax.rsqrt(jnp.mean(center * center, axis=-1, keepdims=True) + NORM_EPS)
    xhat = center * rs
    eg = e * gain
    dv = rs * (
        eg - jnp.mean(eg, axis=-1, keepdims=True) - xhat * jnp.mean(eg * xhat, axis=-1, keepdims=True)
    )
    return dv, e * xhat


def rs_buffers(k):
    nm, nc = CHUNKS[k][1], CHUNKS[k][3]
    r1, r2, r3 = RS_ROWS[k]
    made = [(name, (n, nm, 1, 1, 1, 1, 96, nc)) for name, n in (("x", 4), ("y", 4), ("z", 3))]
    if r1:
        made.append(("3y", (nm, 1, 1, 4, 1, r1, nc)))
    if r2:
        made.append(("3x", (nm, 1, 1, 4, 1, r2, nc)))
    if r3:
        made += [("dz", (3, nm, 1, 1, 1, 1, r3, nc)), ("d", (nm, 1, 1, 1, 1, r3, nc))]
    return made


def layer_kernel(
    sizes,
    tok_hbm,
    mask_hbm,
    cot_hbm,
    qkv_hbm,
    out_hbm,
    up_hbm,
    down_hbm,
    norm_hbm,
    gout_hbm,
    bo_out,
    ig_out,
    stats_ref,
    G,
    PA,
    RSC,
    *rest,
):
    names = [(k, name) for k in range(len(CHUNKS)) for name, _ in rs_buffers(k)]
    n_bufs = len(names)
    RSB = dict(zip(names, rest[:n_bufs]))
    (
        tok_s, key_s, live_s, band_s, x_s, nin_s, qkv_s, ctx_s, mid_s, nm_s, nmT_s, ninT_s,
        cot_s, dmT_s, g_s, d_s, mlp_s, dmn_s, st_send, st_recv,
        mask_ref, qkv_ref, out_ref, norm_ref, gout_ref, loc_sem, g_sem, ag_send, ag_recv, rs_send, rs_recv, ex_send, ex_recv, st_ss, st_rs,
    ) = rest[n_bufs:]
    X, C, Z, Y = sizes
    dp = lax.axis_index("dp")
    mp = lax.axis_index("mp")
    me = {"z": lax.div(dp, Y), "y": lax.rem(dp, Y), "x": lax.div(mp, C), "c": lax.rem(mp, C)}
    size_of = {"x": X, "c": C, "z": Z, "y": Y}

    def device(**over):
        at = dict(me, **over)
        return (at["z"] * Y + at["y"], at["x"] * C + at["c"])

    def shifted(axis, delta):
        return lax.rem(me[axis] + delta, size_of[axis])

    def place(whole, **over):
        return tuple(slice(None) if a in whole else pl.ds(over.get(a, me[a]), 1) for a in "xczy")

    def remote(src, dst, ss, rs, dev):
        return pltpu.make_async_remote_copy(
            src_ref=src, dst_ref=dst, send_sem=ss, recv_sem=rs, device_id=dev, device_id_type=MESH_ID
        )

    far = {a: size_of[a] - 1 - me[a] for a in "xyc"}
    waited = set()

    def wait_recv(kind, k, *names):
        for name in names:
            if (kind, k, name) not in waited:
                waited.add((kind, k, name))
                (ag_copy if kind == "ag" else rs_copy)(k, name).wait_recv()

    def quadrant(q):
        return (far["x"] if q % 2 else me["x"]), (far["y"] if q // 2 else me["y"])

    def bands(table, k):
        r1, r2, r3 = table[k]
        return {"y": pl.ds(0, r1), "x": pl.ds(r1, r2), "z": pl.ds(r1 + r2, r3)}

    def part(buf, b0, chunk, x, c, z, y, rows):
        _, nm, c0, nc = chunk
        at_z = slice(None) if z is None else pl.ds(z, 1)
        return buf.at[pl.ds(b0, nm), pl.ds(x, 1), pl.ds(c, 1), at_z, pl.ds(y, 1), rows, pl.ds(c0, nc)]

    ALL = slice(0, 96)
    AG_NAMES = ("z1", "z2", "z3", "x0", "y0", "x1", "x2", "x3", "y1", "y2", "y3",
                "d", "dz1", "dz2", "dz3", "3y", "3x", "c0", "c1", "c2", "c3")
    RS_NAMES = ("c0", "c1", "c2", "c3", "3y", "3x", "dz1", "dz2", "dz3", "d",
                "x0", "x1", "x2", "x3", "y0", "y1", "y2", "y3", "z1", "z2", "z3")

    def ag_copy(k, name):
        rows = bands(AG_ROWS, k)
        x, y, z, c = me["x"], me["y"], me["z"], me["c"]
        band, to = ALL, {}
        if name[0] == "c":
            (x, y), z, to = quadrant(int(name[1])), None, {"c": far["c"]}
        elif name == "3y":
            x, z, band, to = far["x"], None, rows["y"], {"y": far["y"]}
        elif name == "3x":
            y, z, band, to = far["y"], None, rows["x"], {"x": far["x"]}
        elif name == "d":
            x, band, to = far["x"], rows["z"], {"y": far["y"]}
        elif name[:2] == "dz":
            x, y, band, to = far["x"], far["y"], rows["z"], {"z": shifted("z", int(name[2]))}
        elif name[0] == "z":
            to = {"z": shifted("z", int(name[1]))}
        else:
            z, to = shifted("z", Z - int(name[1])), {name[0]: far[name[0]]}
        ref = part(G, AG_CHUNKS[k][0], AG_CHUNKS[k], x, c, z, y, band)
        at = AG_NAMES.index(name)
        return remote(ref, ref, ag_send.at[k, at], ag_recv.at[k, at], device(**to))

    def ag_names(k):
        r1, r2, r3 = AG_ROWS[k]
        none = (() if r1 else ("3y",)) + (() if r2 else ("3x",)) + (() if r3 else ("d", "dz1", "dz2", "dz3"))
        return [n for n in AG_NAMES if n not in none]

    def ag_start(k, *names):
        for name in names:
            ag_copy(k, name).start()

    def ag_z(k):
        ag_start(k, "z1", "z2", "z3")

    def ag_own(k, axis):
        ag_start(k, axis + "0")

    def ag_pass(k, axis, d):
        wait_recv("ag", k, f"z{d}")
        ag_start(k, f"{axis}{d}")

    def ag_diag(k):
        wait_recv("ag", k, "x0")
        ag_start(k, "d")

    def ag_diag_z(k):
        wait_recv("ag", k, "d")
        ag_start(k, "dz1", "dz2", "dz3")

    def ag_last(k, axis):
        side = "x" if axis == "y" else "y"
        wait_recv("ag", k, *(f"{side}{d}" for d in range(4)))
        ag_start(k, "3" + axis)

    def ag_core(k, q):
        if q == 3:
            wait_recv("ag", k, *(n for n in ag_names(k) if n[0] in "3d"))
        else:
            wait_recv("ag", k, *(f"{'zxy'[q]}{d}" for d in range(0 if q else 1, 4)))
        ag_start(k, f"c{q}")

    def ag_ready(k):
        wait_recv("ag", k, "c0", "c1", "c2", "c3")

    def ag_sent(k):
        for name in ag_names(k):
            ag_copy(k, name).wait_send()

    def grads_of(k):
        return (PA, 0) if CHUNKS[k][0] == 0 else (G, CHUNKS[k][0])

    def rs_copy(k, name):
        buf, b0 = grads_of(k)
        m0, nm, c0, nc = CHUNKS[k]
        rows = bands(RS_ROWS, k)
        x, y, z, c = me["x"], me["y"], me["z"], me["c"]
        band = ALL
        if name[0] == "c":
            (x, y), z, c = quadrant(int(name[1])), None, far["c"]
            to, dst = {"c": far["c"]}, part(RSC, m0, CHUNKS[k], x, 0, None, y, ALL)
        else:
            d = int(name[-1]) if name[-1] in "0123" else 0
            if name == "3y" or name == "3x":
                x, y, z, band, to = far["x"], far["y"], None, rows[name[1]], {name[1]: far[name[1]]}
                dst = RSB[k, name]
            elif name == "d":
                x, y, band, to, dst = far["x"], far["y"], rows["z"], {"y": far["y"]}, RSB[k, "d"]
            elif name[:2] == "dz":
                z = shifted("z", d)
                x, y, band, to, dst = far["x"], far["y"], rows["z"], {"z": z}, RSB[k, "dz"].at[d - 1]
            elif name[0] == "z":
                z = shifted("z", d)
                to, dst = {"z": z}, RSB[k, "z"].at[d - 1]
            else:
                z = shifted("z", d)
                to, dst = {name[0]: far[name[0]]}, RSB[k, name[0]].at[d]
                if name[0] == "x":
                    x = far["x"]
                else:
                    y = far["y"]
        at = RS_NAMES.index(name)
        return remote(part(buf, b0, CHUNKS[k], x, c, z, y, band), dst, rs_send.at[k, at], rs_recv.at[k, at], device(**to))

    def rs_names(k):
        r1, r2, r3 = RS_ROWS[k]
        none = (() if r1 else ("3y",)) + (() if r2 else ("3x",)) + (() if r3 else ("d", "dz1", "dz2", "dz3"))
        return [n for n in RS_NAMES if n not in none]

    def rs_start(k, *names):
        for name in names:
            rs_copy(k, name).start()

    def rs_core(k, q):
        rs_start(k, f"c{q}")

    def rs_first(k, axis):
        rs_start(k, "3" + axis)

    def rs_diag_z(k):
        rs_start(k, "dz1", "dz2", "dz3")

    def rs_diag(k):
        rs_start(k, "d")

    def rs_side(k, axis, d):
        rs_start(k, f"{axis}{d}")

    def rs_z(k, d):
        rs_start(k, f"z{d}")

    def rs_sum(k, x, y, zs, rows, terms):
        buf, b0 = grads_of(k)
        _, nm, c0, nc = CHUNKS[k]

        def one(t, carry):
            mat, zi = lax.div(t, zs[1]), lax.rem(t, zs[1])
            at = (b0 + mat, x, me["c"], zs[0] + zi, y, rows, pl.ds(c0, nc))
            more = terms(mat, zi)
            if len(more) == 1:
                buf[at] = buf[at] + more[0]
            else:
                total = buf[at].astype(F32)
                for term in more:
                    total = total + term.astype(F32)
                buf[at] = total.astype(BF)
            return carry

        lax.fori_loop(0, nm * zs[1], one, 0)

    def rs_add_core(k, q):
        wait_recv("rs", k, f"c{q}")
        x, y = quadrant(q)
        m0, _, c0, nc = CHUNKS[k]
        rs_sum(k, x, y, (0, Z), ALL, lambda mat, zi: [RSC[m0 + mat, x, 0, zi, y, :, pl.ds(c0, nc)]])

    def rs_add_first(k, axis):
        wait_recv("rs", k, "3" + axis)
        x, y = (far["x"], me["y"]) if axis == "y" else (me["x"], far["y"])
        came = RSB[k, "3" + axis]
        rs_sum(k, x, y, (0, Z), bands(RS_ROWS, k)[axis], lambda mat, zi: [came[mat, 0, 0, zi, 0]])

    def rs_add_diag_z(k):
        wait_recv("rs", k, "dz1", "dz2", "dz3")
        came = RSB[k, "dz"]
        rs_sum(k, far["x"], far["y"], (me["z"], 1), bands(RS_ROWS, k)["z"],
               lambda mat, zi: [came[n, mat, 0, 0, 0, 0] for n in range(3)])

    def rs_add_diag(k):
        wait_recv("rs", k, "d")
        came = RSB[k, "d"]
        rs_sum(k, far["x"], me["y"], (me["z"], 1), bands(RS_ROWS, k)["z"],
               lambda mat, zi: [came[mat, 0, 0, 0, 0]])

    def rs_add_side(k, d):
        wait_recv("rs", k, f"x{d}", f"y{d}")
        rs_sum(k, me["x"], me["y"], (shifted("z", d), 1), ALL,
               lambda mat, zi: [RSB[k, a][d, mat, 0, 0, 0, 0] for a in "xy"])

    def rs_final(k):
        wait_recv("rs", k, "x0", "y0", "z1", "z2", "z3")
        buf, b0 = grads_of(k)
        m0, nm, c0, nc = CHUNKS[k]
        cols = pl.ds(c0, nc)
        for mat in range(nm):
            total = buf[b0 + mat, me["x"], me["c"], me["z"], me["y"], :, cols].astype(F32)
            for a in "xy":
                total = total + RSB[k, a][0, mat, 0, 0, 0, 0].astype(F32)
            for n in range(3):
                total = total + RSB[k, "z"][n, mat, 0, 0, 0, 0].astype(F32)
            gout_ref[m0 + mat, :, cols] = total
        home(k).start()

    def home(k):
        m0, nm, c0, nc = CHUNKS[k]
        at = (pl.ds(m0, nm), slice(None), pl.ds(c0, nc))
        return pltpu.make_async_copy(gout_ref.at[at], gout_hbm.at[at], g_sem.at[k])

    def rs_sent(k):
        for name in rs_names(k):
            rs_copy(k, name).wait_send()

    mates = [(0, 1), (1, 0), (1, 1)]

    def mate(j):
        dx, dc = mates[j]
        x2, c2 = lax.rem(me["x"] + dx, X), lax.rem(me["c"] + dc, C)
        return device(x=x2, c=c2), x2 * C + c2

    slab = pl.ds(pl.multiple_of(mp * 32, 32), 32)

    def rows_of(index):
        return pl.ds(pl.multiple_of(index * 32, 32), 32)

    def exchange(which, j):
        two = pl.ds(2 * j, 2)
        made = []
        for n in range(3):
            dev, index = mate(n)
            if which == 0:
                src, dst = cot_hbm.at[index, two], cot_s.at[two, slab, :]
            else:
                src = (nm_s if which == 1 else cot_s).at[two, rows_of(index), :]
                dst = (bo_out if which == 1 else ig_out).at[mp, two]
            made.append(remote(src, dst, ex_send.at[which, j, n], ex_recv.at[which, j, n], dev))
        return made

    cot_own = pltpu.make_async_copy(cot_hbm.at[mp], cot_s.at[:, slab, :], loc_sem.at[0])
    tok_copy = pltpu.make_async_copy(
        tok_hbm.at[pl.ds(pl.multiple_of(mp * 1536, 1536), 1536)], tok_s, loc_sem.at[1]
    )
    bo_own = pltpu.make_async_copy(nm_s.at[:, slab, :], bo_out.at[mp], loc_sem.at[2])
    ig_own = pltpu.make_async_copy(cot_s.at[:, slab, :], ig_out.at[mp], loc_sem.at[3])

    st_axes = "cyxz"

    def st_copies(i):
        axis = st_axes[i]
        return [
            remote(
                st_send.at[i], st_recv.at[i + delta - 1], st_ss.at[i + delta - 1], st_rs.at[i + delta - 1],
                device(**{axis: shifted(axis, delta)}),
            )
            for delta in range(1, size_of[axis])
        ]

    def st_step(i):
        if i == 0:
            total = stats_ref[...]
        else:
            copies = st_copies(i - 1)
            for c in copies:
                c.wait_recv()
            total = st_send[i - 1]
            for n in range(len(copies)):
                total = total + st_recv[i - 1 + n]
        if i < 4:
            st_send[i] = total
            for c in st_copies(i):
                c.start()
        else:
            stats_ref[...] = total

    def low_norm(n):
        return norm_ref[n:n + 1, :].astype(BF).astype(F32)

    lane = lax.broadcasted_iota(jnp.int32, (1, 128), 1)
    lo = (lane < 64).astype(F32).astype(BF)
    hi = (lane >= 64).astype(F32).astype(BF)
    low_eighth = jnp.where(lane < 64, 0.125, 1.0)

    def weight(mat, m, c0, nc):
        m = jnp.int32(m)
        return G[mat, lax.div(m, C), lax.rem(m, C), :, :, :, pl.ds(c0, nc)].reshape(WIDE, nc)

    def put(buf, mat, m, c0, nc, value):
        m = jnp.int32(m)
        buf[mat, lax.div(m, C), lax.rem(m, C), :, :, :, pl.ds(c0, nc)] = value.reshape(Z, Y, 96, nc)

    def block(b):
        return pl.ds(pl.multiple_of(b * 128, 128), 128)

    def rows256(t):
        return pl.ds(pl.multiple_of(t * 256, 256), 256)

    def setup():
        loads[8].wait()
        loads[9].wait()
        col = lax.broadcasted_iota(jnp.int32, (64, 64), 1)
        row = lax.broadcasted_iota(jnp.int32, (64, 64), 0)
        marks = mask_ref[...].astype(F32)
        before = dot_nn(jnp.where(col < row, 1.0, 0.0).astype(BF), marks.astype(BF))
        key_s[...] = jnp.where(marks > 0.0, before, -1.0).astype(BF)
        ri = lax.broadcasted_iota(jnp.int32, (128, 128), 0) // 8 % 4
        ci = lax.broadcasted_iota(jnp.int32, (128, 128), 1) // 8 % 4
        band_s[...] = jnp.where(ri == ci, 0.0, -1e30)
        stats_ref[...] = jnp.zeros_like(stats_ref)
        mid_s[...] = jnp.zeros_like(mid_s)

    def take_block(b, carry):
        slot = lax.broadcasted_iota(jnp.int32, (key_s.shape[1], 128), 0)
        row = lax.broadcasted_iota(jnp.int32, (key_s.shape[1], 128), 1)
        owner = (mp * 6 + b) * 4 + row // 8 % 4
        rank = dot_nn(key_s[...], jnp.where(slot == owner, 1.0, 0.0).astype(BF))
        row = lax.broadcasted_iota(jnp.int32, (64, 128), 1)
        hit = jnp.where(rank == (row // 32 * 8 + row % 8).astype(F32), 1.0, 0.0)
        pick = jnp.concatenate([jnp.where(row // 8 % 4 == n, hit, 0.0) for n in range(4)], axis=0)
        live_s[block(b), :] = jnp.broadcast_to(jnp.sum(hit, axis=0, keepdims=True), (128, 128)).T
        x = dot_tn(pick.astype(BF), tok_s[pl.ds(pl.multiple_of(b * 256, 256), 256), :])
        x_s[block(b), :] = x.astype(BF)
        nin_s[block(b), :] = lnorm(x, low_norm(0), low_norm(1)).astype(BF)
        return carry

    def qkv_first(m, carry):
        w = weight(0, m, 0, 384)
        for t in range(3):
            rows = pl.ds(t * 256, 256)
            out = dot_nn(nin_s[rows, :], w)
            qkv_s[m, rows, 0:128] = (out[:, :128] * 0.125).astype(BF)
            qkv_s[m, rows, 128:384] = out[:, 128:].astype(BF)
        return carry

    def qkv_second(m, carry):
        w = weight(0, m, 384, 256)
        for t in range(3):
            rows = pl.ds(t * 256, 256)
            out = dot_nn(nin_s[rows, :], w)
            first = out[:, :128] * low_eighth
            qkv_s[m, rows, 384:512] = first.astype(BF)
            qkv_s[m, rows, 512:640] = pltpu.roll(first, 64, 1).astype(BF)
            qkv_s[m, rows, 640:768] = pltpu.roll(out[:, 128:], 64, 1).astype(BF)
        return carry

    def keep_p(i, h, p):
        rows = pl.ds(pl.multiple_of(i * 64, 64), 64)
        tok_s[rows, h * 128:(h + 1) * 128] = p[:64]
        tok_s[rows, 384 + h * 128:512 + h * 128] = p[64:]

    def kept_p(i, h):
        rows = pl.ds(pl.multiple_of(i * 64, 64), 64)
        return jnp.concatenate(
            [tok_s[rows, h * 128:(h + 1) * 128], tok_s[rows, 384 + h * 128:512 + h * 128]], axis=0
        )

    def softmax(s):
        e = jnp.exp(s - jnp.max(s, axis=0, keepdims=True))
        return (e * (1.0 / jnp.sum(e, axis=0, keepdims=True))).astype(BF)

    def attend_first(j, carry):
        at = [(lax.div(j, 2), lax.rem(j, 2) * 3 + u) for u in range(3)]
        qs, ks, vs = ([qkv_s[m, block(b), n * 128:(n + 1) * 128] for m, b in at] for n in range(3))
        scores = [dot_nt(k, q * side) + band_s[...] for q, k in zip(qs, ks) for side in (lo, hi)]
        probs = [softmax(x) for x in scores]
        for u, (m, b) in enumerate(at):
            p0, p1 = probs[2 * u], probs[2 * u + 1]
            keep_p(m * 6 + b, 0, p0)
            keep_p(m * 6 + b, 1, p1)
            ctx_s[m, block(b), 128:256] = (dot_tn(p0, vs[u] * lo) + dot_tn(p1, vs[u] * hi)).astype(BF)
        return carry

    def attend_second(j, carry):
        at = [(j, u) for u in range(6)]
        qs, ks, vs = ([qkv_s[m, block(b), n * 128:(n + 1) * 128] for m, b in at] for n in range(3, 6))
        scores = [dot_nt(k, q * lo) + band_s[...] for q, k in zip(qs, ks)]
        probs = [softmax(x) for x in scores]
        for u, (m, b) in enumerate(at):
            keep_p(m * 6 + b, 2, probs[u])
            ctx_s[m, block(b), 0:128] = dot_tn(probs[u], vs[u] * hi).astype(BF)
        return carry

    def mid_tile(m, carry):
        w = weight(0, m, 512, 256)
        for t in range(3):
            rows = pl.ds(t * 256, 256)
            mid_s[rows, :] += dot_nt(ctx_s[m, rows, :], w)
        return carry

    def mid_block(b, carry):
        rows = block(b)
        attn = mid_s[rows, :]
        live = live_s[rows, :][:, :1]
        stats_ref[4:5, :] += jnp.sum(attn * attn * live, axis=0, keepdims=True)
        mid = x_s[rows, :].astype(F32) + attn
        mid_s[rows, :] = mid
        nm_s[b] = lnorm(mid, low_norm(2), low_norm(3)).astype(BF)
        return carry

    def transpose_into(dst, src):
        def one(b, carry):
            part = src(b)
            for j in range(6):
                dst[pl.ds(j * 128, 128), block(b)] = part[:, j * 128:(j + 1) * 128].T
            return carry

        lax.fori_loop(0, 6, one, 0)

    def cot_block(b, carry):
        live = live_s[block(b), :][:, :1]
        cot_s[b] = (cot_s[b].astype(F32) * live).astype(BF)
        return carry

    def mlp_pair(c0, nc):
        def tile(j, carry):
            pair = [2 * j, 2 * j + 1]
            w_up = [weight(1, m, c0, nc) for m in pair]
            w_down = [weight(2, m, c0, nc) for m in pair]
            for t in range(3):
                rows = pl.ds(t * 256, 256)
                normed = nm_s[2 * t:2 * t + 2].reshape(256, WIDE)
                wanted = cot_s[2 * t:2 * t + 2].reshape(256, WIDE)
                for u in range(2):
                    act, slope = gelu_pair(dot_nn(normed, w_up[u]))
                    d_act = dot_nn(wanted, w_down[u])
                    g_s[rows, u * 256:(u + 1) * 256] = act.astype(BF)
                    d_s[rows, u * 256:(u + 1) * 256] = (d_act * slope).astype(BF)
            for t in range(3):
                rows = pl.ds(t * 256, 256)
                for h in range(3):
                    cols = slice(h * 256, (h + 1) * 256)
                    for total, held, w in ((mlp_s, g_s, w_down), (dmn_s, d_s, w_up)):
                        total[rows, cols] += dot_nt(held[rows, 0:256], w[0][cols]) + dot_nt(
                            held[rows, 256:512], w[1][cols]
                        )
            for u, m in enumerate(pair):
                put(G, 2, m, c0, nc, dot_nn(dmT_s[...], g_s[:, u * 256:(u + 1) * 256]).astype(BF))
                put(G, 1, m, c0, nc, dot_nn(nmT_s[...], d_s[:, u * 256:(u + 1) * 256]).astype(BF))
            return carry

        return tile

    def end_block(b, carry):
        rows = block(b)
        live = live_s[rows, :][:, :1]
        mlp = mlp_s[rows, :]
        mid = mid_s[rows, :]
        out = (mid + mlp) * live
        stats_ref[5:6, :] += jnp.sum(mlp * mlp * live, axis=0, keepdims=True)
        stats_ref[6:7, :] += jnp.sum(out * out, axis=0, keepdims=True)
        nm_s[b] = out.astype(BF)
        e = dmn_s[rows, :]
        dv, ex = lnorm_back(mid, e, low_norm(2))
        stats_ref[2:3, :] += jnp.sum(ex, axis=0, keepdims=True)
        stats_ref[3:4, :] += jnp.sum(e, axis=0, keepdims=True)
        d_mid = cot_s[b].astype(F32) + dv
        mlp_s[rows, :] = d_mid
        cot_s[b] = d_mid.astype(BF)
        return carry

    def dctx_tile(m, carry):
        w = weight(0, m, 512, 256)
        for t in range(3):
            rows = pl.ds(t * 256, 256)
            out = dot_nn(cot_s[2 * t:2 * t + 2].reshape(256, WIDE), w)
            g_s[rows, 0:256] = out.astype(BF)
            g_s[rows, 256:384] = pltpu.roll(out[:, :128], 64, 1).astype(BF)
        return carry

    def score_back(p, d_probs):
        pf = p.astype(F32)
        w = pf * d_probs
        return (w - pf * jnp.sum(w, axis=0, keepdims=True)).astype(BF)

    def attend_back(j, carry):
        m = lax.div(j, 2)
        at = [lax.rem(j, 2) * 3 + u for u in range(3)]
        held = [[qkv_s[m, block(b), n * 128:(n + 1) * 128] for n in range(6)] for b in at]
        came = [[g_s[block(b), n * 128:(n + 1) * 128] for n in range(3)] for b in at]
        probs = [[kept_p(m * 6 + b, h) for h in range(3)] for b in at]
        d_probs = [
            [dot_nt(v, d01 * lo), dot_nt(v, d01 * hi), dot_nt(v2, d2 * hi)]
            for (q, k, v, q2, k2, v2), (d2, d01, d2r) in zip(held, came)
        ]
        d_scores = [[score_back(p, d) for p, d in zip(ps, ds)] for ps, ds in zip(probs, d_probs)]
        for b, (q, k, v, q2, k2, v2), (d2, d01, d2r), (p0, p1, p2), (s0, s1, s2) in zip(
            at, held, came, probs, d_scores
        ):
            dk = dot_nn(s0, q * lo) + dot_nn(s1, q * hi)
            dv = dot_nn(p0, d01 * lo) + dot_nn(p1, d01 * hi)
            dv2 = dot_nn(p2, d2r * lo)
            dq = dot_tn(s0, k * lo) + dot_tn(s1, k * hi)
            dqk2 = dot_tn(s2, k2 * lo) * 0.125 + dot_nn(s2, k2 * hi)
            for n, out in enumerate((dq * 0.125, dk, dv, dqk2, dv2)):
                qkv_s[m, block(b), n * 128:(n + 1) * 128] = out.astype(BF)
        return carry

    def put_all(m, c0, nc, value):
        put(PA, 0, m, c0, nc, value)

    def grad_a0(m, carry):
        put_all(m, 0, 384, dot_nn(ninT_s[...], qkv_s[m, :, 0:384]).astype(BF))
        return carry

    def grad_a1(m, carry):
        out_part = dot_nn(dmT_s[...], ctx_s[m])
        qkv_part = dot_nn(ninT_s[...], qkv_s[m, :, 384:640])
        put_all(m, 384, 128, qkv_part[:, :128].astype(BF))
        put_all(m, 512, 128, (qkv_part[:, 128:] + out_part[:, :128]).astype(BF))
        put_all(m, 640, 128, out_part[:, 128:].astype(BF))
        return carry

    def in_tile(m, carry):
        w = weight(0, m, 0, 640)
        for t in range(3):
            rows = pl.ds(t * 256, 256)
            dmn_s[rows, :] += dot_nt(qkv_s[m, rows, 0:640], w)
        return carry

    def in_block(b, carry):
        rows = block(b)
        e = dmn_s[rows, :]
        dv, ex = lnorm_back(x_s[rows, :].astype(F32), e, low_norm(0))
        stats_ref[0:1, :] += jnp.sum(ex, axis=0, keepdims=True)
        stats_ref[1:2, :] += jnp.sum(e, axis=0, keepdims=True)
        live = live_s[rows, :][:, :1]
        cot_s[b] = ((mlp_s[rows, :] + dv) * live).astype(BF)
        return carry

    def loop(first, last, body):
        if last == first + 1:
            body(jnp.int32(first), 0)
        else:
            lax.fori_loop(first, last, body, 0)

    def turn_in():
        transpose_into(ninT_s, lambda b: nin_s[block(b), :])

    def cot_start(j):
        for c in exchange(0, j):
            c.start()

    def cot_ready():
        cot_own.wait()
        for j in range(3):
            for c in exchange(0, j):
                c.wait_recv()
        loop(0, 6, cot_block)
        transpose_into(dmT_s, lambda b: cot_s[b])
        mlp_s[...] = jnp.zeros_like(mlp_s)
        dmn_s[...] = jnp.zeros_like(dmn_s)

    def middle():
        loop(0, 6, mid_block)
        transpose_into(nmT_s, lambda b: nm_s[b])

    def turn():
        dmn_s[...] = jnp.zeros_like(dmn_s)
        transpose_into(dmT_s, lambda b: cot_s[b])

    def bo_start(j):
        for c in exchange(1, j):
            c.start()
        if j == 2:
            bo_own.start()

    def ig_start(j):
        for c in exchange(2, j):
            c.start()
        if j == 2:
            ig_own.start()

    def finish():
        for k in range(len(AG_CHUNKS)):
            if AG_CHUNKS[k][0] == 0:
                ag_sent(k)
        for k in range(len(CHUNKS)):
            rs_sent(k)
            home(k).wait()
        for j in range(3):
            for c in exchange(0, j):
                c.wait_send()
            for c in (*exchange(1, j), *exchange(2, j)):
                c.wait()
        bo_own.wait()
        ig_own.wait()
        for i in range(4):
            for c in st_copies(i):
                c.wait_send()

    first_in = {
        4: (qkv_hbm, qkv_ref), 5: (out_hbm, out_ref), 6: (up_hbm, mlp_s.at[pl.ds(0, 96)]),
        7: (down_hbm, mlp_s.at[pl.ds(96, 96)]), 8: (mask_hbm, mask_ref), 9: (norm_hbm, norm_ref),
    }
    loads = {n: pltpu.make_async_copy(src, dst, loc_sem.at[n]) for n, (src, dst) in first_in.items()}
    for copy in (*loads.values(), tok_copy, cot_own):
        copy.start()
    barrier = pltpu.get_barrier_semaphore()
    greet = [device(c=1 - me["c"]), device(y=1 - me["y"]), device(x=1 - me["x"]),
             device(x=1 - me["x"], c=1 - me["c"])]
    greet += [device(z=shifted("z", n)) for n in range(1, Z)]
    for dev in greet:
        pl.semaphore_signal(barrier, inc=1, device_id=dev, device_id_type=MESH_ID)
    here = (me["x"], me["c"], me["z"], me["y"], slice(None))
    loads[4].wait()
    for t in range(3):
        G[(0, *here, pl.ds(t * 128, 128))] = qkv_ref[t, :, 0:128].astype(BF)
    pl.semaphore_wait(barrier, len(greet))

    def rest_of_first():
        last = [qkv_ref[t, :, 128:192] for t in range(3)]
        loads[5].wait()
        out_t = out_ref[...].T
        G[(0, *here, pl.ds(384, 128))] = jnp.concatenate(last[:2], axis=1).astype(BF)
        G[(0, *here, pl.ds(512, 128))] = jnp.concatenate([last[2], out_t[:, 128:192]], axis=1).astype(BF)
        G[(0, *here, pl.ds(640, 128))] = out_t[:, 0:128].astype(BF)

    def rest_of_weights():
        loads[6].wait()
        loads[7].wait()
        G[(1, *here, slice(None))] = mlp_s[0:96, :].astype(BF)
        G[(2, *here, slice(None))] = mlp_s[96:192, :].astype(BF)

    ag_own(0, 'x')
    cot_start(0)
    setup()
    rest_of_first()
    ag_own(1, 'y')
    ag_z(0)
    tok_copy.wait()
    loop(0, 2, take_block)
    cot_start(1)
    loop(2, 4, take_block)
    ag_z(1)
    rest_of_weights()
    ag_own(3, 'y')
    ag_pass(0, 'y', 1)
    cot_start(2)
    ag_own(4, 'y')
    ag_pass(0, 'x', 3)
    ag_pass(0, 'x', 1)
    ag_core(0, 0)
    ag_pass(0, 'y', 2)
    loop(4, 6, take_block)
    ag_own(0, 'y')
    ag_z(2)
    ag_z(3)
    ag_pass(0, 'x', 2)
    ag_pass(1, 'x', 1)
    ag_pass(1, 'x', 2)
    ag_pass(1, 'y', 2)
    ag_pass(1, 'y', 3)
    ag_pass(1, 'y', 1)
    ag_pass(0, 'y', 3)
    ag_pass(1, 'x', 3)
    ag_last(0, 'y')
    ag_own(1, 'x')
    ag_core(1, 0)
    ag_last(1, 'x')
    ag_last(1, 'y')
    ag_pass(2, 'y', 1)
    ag_core(1, 1)
    ag_last(0, 'x')
    ag_core(0, 1)
    ag_own(2, 'y')
    cot_ready()
    ag_own(2, 'x')
    ag_core(1, 2)
    ag_pass(3, 'x', 1)
    ag_core(1, 3)
    ag_pass(2, 'x', 1)
    ag_core(0, 3)
    ag_core(0, 2)
    ag_z(4)
    ag_pass(2, 'x', 3)
    ag_ready(1)
    loop(3, 4, qkv_second)
    ag_pass(2, 'y', 2)
    ag_pass(2, 'y', 3)
    loop(1, 2, qkv_second)
    loop(0, 1, qkv_second)
    ag_ready(0)
    loop(2, 3, qkv_second)
    turn_in()
    ag_pass(3, 'y', 2)
    loop(1, 2, qkv_first)
    ag_pass(3, 'x', 2)
    ag_pass(3, 'y', 3)
    loop(2, 3, qkv_first)
    ag_pass(2, 'x', 2)
    ag_pass(3, 'y', 1)
    loop(3, 4, attend_second)
    ag_core(2, 0)
    loop(1, 2, attend_second)
    ag_last(2, 'x')
    loop(4, 6, attend_first)
    ag_pass(3, 'x', 3)
    ag_own(3, 'x')
    loop(2, 4, attend_first)
    ag_pass(4, 'x', 1)
    ag_core(2, 2)
    loop(0, 1, qkv_first)
    loop(3, 4, qkv_first)
    ag_last(2, 'y')
    loop(0, 1, attend_second)
    loop(6, 8, attend_first)
    loop(0, 2, attend_first)
    ag_core(2, 1)
    loop(3, 4, mid_tile)
    ag_core(3, 0)
    ag_pass(4, 'y', 1)
    loop(1, 2, mid_tile)
    loop(2, 3, attend_second)
    ag_last(3, 'x')
    loop(0, 1, mid_tile)
    loop(2, 3, mid_tile)
    ag_core(2, 3)
    ag_pass(4, 'y', 2)
    middle()
    ag_own(4, 'x')
    ag_last(3, 'y')
    ag_pass(4, 'x', 2)
    ag_core(4, 0)
    ag_core(3, 1)
    ag_ready(2)
    ag_pass(4, 'x', 3)
    ag_core(3, 2)
    ag_sent(2)
    loop(0, 1, mlp_pair(0, 256))
    ag_pass(4, 'y', 3)
    ag_core(3, 3)
    loop(1, 2, mlp_pair(0, 256))
    ag_core(4, 2)
    rs_core(2, 1)
    ag_ready(3)
    rs_core(2, 3)
    rs_core(2, 2)
    ag_last(4, 'x')
    rs_core(2, 0)
    ag_last(4, 'y')
    ag_sent(3)
    loop(0, 1, mlp_pair(256, 256))
    rs_add_core(2, 3)
    rs_first(2, 'y')
    rs_add_core(2, 1)
    rs_add_core(2, 2)
    rs_side(2, 'y', 3)
    rs_diag_z(2)
    rs_side(2, 'y', 1)
    ag_core(4, 1)
    ag_core(4, 3)
    loop(1, 2, mlp_pair(256, 256))
    rs_core(3, 3)
    rs_add_core(2, 0)
    rs_side(2, 'y', 2)
    rs_core(3, 2)
    rs_add_first(2, 'y')
    ag_ready(4)
    ag_sent(4)
    loop(0, 1, mlp_pair(512, 256))
    rs_side(2, 'x', 2)
    rs_add_core(3, 3)
    rs_first(3, 'y')
    rs_core(3, 1)
    rs_side(2, 'x', 3)
    rs_diag_z(3)
    rs_side(2, 'x', 1)
    loop(1, 2, mlp_pair(512, 256))
    loop(0, 2, end_block)
    rs_add_core(3, 2)
    rs_core(4, 3)
    loop(2, 4, end_block)
    rs_add_side(2, 3)
    bo_start(1)
    rs_core(4, 2)
    rs_core(4, 1)
    rs_add_side(2, 2)
    loop(4, 6, end_block)
    rs_side(3, 'y', 1)
    rs_add_core(4, 3)
    rs_side(3, 'y', 2)
    bo_start(2)
    rs_add_side(2, 1)
    loop(0, 1, dctx_tile)
    rs_add_core(4, 2)
    rs_add_core(3, 1)
    rs_add_diag_z(2)
    rs_diag_z(4)
    turn()
    loop(0, 2, attend_back)
    rs_first(4, 'y')
    loop(1, 2, dctx_tile)
    rs_add_first(3, 'y')
    rs_side(3, 'x', 2)
    rs_side(3, 'x', 3)
    rs_diag(2)
    loop(2, 4, attend_back)
    loop(1, 2, grad_a0)
    rs_side(4, 'y', 3)
    rs_side(4, 'y', 2)
    rs_z(2, 3)
    rs_side(3, 'x', 1)
    loop(2, 3, dctx_tile)
    loop(4, 6, attend_back)
    loop(2, 3, grad_a0)
    rs_z(2, 1)
    rs_add_core(4, 1)
    rs_core(3, 0)
    loop(3, 4, dctx_tile)
    loop(0, 1, grad_a0)
    rs_side(3, 'y', 0)
    rs_z(2, 2)
    rs_add_first(4, 'y')
    rs_side(4, 'x', 1)
    rs_side(4, 'x', 2)
    loop(6, 8, attend_back)
    loop(3, 4, grad_a0)
    rs_core(0, 3)
    rs_core(4, 0)
    loop(3, 4, grad_a1)
    rs_side(4, 'x', 3)
    loop(0, 1, grad_a1)
    rs_add_core(0, 3)
    rs_first(0, 'y')
    rs_diag_z(0)
    loop(1, 3, grad_a1)
    rs_add_core(4, 0)
    rs_core(1, 3)
    rs_add_side(4, 2)
    rs_core(0, 1)
    rs_core(0, 0)
    rs_z(4, 2)
    rs_add_diag(2)
    bo_start(0)
    rs_side(3, 'y', 3)
    loop(2, 3, in_tile)
    rs_side(4, 'y', 1)
    rs_core(1, 0)
    rs_side(2, 'x', 0)
    rs_add_core(1, 3)
    rs_core(1, 1)
    loop(3, 4, in_tile)
    rs_core(1, 2)
    rs_add_core(0, 1)
    rs_add_first(0, 'y')
    rs_side(0, 'x', 1)
    rs_diag_z(1)
    loop(0, 1, in_tile)
    rs_side(0, 'x', 3)
    loop(1, 2, in_tile)
    rs_first(1, 'y')
    loop(0, 2, in_block)
    rs_core(0, 2)
    rs_add_core(3, 0)
    rs_add_side(4, 3)
    rs_add_core(1, 2)
    rs_add_core(0, 0)
    rs_add_diag_z(3)
    rs_side(0, 'x', 2)
    rs_diag(3)
    rs_add_side(3, 2)
    rs_z(4, 3)
    rs_add_side(4, 1)
    loop(2, 4, in_block)
    rs_side(1, 'y', 2)
    rs_z(3, 2)
    rs_add_core(1, 1)
    rs_add_core(0, 2)
    rs_add_diag_z(4)
    loop(4, 6, in_block)
    rs_add_first(1, 'y')
    rs_side(1, 'x', 2)
    rs_add_side(3, 1)
    rs_side(1, 'x', 3)
    rs_z(3, 1)
    st_step(0)
    rs_side(0, 'y', 1)
    st_step(1)
    rs_add_core(1, 0)
    rs_add_diag_z(1)
    rs_z(4, 1)
    rs_side(1, 'x', 1)
    rs_diag(4)
    rs_diag(1)
    rs_add_diag(3)
    rs_side(4, 'y', 0)
    st_step(2)
    rs_add_side(3, 3)
    ig_start(1)
    rs_add_side(0, 1)
    rs_add_diag_z(0)
    st_step(3)
    rs_add_side(1, 2)
    rs_z(3, 3)
    rs_z(1, 2)
    rs_side(0, 'y', 0)
    rs_side(1, 'y', 1)
    rs_add_diag(4)
    ig_start(2)
    rs_diag(0)
    rs_side(3, 'x', 0)
    rs_add_diag(1)
    rs_side(1, 'y', 3)
    rs_side(0, 'y', 3)
    rs_side(2, 'y', 0)
    rs_side(4, 'x', 0)
    st_step(4)
    rs_add_side(1, 3)
    rs_z(0, 1)
    ig_start(0)
    rs_add_side(0, 3)
    rs_side(1, 'x', 0)
    rs_add_side(1, 1)
    rs_side(0, 'y', 2)
    rs_z(1, 3)
    rs_z(0, 3)
    rs_final(2)
    rs_add_diag(0)
    rs_side(0, 'x', 0)
    rs_final(3)
    rs_final(4)
    rs_side(1, 'y', 0)
    rs_add_side(0, 2)
    rs_z(1, 1)
    rs_z(0, 2)
    rs_final(1)
    rs_final(0)
    finish()


def fits_fused(mesh):
    return mesh.shape["dp"] == 8 and mesh.shape["mp"] == 4


def renew_kernel(count, grads, bo, ig, stats, *rest):
    ins, (bo_new, ig_new, rms), news = rest[:15], rest[15:18], rest[18:]

    def rows(t, carry):
        for b in range(bo.shape[1]):
            bo_new[t, b] = bo[t, b].astype(F32)
            ig_new[t, b] = ig[t, b].astype(F32)
        return carry

    lax.fori_loop(0, bo.shape[0], rows, 0)
    size = jnp.sqrt(jnp.sum(stats[...], axis=1, keepdims=True) / count)
    for n in range(3):
        rms[n] = size[4 + n, 0]

    def step(n, at, gradient, rate):
        weight, momentum, average = (ref[at] for ref in ins[3 * n:3 * n + 3])
        for ref, value in zip(news[4 * n:4 * n + 4], renew_weight(weight, momentum, average, gradient, rate)):
            ref[at] = value

    whole = slice(None)
    for t in range(3):
        step(0, (t, whole, pl.ds(0, 128)), grads[0, :, 128 * t:128 * t + 128], MATRIX_RATE)
        step(0, (t, whole, pl.ds(128, 64)), grads[0, :, 384 + 64 * t:448 + 64 * t], MATRIX_RATE)
    step(1, (pl.ds(0, 128), whole), grads[0, :, 640:768].T, OUTPUT_RATE)
    step(1, (pl.ds(128, 64), whole), grads[0, :, 512:640].T[64:], OUTPUT_RATE)
    step(2, (whole, whole), grads[1], MATRIX_RATE)
    step(3, (whole, whole), grads[2], MATRIX_RATE)
    step(4, (whole, whole), stats[0:4], NORM_RATE)


def local_fused(
    tokens,
    visible_mask,
    cotangent,
    qkv_weight,
    qkv_momentum,
    qkv_average,
    out_weight,
    out_momentum,
    out_average,
    up_weight,
    up_momentum,
    up_average,
    down_weight,
    down_momentum,
    down_average,
    norm_params,
    norm_momentum,
    norm_average,
):
    data_size = lax.axis_size("dp")
    model_size = lax.axis_size("mp")
    slots, patches, width = tokens.shape
    quarter = cotangent.shape[1]
    sizes = (model_size // 2, 2, data_size // 2, 2)
    X, C, Z, Y = sizes
    blocks = slots // (4 * model_size)
    group = blocks * 32
    bufs = [pltpu.VMEM(shape, BF) for k in range(len(CHUNKS)) for _, shape in rs_buffers(k)]
    n_chunk = len(CHUNKS)
    rows = blocks * 128
    vmem = pltpu.VMEM
    dma = pltpu.SemaphoreType.DMA
    scratch = [
        vmem((3, X, C, Z, Y, 96, WIDE), BF),
        vmem((1, X, C, Z, Y, 96, WIDE), BF),
        vmem((3, X, 1, Z, Y, 96, WIDE), BF),
        *bufs,
        vmem((24 * patches, WIDE), BF),
        vmem((patches, slots), BF),
        vmem((rows, 128), F32),
        vmem((128, 128), F32),
        vmem((rows, WIDE), BF),
        vmem((rows, WIDE), BF),
        vmem((4, rows, WIDE), BF),
        vmem((4, rows, 256), BF),
        vmem((rows, WIDE), F32),
        vmem((blocks, 128, WIDE), BF),
        vmem((WIDE, rows), BF),
        vmem((WIDE, rows), BF),
        vmem((blocks, 128, WIDE), BF),
        vmem((WIDE, rows), BF),
        vmem((rows, 512), BF),
        vmem((rows, 512), BF),
        vmem((rows, WIDE), F32),
        vmem((rows, WIDE), F32),
        vmem((4, 8, WIDE), F32),
        vmem((6, 8, WIDE), F32),
        vmem((patches, slots), jnp.int32),
        vmem(qkv_weight.shape, F32),
        vmem(out_weight.shape, F32),
        vmem(norm_params.shape, F32),
        vmem((3, 96, WIDE), F32),
        dma((10,)),
        dma((n_chunk,)),
        dma((len(AG_CHUNKS), 21)),
        dma((len(AG_CHUNKS), 21)),
        dma((n_chunk, 21)),
        dma((n_chunk, 21)),
        dma((3, 3, 3)),
        dma((3, 3, 3)),
        dma((6,)),
        dma((6,)),
    ]
    in_vmem = pl.BlockSpec(memory_space=pltpu.VMEM)
    anywhere = pl.BlockSpec(memory_space=pl.ANY)
    grads, bo, ig, stats = pl.pallas_call(
        functools.partial(layer_kernel, sizes),
        out_shape=(
            jax.ShapeDtypeStruct((3, 96, WIDE), F32),
            jax.ShapeDtypeStruct((model_size, blocks, 32, WIDE), BF),
            jax.ShapeDtypeStruct((model_size, blocks, 32, WIDE), BF),
            jax.ShapeDtypeStruct((8, WIDE), F32),
        ),
        in_specs=[anywhere] * 8,
        out_specs=(anywhere, anywhere, anywhere, in_vmem),
        scratch_shapes=scratch,
        compiler_params=pltpu.CompilerParams(
            collective_id=0, has_side_effects=True, vmem_limit_bytes=VMEM_BYTES
        ),
        name="layer",
    )(
        tokens.reshape(slots * patches, width),
        visible_mask.T,
        cotangent.reshape(model_size, blocks, 32, width),
        qkv_weight,
        out_weight,
        up_weight,
        down_weight.T,
        norm_params,
    )
    visible_count = quarter * model_size
    triples = (
        (qkv_weight, qkv_momentum, qkv_average),
        (out_weight, out_momentum, out_average),
        (up_weight, up_momentum, up_average),
        (down_weight.T, down_momentum.T, down_average.T),
        (norm_params, norm_momentum, norm_average),
    )
    shares = jax.ShapeDtypeStruct((model_size, blocks, 32, width), F32)
    news = []
    for weight, _, _ in triples:
        news += [jax.ShapeDtypeStruct(weight.shape, F32)] * 3 + [jax.ShapeDtypeStruct(weight.shape, BF)]
    block_out, input_grad, rms, *new = pl.pallas_call(
        functools.partial(renew_kernel, visible_count * data_size * FLD_DEV * width),
        out_shape=(shares, shares, jax.ShapeDtypeStruct((3,), F32), *news),
        in_specs=[in_vmem] * (4 + 3 * len(triples)),
        out_specs=(in_vmem, in_vmem, pl.BlockSpec(memory_space=pltpu.SMEM)) + (in_vmem,) * len(news),
        compiler_params=pltpu.CompilerParams(vmem_limit_bytes=VMEM_BYTES),
        name="renew",
    )(grads, bo, ig, stats, *(array for triple in triples for array in triple))
    block_out = block_out.reshape(slots, quarter, width)
    input_grad = input_grad.reshape(slots, quarter, width)
    new[12:16] = [array.T for array in new[12:16]]
    return (block_out, input_grad, rms, *new)


def local_general(
    tokens,
    visible_mask,
    cotangent,
    qkv_weight,
    qkv_momentum,
    qkv_average,
    out_weight,
    out_momentum,
    out_average,
    up_weight,
    up_momentum,
    up_average,
    down_weight,
    down_momentum,
    down_average,
    norm_params,
    norm_momentum,
    norm_average,
):
    data_size = lax.axis_size("dp")
    model_size = lax.axis_size("mp")
    data_rank = lax.axis_index("dp")
    model_rank = lax.axis_index("mp")
    slot_count, patch_count, feature_count = tokens.shape
    quarter = cotangent.shape[1]
    visible_count = quarter * model_size
    capacity = (slot_count + data_size - 1) // data_size
    owned_fields = FLD_DEV
    pad_total = data_size * capacity
    per_field = jnp.sum(visible_mask, axis=1)
    field_total = jnp.sum(per_field) // visible_count
    all_fields = lax.all_gather(field_total.reshape(1), "dp", axis=0, tiled=True)
    firsts = jnp.cumsum(all_fields) - all_fields
    my_first = firsts[data_rank]
    patch_ids = jnp.arange(patch_count, dtype=jnp.int32)
    sort_keys = (1 - visible_mask) * patch_count + patch_ids[None, :]
    ranked = jnp.argsort(sort_keys, axis=1)
    my_order = lax.dynamic_slice_in_dim(ranked, model_rank * quarter, quarter, 1)
    visible = jnp.take_along_axis(tokens, my_order[:, :, None], axis=1)
    owner_ids = jnp.arange(data_size, dtype=jnp.int32)[:, None]
    slot_ids = jnp.arange(capacity, dtype=jnp.int32)[None, :]
    source_field = slot_ids * data_size + (owner_ids - my_first) % data_size
    send_live = (source_field < field_total).reshape(-1)[:, None, None]
    source_pick = jnp.minimum(source_field, slot_count - 1).reshape(-1)
    sent_rows = jnp.where(send_live, visible[source_pick], jnp.zeros((), jnp.bfloat16))
    sent_grads = jnp.where(send_live, cotangent[source_pick], jnp.zeros((), jnp.bfloat16))
    got_rows, got_grads = (
        lax.all_to_all(sent_rows, "dp", split_axis=0, concat_axis=0, tiled=True),
        lax.all_to_all(sent_grads, "dp", split_axis=0, concat_axis=0, tiled=True),
    )
    arrive = slot_ids * data_size + (data_rank - firsts[:, None]) % data_size
    flat_live = (arrive < all_fields[:, None]).reshape(-1)
    order_keys = jnp.where(flat_live, 0, pad_total) + jnp.arange(pad_total, dtype=jnp.int32)
    chosen = jnp.argsort(order_keys)[:owned_fields]
    share_rows = owned_fields * quarter
    mine_rows = got_rows[chosen].reshape(share_rows, feature_count)
    mine_grads = got_grads[chosen].reshape(share_rows, feature_count)
    w_qkv, w_out, w_up, w_down = (
        lax.all_gather(qkv_weight.astype(jnp.bfloat16), "dp", axis=1, tiled=True),
        lax.all_gather(out_weight.astype(jnp.bfloat16), "dp", axis=1, tiled=True),
        lax.all_gather(up_weight.astype(jnp.bfloat16), "dp", axis=0, tiled=True),
        lax.all_gather(down_weight.astype(jnp.bfloat16), "dp", axis=1, tiled=True),
    )
    norm_low = lax.optimization_barrier(norm_params.astype(jnp.bfloat16)).astype(jnp.float32)
    total_rows = share_rows * model_size
    local_width = w_qkv.shape[2]
    head_local = local_width // HDIM
    score_scale = HDIM ** (-0.5)
    x_share = mine_rows.astype(jnp.float32)
    normed_share, norm_in_back = jax.vjp(layer_norm, x_share, norm_low[0], norm_low[1])
    normed_all = lax.all_gather(normed_share.astype(jnp.bfloat16), "mp", axis=0, tiled=True)
    qkv_rows = jnp.einsum(
        "rd,tde->tre", normed_all, w_qkv, preferred_element_type=jnp.float32
    ).astype(jnp.bfloat16)
    qkv_six = qkv_rows.reshape(3, model_size, owned_fields, quarter, head_local, HDIM)
    queries = qkv_six[0]
    key_rows = qkv_six[1]
    values = qkv_six[2]
    scores = (
        jnp.einsum("afbhe,cfdhe->fhabcd", queries, key_rows, preferred_element_type=jnp.float32)
        * score_scale
    )
    scores = scores.reshape(owned_fields, head_local, visible_count, visible_count)
    attention = jax.nn.softmax(scores, axis=-1)
    att_six = attention.astype(jnp.bfloat16).reshape(
        owned_fields, head_local, model_size, quarter, model_size, quarter
    )
    context = jnp.einsum("fhabcd,cfdhe->afbhe", att_six, values, preferred_element_type=jnp.float32)
    context = context.astype(jnp.bfloat16).reshape(total_rows, local_width)
    attn_share = lax.psum_scatter(
        jnp.dot(context, w_out, preferred_element_type=jnp.float32).astype(jnp.bfloat16),
        "mp",
        scatter_dimension=0,
        tiled=True,
    ).astype(jnp.float32)
    mid_share = x_share + attn_share
    normed_mid, norm_mid_back = jax.vjp(layer_norm, mid_share, norm_low[2], norm_low[3])
    mid_all, grad_all = (
        lax.all_gather(normed_mid.astype(jnp.bfloat16), "mp", axis=0, tiled=True),
        lax.all_gather(mine_grads, "mp", axis=0, tiled=True),
    )
    pre_act = jnp.dot(mid_all, w_up, preferred_element_type=jnp.float32)
    gelu_float, gelu_back = jax.vjp(gelu_exact, pre_act)
    gelu_out = gelu_float.astype(jnp.bfloat16)
    mlp_share = lax.psum_scatter(
        jnp.dot(gelu_out, w_down, preferred_element_type=jnp.float32).astype(jnp.bfloat16),
        "mp",
        scatter_dimension=0,
        tiled=True,
    ).astype(jnp.float32)
    out_share = mid_share + mlp_share
    squares = jnp.stack(
        [
            jnp.sum(attn_share * attn_share),
            jnp.sum(mlp_share * mlp_share),
            jnp.sum(out_share * out_share),
        ]
    )
    grad_down = jnp.einsum("rf,rd->fd", gelu_out, grad_all, preferred_element_type=jnp.float32)
    d_act = jnp.einsum("rd,fd->rf", grad_all, w_down, preferred_element_type=jnp.float32)
    d_pre = gelu_back(d_act)[0].astype(jnp.bfloat16)
    grad_up = jnp.einsum("rd,rf->df", mid_all, d_pre, preferred_element_type=jnp.float32)
    d_mid_norm = lax.psum_scatter(
        jnp.einsum("rf,df->rd", d_pre, w_up, preferred_element_type=jnp.float32).astype(
            jnp.bfloat16
        ),
        "mp",
        scatter_dimension=0,
        tiled=True,
    ).astype(jnp.float32)
    d_mid_part, grad_gain_mid, grad_shift_mid = norm_mid_back(d_mid_norm)
    d_middle = mine_grads.astype(jnp.float32) + d_mid_part
    d_att_all = lax.all_gather(d_middle.astype(jnp.bfloat16), "mp", axis=0, tiled=True)
    grad_out = jnp.einsum("rc,rd->cd", context, d_att_all, preferred_element_type=jnp.float32)
    d_context = jnp.einsum(
        "rd,cd->rc", d_att_all, w_out, preferred_element_type=jnp.float32
    ).astype(jnp.bfloat16)
    d_ctx_six = d_context.reshape(model_size, owned_fields, quarter, head_local, HDIM)
    d_probs = jnp.einsum(
        "afbhe,cfdhe->fhabcd", d_ctx_six, values, preferred_element_type=jnp.float32
    )
    d_probs = d_probs.reshape(owned_fields, head_local, visible_count, visible_count)
    d_values = jnp.einsum(
        "fhabcd,afbhe->cfdhe", att_six, d_ctx_six, preferred_element_type=jnp.float32
    )
    d_scores = (
        attention * (d_probs - jnp.sum(d_probs * attention, axis=-1, keepdims=True))
    ).astype(jnp.bfloat16)
    d_six = d_scores.reshape(owned_fields, head_local, model_size, quarter, model_size, quarter)
    d_queries = (
        jnp.einsum("fhabcd,cfdhe->afbhe", d_six, key_rows, preferred_element_type=jnp.float32)
        * score_scale
    )
    d_keys = (
        jnp.einsum("fhabcd,afbhe->cfdhe", d_six, queries, preferred_element_type=jnp.float32)
        * score_scale
    )
    d_qkv = (
        jnp.stack([d_queries, d_keys, d_values])
        .astype(jnp.bfloat16)
        .reshape(3, total_rows, local_width)
    )
    grad_qkv = jnp.einsum("rd,tre->tde", normed_all, d_qkv, preferred_element_type=jnp.float32)
    d_in_norm = lax.psum_scatter(
        jnp.einsum("tre,tde->rd", d_qkv, w_qkv, preferred_element_type=jnp.float32).astype(
            jnp.bfloat16
        ),
        "mp",
        scatter_dimension=0,
        tiled=True,
    ).astype(jnp.float32)
    d_in_part, grad_gain_in, grad_shift_in = norm_in_back(d_in_norm)
    d_input = d_middle + d_in_part
    gradients = (grad_qkv, grad_out, grad_up, grad_down)
    summed = lax.psum((gradients[0], gradients[1], gradients[2], gradients[3]), "dp")
    qkv_grad = lax.dynamic_slice_in_dim(
        summed[0], data_rank * qkv_weight.shape[1], qkv_weight.shape[1], 1
    )
    out_grad = lax.dynamic_slice_in_dim(
        summed[1], data_rank * out_weight.shape[1], out_weight.shape[1], 1
    )
    up_grad = lax.dynamic_slice_in_dim(
        summed[2], data_rank * up_weight.shape[0], up_weight.shape[0], 0
    )
    down_grad = lax.dynamic_slice_in_dim(
        summed[3], data_rank * down_weight.shape[1], down_weight.shape[1], 1
    )

    def spread_back(share_block):
        padded = jnp.zeros((pad_total, quarter, feature_count), jnp.float32)
        return padded.at[chosen].set(share_block.reshape(owned_fields, quarter, feature_count))

    back_out, back_grad = (
        lax.all_to_all(
            spread_back(out_share).astype(jnp.bfloat16),
            "dp",
            split_axis=0,
            concat_axis=0,
            tiled=True,
        ).astype(jnp.float32),
        lax.all_to_all(
            spread_back(d_input).astype(jnp.bfloat16), "dp", split_axis=0, concat_axis=0, tiled=True
        ).astype(jnp.float32),
    )
    field_ids = jnp.arange(slot_count, dtype=jnp.int32)
    home_slot = (my_first + field_ids) % data_size * capacity + field_ids // data_size
    field_live = (field_ids < field_total)[:, None, None]
    block_out = jnp.where(field_live, back_out[home_slot], 0.0)
    input_grad = jnp.where(field_live, back_grad[home_slot], 0.0)
    norm_grad = jnp.stack([grad_gain_in, grad_shift_in, grad_gain_mid, grad_shift_mid])
    totals, norm_grad = lax.psum((squares, norm_grad), ("dp", "mp"))
    branch_rms = jnp.sqrt(totals / (visible_count * data_size * FLD_DEV * feature_count))
    qkv_new = renew_weight(qkv_weight, qkv_momentum, qkv_average, qkv_grad, MATRIX_RATE)
    out_new = renew_weight(out_weight, out_momentum, out_average, out_grad, OUTPUT_RATE)
    up_new = renew_weight(up_weight, up_momentum, up_average, up_grad, MATRIX_RATE)
    down_new = renew_weight(down_weight, down_momentum, down_average, down_grad, MATRIX_RATE)
    norm_new = renew_weight(norm_params, norm_momentum, norm_average, norm_grad, NORM_RATE)
    return (
        block_out,
        input_grad,
        branch_rms,
        qkv_new[0],
        qkv_new[1],
        qkv_new[2],
        qkv_new[3],
        out_new[0],
        out_new[1],
        out_new[2],
        out_new[3],
        up_new[0],
        up_new[1],
        up_new[2],
        up_new[3],
        down_new[0],
        down_new[1],
        down_new[2],
        down_new[3],
        norm_new[0],
        norm_new[1],
        norm_new[2],
        norm_new[3],
    )


def solution(mesh):
    in_specs = (
        P("dp", None, None),
        P("dp", None),
        P("dp", "mp", None),
        P(None, "dp", "mp"),
        P(None, "dp", "mp"),
        P(None, "dp", "mp"),
        P("mp", "dp"),
        P("mp", "dp"),
        P("mp", "dp"),
        P("dp", "mp"),
        P("dp", "mp"),
        P("dp", "mp"),
        P("mp", "dp"),
        P("mp", "dp"),
        P("mp", "dp"),
        P(),
        P(),
        P(),
    )
    out_specs = (
        P("dp", "mp", None),
        P("dp", "mp", None),
        P(),
        P(None, "dp", "mp"),
        P(None, "dp", "mp"),
        P(None, "dp", "mp"),
        P(None, "dp", "mp"),
        P("mp", "dp"),
        P("mp", "dp"),
        P("mp", "dp"),
        P("mp", "dp"),
        P("dp", "mp"),
        P("dp", "mp"),
        P("dp", "mp"),
        P("dp", "mp"),
        P("mp", "dp"),
        P("mp", "dp"),
        P("mp", "dp"),
        P("mp", "dp"),
        P(),
        P(),
        P(),
        P(),
    )
    local = local_fused if fits_fused(mesh) else local_general
    return jax.shard_map(local, mesh=mesh, in_specs=in_specs, out_specs=out_specs, check_vma=False)
```

```python
import functools

import jax
import jax.numpy as jnp
from jax import lax
from jax.experimental import pallas as pl
from jax.experimental.pallas import tpu as pltpu
from jax.sharding import PartitionSpec as P

HDIM = 64
FLD_DEV = 64


NORM_EPS = 1e-06
MOMENTUM_RATE = 0.9
MATRIX_RATE = 4e-05
OUTPUT_RATE = 0.00025
NORM_RATE = 0.0003
AVERAGE_DECAY = 0.7


def layer_norm(row_values, norm_gain, norm_shift):
    center = row_values - jnp.mean(row_values, axis=-1, keepdims=True)
    spread = jnp.mean(center * center, axis=-1, keepdims=True)
    return center * lax.rsqrt(spread + NORM_EPS) * norm_gain + norm_shift


def gelu_exact(values):
    return jax.nn.gelu(values, approximate=False)


def renew_weight(weight, momentum, average, gradient, step_rate):
    moment = MOMENTUM_RATE * momentum + gradient
    updated = weight - step_rate * (gradient + MOMENTUM_RATE * moment)
    smooth = AVERAGE_DECAY * average + (1.0 - AVERAGE_DECAY) * updated
    return (moment, updated, smooth, updated.astype(jnp.bfloat16))


BF = jnp.bfloat16
F32 = jnp.float32
MESH_ID = pl.DeviceIdType.MESH
WIDE = 768
VMEM_BYTES = 63 * 1024 * 1024
AG_CHUNKS = ((0, 1, 0, 384), (0, 1, 384, 384), (1, 2, 0, 256), (1, 2, 256, 256), (1, 2, 512, 256))
CHUNKS = ((0, 1, 0, 384), (0, 1, 384, 384), (1, 2, 0, 256), (1, 2, 256, 256), (1, 2, 512, 256))
AG_ROWS = ((64, 32, 0), (64, 32, 0), (48, 48, 0), (48, 48, 0), (48, 48, 0))
RS_ROWS = ((48, 0, 48), (48, 0, 48), (48, 0, 48), (48, 0, 48), (48, 0, 48))


def dot_nn(a, b):
    return jnp.dot(a, b, preferred_element_type=F32)


def dot_nt(a, b):
    return lax.dot_general(a, b, (((1,), (1,)), ((), ())), preferred_element_type=F32)


def dot_tn(a, b):
    return lax.dot_general(a, b, (((0,), (0,)), ((), ())), preferred_element_type=F32)


def gelu_pair(v):
    size = jnp.abs(v)
    bell = jnp.exp(v * v * -0.5)
    t = 1.0 / (1.0 + (0.3275911 * 0.7071067811865476) * size)
    poly = t * (
        0.254829592
        + t * (-0.284496736 + t * (1.421413741 + t * (-1.453152027 + t * 1.061405429)))
    )
    tail = 0.5 * poly * bell
    phi = jnp.where(v < 0.0, tail, 1.0 - tail)
    return v * phi, phi + v * bell * 0.3989422804014327


def lnorm(v, gain, shift):
    center = v - jnp.mean(v, axis=-1, keepdims=True)
    rs = lax.rsqrt(jnp.mean(center * center, axis=-1, keepdims=True) + NORM_EPS)
    return center * rs * gain + shift


def lnorm_back(v, e, gain):
    center = v - jnp.mean(v, axis=-1, keepdims=True)
    rs = lax.rsqrt(jnp.mean(center * center, axis=-1, keepdims=True) + NORM_EPS)
    xhat = center * rs
    eg = e * gain
    dv = rs * (
        eg - jnp.mean(eg, axis=-1, keepdims=True) - xhat * jnp.mean(eg * xhat, axis=-1, keepdims=True)
    )
    return dv, e * xhat


def rs_buffers(k):
    nm, nc = CHUNKS[k][1], CHUNKS[k][3]
    r1, r2, r3 = RS_ROWS[k]
    made = [(name, (n, nm, 1, 1, 1, 1, 96, nc)) for name, n in (("x", 4), ("y", 4), ("z", 3))]
    if r1:
        made.append(("3y", (nm, 1, 1, 4, 1, r1, nc)))
    if r2:
        made.append(("3x", (nm, 1, 1, 4, 1, r2, nc)))
    if r3:
        made += [("dz", (3, nm, 1, 1, 1, 1, r3, nc)), ("d", (nm, 1, 1, 1, 1, r3, nc))]
    return made


def layer_kernel(
    sizes,
    tok_hbm,
    mask_hbm,
    cot_hbm,
    qkv_hbm,
    out_hbm,
    up_hbm,
    down_hbm,
    norm_hbm,
    gout_hbm,
    bo_out,
    ig_out,
    stats_ref,
    G,
    PA,
    RSC,
    *rest,
):
    names = [(k, name) for k in range(len(CHUNKS)) for name, _ in rs_buffers(k)]
    n_bufs = len(names)
    RSB = dict(zip(names, rest[:n_bufs]))
    (
        tok_s, key_s, live_s, band_s, x_s, nin_s, qkv_s, ctx_s, mid_s, nm_s, nmT_s, ninT_s,
        cot_s, dmT_s, g_s, d_s, mlp_s, dmn_s, st_send, st_recv,
        mask_ref, qkv_ref, out_ref, norm_ref, gout_ref, loc_sem, g_sem, ag_send, ag_recv, rs_send, rs_recv, ex_send, ex_recv, st_ss, st_rs,
    ) = rest[n_bufs:]
    X, C, Z, Y = sizes
    dp = lax.axis_index("dp")
    mp = lax.axis_index("mp")
    me = {"z": lax.div(dp, Y), "y": lax.rem(dp, Y), "x": lax.div(mp, C), "c": lax.rem(mp, C)}
    size_of = {"x": X, "c": C, "z": Z, "y": Y}

    def device(**over):
        at = dict(me, **over)
        return (at["z"] * Y + at["y"], at["x"] * C + at["c"])

    def shifted(axis, delta):
        return lax.rem(me[axis] + delta, size_of[axis])

    def place(whole, **over):
        return tuple(slice(None) if a in whole else pl.ds(over.get(a, me[a]), 1) for a in "xczy")

    def remote(src, dst, ss, rs, dev):
        return pltpu.make_async_remote_copy(
            src_ref=src, dst_ref=dst, send_sem=ss, recv_sem=rs, device_id=dev, device_id_type=MESH_ID
        )

    far = {a: size_of[a] - 1 - me[a] for a in "xyc"}
    waited = set()

    def wait_recv(kind, k, *names):
        for name in names:
            if (kind, k, name) not in waited:
                waited.add((kind, k, name))
                (ag_copy if kind == "ag" else rs_copy)(k, name).wait_recv()

    def quadrant(q):
        return (far["x"] if q % 2 else me["x"]), (far["y"] if q // 2 else me["y"])

    def bands(table, k):
        r1, r2, r3 = table[k]
        return {"y": pl.ds(0, r1), "x": pl.ds(r1, r2), "z": pl.ds(r1 + r2, r3)}

    def part(buf, b0, chunk, x, c, z, y, rows):
        _, nm, c0, nc = chunk
        at_z = slice(None) if z is None else pl.ds(z, 1)
        return buf.at[pl.ds(b0, nm), pl.ds(x, 1), pl.ds(c, 1), at_z, pl.ds(y, 1), rows, pl.ds(c0, nc)]

    ALL = slice(0, 96)
    AG_NAMES = ("z1", "z2", "z3", "x0", "y0", "x1", "x2", "x3", "y1", "y2", "y3",
                "d", "dz1", "dz2", "dz3", "3y", "3x", "c0", "c1", "c2", "c3")
    RS_NAMES = ("c0", "c1", "c2", "c3", "3y", "3x", "dz1", "dz2", "dz3", "d",
                "x0", "x1", "x2", "x3", "y0", "y1", "y2", "y3", "z1", "z2", "z3")

    def ag_copy(k, name):
        rows = bands(AG_ROWS, k)
        x, y, z, c = me["x"], me["y"], me["z"], me["c"]
        band, to = ALL, {}
        if name[0] == "c":
            (x, y), z, to = quadrant(int(name[1])), None, {"c": far["c"]}
        elif name == "3y":
            x, z, band, to = far["x"], None, rows["y"], {"y": far["y"]}
        elif name == "3x":
            y, z, band, to = far["y"], None, rows["x"], {"x": far["x"]}
        elif name == "d":
            x, band, to = far["x"], rows["z"], {"y": far["y"]}
        elif name[:2] == "dz":
            x, y, band, to = far["x"], far["y"], rows["z"], {"z": shifted("z", int(name[2]))}
        elif name[0] == "z":
            to = {"z": shifted("z", int(name[1]))}
        else:
            z, to = shifted("z", Z - int(name[1])), {name[0]: far[name[0]]}
        ref = part(G, AG_CHUNKS[k][0], AG_CHUNKS[k], x, c, z, y, band)
        at = AG_NAMES.index(name)
        return remote(ref, ref, ag_send.at[k, at], ag_recv.at[k, at], device(**to))

    def ag_names(k):
        r1, r2, r3 = AG_ROWS[k]
        none = (() if r1 else ("3y",)) + (() if r2 else ("3x",)) + (() if r3 else ("d", "dz1", "dz2", "dz3"))
        return [n for n in AG_NAMES if n not in none]

    def ag_start(k, *names):
        for name in names:
            ag_copy(k, name).start()

    def ag_z(k):
        ag_start(k, "z1", "z2", "z3")

    def ag_own(k, axis):
        ag_start(k, axis + "0")

    def ag_pass(k, axis, d):
        wait_recv("ag", k, f"z{d}")
        ag_start(k, f"{axis}{d}")

    def ag_diag(k):
        wait_recv("ag", k, "x0")
        ag_start(k, "d")

    def ag_diag_z(k):
        wait_recv("ag", k, "d")
        ag_start(k, "dz1", "dz2", "dz3")

    def ag_last(k, axis):
        side = "x" if axis == "y" else "y"
        wait_recv("ag", k, *(f"{side}{d}" for d in range(4)))
        ag_start(k, "3" + axis)

    def ag_core(k, q):
        if q == 3:
            wait_recv("ag", k, *(n for n in ag_names(k) if n[0] in "3d"))
        else:
            wait_recv("ag", k, *(f"{'zxy'[q]}{d}" for d in range(0 if q else 1, 4)))
        ag_start(k, f"c{q}")

    def ag_ready(k):
        wait_recv("ag", k, "c0", "c1", "c2", "c3")

    def ag_sent(k):
        for name in ag_names(k):
            ag_copy(k, name).wait_send()

    def grads_of(k):
        return (PA, 0) if CHUNKS[k][0] == 0 else (G, CHUNKS[k][0])

    def rs_copy(k, name):
        buf, b0 = grads_of(k)
        m0, nm, c0, nc = CHUNKS[k]
        rows = bands(RS_ROWS, k)
        x, y, z, c = me["x"], me["y"], me["z"], me["c"]
        band = ALL
        if name[0] == "c":
            (x, y), z, c = quadrant(int(name[1])), None, far["c"]
            to, dst = {"c": far["c"]}, part(RSC, m0, CHUNKS[k], x, 0, None, y, ALL)
        else:
            d = int(name[-1]) if name[-1] in "0123" else 0
            if name == "3y" or name == "3x":
                x, y, z, band, to = far["x"], far["y"], None, rows[name[1]], {name[1]: far[name[1]]}
                dst = RSB[k, name]
            elif name == "d":
                x, y, band, to, dst = far["x"], far["y"], rows["z"], {"y": far["y"]}, RSB[k, "d"]
            elif name[:2] == "dz":
                z = shifted("z", d)
                x, y, band, to, dst = far["x"], far["y"], rows["z"], {"z": z}, RSB[k, "dz"].at[d - 1]
            elif name[0] == "z":
                z = shifted("z", d)
                to, dst = {"z": z}, RSB[k, "z"].at[d - 1]
            else:
                z = shifted("z", d)
                to, dst = {name[0]: far[name[0]]}, RSB[k, name[0]].at[d]
                if name[0] == "x":
                    x = far["x"]
                else:
                    y = far["y"]
        at = RS_NAMES.index(name)
        return remote(part(buf, b0, CHUNKS[k], x, c, z, y, band), dst, rs_send.at[k, at], rs_recv.at[k, at], device(**to))

    def rs_names(k):
        r1, r2, r3 = RS_ROWS[k]
        none = (() if r1 else ("3y",)) + (() if r2 else ("3x",)) + (() if r3 else ("d", "dz1", "dz2", "dz3"))
        return [n for n in RS_NAMES if n not in none]

    def rs_start(k, *names):
        for name in names:
            rs_copy(k, name).start()

    def rs_core(k, q):
        rs_start(k, f"c{q}")

    def rs_first(k, axis):
        rs_start(k, "3" + axis)

    def rs_diag_z(k):
        rs_start(k, "dz1", "dz2", "dz3")

    def rs_diag(k):
        rs_start(k, "d")

    def rs_side(k, axis, d):
        rs_start(k, f"{axis}{d}")

    def rs_z(k, d):
        rs_start(k, f"z{d}")

    def rs_sum(k, x, y, zs, rows, terms):
        buf, b0 = grads_of(k)
        _, nm, c0, nc = CHUNKS[k]

        def one(t, carry):
            mat, zi = lax.div(t, zs[1]), lax.rem(t, zs[1])
            at = (b0 + mat, x, me["c"], zs[0] + zi, y, rows, pl.ds(c0, nc))
            more = terms(mat, zi)
            if len(more) == 1:
                buf[at] = buf[at] + more[0]
            else:
                total = buf[at].astype(F32)
                for term in more:
                    total = total + term.astype(F32)
                buf[at] = total.astype(BF)
            return carry

        lax.fori_loop(0, nm * zs[1], one, 0)

    def rs_add_core(k, q):
        wait_recv("rs", k, f"c{q}")
        x, y = quadrant(q)
        m0, _, c0, nc = CHUNKS[k]
        rs_sum(k, x, y, (0, Z), ALL, lambda mat, zi: [RSC[m0 + mat, x, 0, zi, y, :, pl.ds(c0, nc)]])

    def rs_add_first(k, axis):
        wait_recv("rs", k, "3" + axis)
        x, y = (far["x"], me["y"]) if axis == "y" else (me["x"], far["y"])
        came = RSB[k, "3" + axis]
        rs_sum(k, x, y, (0, Z), bands(RS_ROWS, k)[axis], lambda mat, zi: [came[mat, 0, 0, zi, 0]])

    def rs_add_diag_z(k):
        wait_recv("rs", k, "dz1", "dz2", "dz3")
        came = RSB[k, "dz"]
        rs_sum(k, far["x"], far["y"], (me["z"], 1), bands(RS_ROWS, k)["z"],
               lambda mat, zi: [came[n, mat, 0, 0, 0, 0] for n in range(3)])

    def rs_add_diag(k):
        wait_recv("rs", k, "d")
        came = RSB[k, "d"]
        rs_sum(k, far["x"], me["y"], (me["z"], 1), bands(RS_ROWS, k)["z"],
               lambda mat, zi: [came[mat, 0, 0, 0, 0]])

    def rs_add_side(k, d):
        wait_recv("rs", k, f"x{d}", f"y{d}")
        rs_sum(k, me["x"], me["y"], (shifted("z", d), 1), ALL,
               lambda mat, zi: [RSB[k, a][d, mat, 0, 0, 0, 0] for a in "xy"])

    def rs_final(k):
        wait_recv("rs", k, "x0", "y0", "z1", "z2", "z3")
        buf, b0 = grads_of(k)
        m0, nm, c0, nc = CHUNKS[k]
        cols = pl.ds(c0, nc)
        for mat in range(nm):
            total = buf[b0 + mat, me["x"], me["c"], me["z"], me["y"], :, cols].astype(F32)
            for a in "xy":
                total = total + RSB[k, a][0, mat, 0, 0, 0, 0].astype(F32)
            for n in range(3):
                total = total + RSB[k, "z"][n, mat, 0, 0, 0, 0].astype(F32)
            gout_ref[m0 + mat, :, cols] = total
        home(k).start()

    def home(k):
        m0, nm, c0, nc = CHUNKS[k]
        at = (pl.ds(m0, nm), slice(None), pl.ds(c0, nc))
        return pltpu.make_async_copy(gout_ref.at[at], gout_hbm.at[at], g_sem.at[k])

    def rs_sent(k):
        for name in rs_names(k):
            rs_copy(k, name).wait_send()

    mates = [(0, 1), (1, 0), (1, 1)]

    def mate(j):
        dx, dc = mates[j]
        x2, c2 = lax.rem(me["x"] + dx, X), lax.rem(me["c"] + dc, C)
        return device(x=x2, c=c2), x2 * C + c2

    slab = pl.ds(pl.multiple_of(mp * 32, 32), 32)

    def rows_of(index):
        return pl.ds(pl.multiple_of(index * 32, 32), 32)

    def exchange(which, j):
        two = pl.ds(2 * j, 2)
        made = []
        for n in range(3):
            dev, index = mate(n)
            if which == 0:
                src, dst = cot_hbm.at[index, two], cot_s.at[two, slab, :]
            else:
                src = (nm_s if which == 1 else cot_s).at[two, rows_of(index), :]
                dst = (bo_out if which == 1 else ig_out).at[mp, two]
            made.append(remote(src, dst, ex_send.at[which, j, n], ex_recv.at[which, j, n], dev))
        return made

    cot_own = pltpu.make_async_copy(cot_hbm.at[mp], cot_s.at[:, slab, :], loc_sem.at[0])
    tok_copy = pltpu.make_async_copy(
        tok_hbm.at[pl.ds(pl.multiple_of(mp * 1536, 1536), 1536)], tok_s, loc_sem.at[1]
    )
    bo_own = pltpu.make_async_copy(nm_s.at[:, slab, :], bo_out.at[mp], loc_sem.at[2])
    ig_own = pltpu.make_async_copy(cot_s.at[:, slab, :], ig_out.at[mp], loc_sem.at[3])

    st_axes = "cyxz"

    def st_copies(i):
        axis = st_axes[i]
        return [
            remote(
                st_send.at[i], st_recv.at[i + delta - 1], st_ss.at[i + delta - 1], st_rs.at[i + delta - 1],
                device(**{axis: shifted(axis, delta)}),
            )
            for delta in range(1, size_of[axis])
        ]

    def st_step(i):
        if i == 0:
            total = stats_ref[...]
        else:
            copies = st_copies(i - 1)
            for c in copies:
                c.wait_recv()
            total = st_send[i - 1]
            for n in range(len(copies)):
                total = total + st_recv[i - 1 + n]
        if i < 4:
            st_send[i] = total
            for c in st_copies(i):
                c.start()
        else:
            stats_ref[...] = total

    def low_norm(n):
        return norm_ref[n:n + 1, :].astype(BF).astype(F32)

    lane = lax.broadcasted_iota(jnp.int32, (1, 128), 1)
    lo = (lane < 64).astype(F32).astype(BF)
    hi = (lane >= 64).astype(F32).astype(BF)
    low_eighth = jnp.where(lane < 64, 0.125, 1.0)

    def weight(mat, m, c0, nc):
        m = jnp.int32(m)
        return G[mat, lax.div(m, C), lax.rem(m, C), :, :, :, pl.ds(c0, nc)].reshape(WIDE, nc)

    def put(buf, mat, m, c0, nc, value):
        m = jnp.int32(m)
        buf[mat, lax.div(m, C), lax.rem(m, C), :, :, :, pl.ds(c0, nc)] = value.reshape(Z, Y, 96, nc)

    def block(b):
        return pl.ds(pl.multiple_of(b * 128, 128), 128)

    def rows256(t):
        return pl.ds(pl.multiple_of(t * 256, 256), 256)

    def setup():
        loads[8].wait()
        loads[9].wait()
        col = lax.broadcasted_iota(jnp.int32, (64, 64), 1)
        row = lax.broadcasted_iota(jnp.int32, (64, 64), 0)
        marks = mask_ref[...].astype(F32)
        before = dot_nn(jnp.where(col < row, 1.0, 0.0).astype(BF), marks.astype(BF))
        key_s[...] = jnp.where(marks > 0.0, before, -1.0).astype(BF)
        ri = lax.broadcasted_iota(jnp.int32, (128, 128), 0) // 8 % 4
        ci = lax.broadcasted_iota(jnp.int32, (128, 128), 1) // 8 % 4
        band_s[...] = jnp.where(ri == ci, 0.0, -1e30)
        stats_ref[...] = jnp.zeros_like(stats_ref)
        mid_s[...] = jnp.zeros_like(mid_s)

    def take_block(b, carry):
        slot = lax.broadcasted_iota(jnp.int32, (key_s.shape[1], 128), 0)
        row = lax.broadcasted_iota(jnp.int32, (key_s.shape[1], 128), 1)
        owner = (mp * 6 + b) * 4 + row // 8 % 4
        rank = dot_nn(key_s[...], jnp.where(slot == owner, 1.0, 0.0).astype(BF))
        row = lax.broadcasted_iota(jnp.int32, (64, 128), 1)
        hit = jnp.where(rank == (row // 32 * 8 + row % 8).astype(F32), 1.0, 0.0)
        pick = jnp.concatenate([jnp.where(row // 8 % 4 == n, hit, 0.0) for n in range(4)], axis=0)
        live_s[block(b), :] = jnp.broadcast_to(jnp.sum(hit, axis=0, keepdims=True), (128, 128)).T
        x = dot_tn(pick.astype(BF), tok_s[pl.ds(pl.multiple_of(b * 256, 256), 256), :])
        x_s[block(b), :] = x.astype(BF)
        nin_s[block(b), :] = lnorm(x, low_norm(0), low_norm(1)).astype(BF)
        return carry

    def qkv_first(m, carry):
        w = weight(0, m, 0, 384)
        for t in range(3):
            rows = pl.ds(t * 256, 256)
            out = dot_nn(nin_s[rows, :], w)
            qkv_s[m, rows, 0:128] = (out[:, :128] * 0.125).astype(BF)
            qkv_s[m, rows, 128:384] = out[:, 128:].astype(BF)
        return carry

    def qkv_second(m, carry):
        w = weight(0, m, 384, 256)
        for t in range(3):
            rows = pl.ds(t * 256, 256)
            out = dot_nn(nin_s[rows, :], w)
            first = out[:, :128] * low_eighth
            qkv_s[m, rows, 384:512] = first.astype(BF)
            qkv_s[m, rows, 512:640] = pltpu.roll(first, 64, 1).astype(BF)
            qkv_s[m, rows, 640:768] = pltpu.roll(out[:, 128:], 64, 1).astype(BF)
        return carry

    def keep_p(i, h, p):
        rows = pl.ds(pl.multiple_of(i * 64, 64), 64)
        tok_s[rows, h * 128:(h + 1) * 128] = p[:64]
        tok_s[rows, 384 + h * 128:512 + h * 128] = p[64:]

    def kept_p(i, h):
        rows = pl.ds(pl.multiple_of(i * 64, 64), 64)
        return jnp.concatenate(
            [tok_s[rows, h * 128:(h + 1) * 128], tok_s[rows, 384 + h * 128:512 + h * 128]], axis=0
        )

    def softmax(s):
        e = jnp.exp(s - jnp.max(s, axis=0, keepdims=True))
        return (e * (1.0 / jnp.sum(e, axis=0, keepdims=True))).astype(BF)

    def attend_first(j, carry):
        at = [(lax.div(j, 2), lax.rem(j, 2) * 3 + u) for u in range(3)]
        qs, ks, vs = ([qkv_s[m, block(b), n * 128:(n + 1) * 128] for m, b in at] for n in range(3))
        scores = [dot_nt(k, q * side) + band_s[...] for q, k in zip(qs, ks) for side in (lo, hi)]
        probs = [softmax(x) for x in scores]
        for u, (m, b) in enumerate(at):
            p0, p1 = probs[2 * u], probs[2 * u + 1]
            keep_p(m * 6 + b, 0, p0)
            keep_p(m * 6 + b, 1, p1)
            ctx_s[m, block(b), 128:256] = (dot_tn(p0, vs[u] * lo) + dot_tn(p1, vs[u] * hi)).astype(BF)
        return carry

    def attend_second(j, carry):
        at = [(j, u) for u in range(6)]
        qs, ks, vs = ([qkv_s[m, block(b), n * 128:(n + 1) * 128] for m, b in at] for n in range(3, 6))
        scores = [dot_nt(k, q * lo) + band_s[...] for q, k in zip(qs, ks)]
        probs = [softmax(x) for x in scores]
        for u, (m, b) in enumerate(at):
            keep_p(m * 6 + b, 2, probs[u])
            ctx_s[m, block(b), 0:128] = dot_tn(probs[u], vs[u] * hi).astype(BF)
        return carry

    def mid_tile(m, carry):
        w = weight(0, m, 512, 256)
        for t in range(3):
            rows = pl.ds(t * 256, 256)
            mid_s[rows, :] += dot_nt(ctx_s[m, rows, :], w)
        return carry

    def mid_block(b, carry):
        rows = block(b)
        attn = mid_s[rows, :]
        live = live_s[rows, :][:, :1]
        stats_ref[4:5, :] += jnp.sum(attn * attn * live, axis=0, keepdims=True)
        mid = x_s[rows, :].astype(F32) + attn
        mid_s[rows, :] = mid
        nm_s[b] = lnorm(mid, low_norm(2), low_norm(3)).astype(BF)
        return carry

    def transpose_into(dst, src):
        def one(b, carry):
            part = src(b)
            for j in range(6):
                dst[pl.ds(j * 128, 128), block(b)] = part[:, j * 128:(j + 1) * 128].T
            return carry

        lax.fori_loop(0, 6, one, 0)

    def cot_block(b, carry):
        live = live_s[block(b), :][:, :1]
        cot_s[b] = (cot_s[b].astype(F32) * live).astype(BF)
        return carry

    def mlp_pair(c0, nc):
        def tile(j, carry):
            pair = [2 * j, 2 * j + 1]
            w_up = [weight(1, m, c0, nc) for m in pair]
            w_down = [weight(2, m, c0, nc) for m in pair]
            for t in range(3):
                rows = pl.ds(t * 256, 256)
                normed = nm_s[2 * t:2 * t + 2].reshape(256, WIDE)
                wanted = cot_s[2 * t:2 * t + 2].reshape(256, WIDE)
                for u in range(2):
                    act, slope = gelu_pair(dot_nn(normed, w_up[u]))
                    d_act = dot_nn(wanted, w_down[u])
                    g_s[rows, u * 256:(u + 1) * 256] = act.astype(BF)
                    d_s[rows, u * 256:(u + 1) * 256] = (d_act * slope).astype(BF)
            for t in range(3):
                rows = pl.ds(t * 256, 256)
                for h in range(3):
                    cols = slice(h * 256, (h + 1) * 256)
                    for total, held, w in ((mlp_s, g_s, w_down), (dmn_s, d_s, w_up)):
                        total[rows, cols] += dot_nt(held[rows, 0:256], w[0][cols]) + dot_nt(
                            held[rows, 256:512], w[1][cols]
                        )
            for u, m in enumerate(pair):
                put(G, 2, m, c0, nc, dot_nn(dmT_s[...], g_s[:, u * 256:(u + 1) * 256]).astype(BF))
                put(G, 1, m, c0, nc, dot_nn(nmT_s[...], d_s[:, u * 256:(u + 1) * 256]).astype(BF))
            return carry

        return tile

    def end_block(b, carry):
        rows = block(b)
        live = live_s[rows, :][:, :1]
        mlp = mlp_s[rows, :]
        mid = mid_s[rows, :]
        out = (mid + mlp) * live
        stats_ref[5:6, :] += jnp.sum(mlp * mlp * live, axis=0, keepdims=True)
        stats_ref[6:7, :] += jnp.sum(out * out, axis=0, keepdims=True)
        nm_s[b] = out.astype(BF)
        e = dmn_s[rows, :]
        dv, ex = lnorm_back(mid, e, low_norm(2))
        stats_ref[2:3, :] += jnp.sum(ex, axis=0, keepdims=True)
        stats_ref[3:4, :] += jnp.sum(e, axis=0, keepdims=True)
        d_mid = cot_s[b].astype(F32) + dv
        mlp_s[rows, :] = d_mid
        cot_s[b] = d_mid.astype(BF)
        return carry

    def dctx_tile(m, carry):
        w = weight(0, m, 512, 256)
        for t in range(3):
            rows = pl.ds(t * 256, 256)
            out = dot_nn(cot_s[2 * t:2 * t + 2].reshape(256, WIDE), w)
            g_s[rows, 0:256] = out.astype(BF)
            g_s[rows, 256:384] = pltpu.roll(out[:, :128], 64, 1).astype(BF)
        return carry

    def score_back(p, d_probs):
        pf = p.astype(F32)
        w = pf * d_probs
        return (w - pf * jnp.sum(w, axis=0, keepdims=True)).astype(BF)

    def attend_back(j, carry):
        m = lax.div(j, 2)
        at = [lax.rem(j, 2) * 3 + u for u in range(3)]
        held = [[qkv_s[m, block(b), n * 128:(n + 1) * 128] for n in range(6)] for b in at]
        came = [[g_s[block(b), n * 128:(n + 1) * 128] for n in range(3)] for b in at]
        probs = [[kept_p(m * 6 + b, h) for h in range(3)] for b in at]
        d_probs = [
            [dot_nt(v, d01 * lo), dot_nt(v, d01 * hi), dot_nt(v2, d2 * hi)]
            for (q, k, v, q2, k2, v2), (d2, d01, d2r) in zip(held, came)
        ]
        d_scores = [[score_back(p, d) for p, d in zip(ps, ds)] for ps, ds in zip(probs, d_probs)]
        for b, (q, k, v, q2, k2, v2), (d2, d01, d2r), (p0, p1, p2), (s0, s1, s2) in zip(
            at, held, came, probs, d_scores
        ):
            dk = dot_nn(s0, q * lo) + dot_nn(s1, q * hi)
            dv = dot_nn(p0, d01 * lo) + dot_nn(p1, d01 * hi)
            dv2 = dot_nn(p2, d2r * lo)
            dq = dot_tn(s0, k * lo) + dot_tn(s1, k * hi)
            dqk2 = dot_tn(s2, k2 * lo) * 0.125 + dot_nn(s2, k2 * hi)
            for n, out in enumerate((dq * 0.125, dk, dv, dqk2, dv2)):
                qkv_s[m, block(b), n * 128:(n + 1) * 128] = out.astype(BF)
        return carry

    def put_all(m, c0, nc, value):
        put(PA, 0, m, c0, nc, value)

    def grad_a0(m, carry):
        put_all(m, 0, 384, dot_nn(ninT_s[...], qkv_s[m, :, 0:384]).astype(BF))
        return carry

    def grad_a1(m, carry):
        out_part = dot_nn(dmT_s[...], ctx_s[m])
        qkv_part = dot_nn(ninT_s[...], qkv_s[m, :, 384:640])
        put_all(m, 384, 128, qkv_part[:, :128].astype(BF))
        put_all(m, 512, 128, (qkv_part[:, 128:] + out_part[:, :128]).astype(BF))
        put_all(m, 640, 128, out_part[:, 128:].astype(BF))
        return carry

    def in_tile(m, carry):
        w = weight(0, m, 0, 640)
        for t in range(3):
            rows = pl.ds(t * 256, 256)
            dmn_s[rows, :] += dot_nt(qkv_s[m, rows, 0:640], w)
        return carry

    def in_block(b, carry):
        rows = block(b)
        e = dmn_s[rows, :]
        dv, ex = lnorm_back(x_s[rows, :].astype(F32), e, low_norm(0))
        stats_ref[0:1, :] += jnp.sum(ex, axis=0, keepdims=True)
        stats_ref[1:2, :] += jnp.sum(e, axis=0, keepdims=True)
        live = live_s[rows, :][:, :1]
        cot_s[b] = ((mlp_s[rows, :] + dv) * live).astype(BF)
        return carry

    def loop(first, last, body):
        if last == first + 1:
            body(jnp.int32(first), 0)
        else:
            lax.fori_loop(first, last, body, 0)

    def turn_in():
        transpose_into(ninT_s, lambda b: nin_s[block(b), :])

    def cot_start(j):
        for c in exchange(0, j):
            c.start()

    def cot_ready():
        cot_own.wait()
        for j in range(3):
            for c in exchange(0, j):
                c.wait_recv()
        loop(0, 6, cot_block)
        transpose_into(dmT_s, lambda b: cot_s[b])
        mlp_s[...] = jnp.zeros_like(mlp_s)
        dmn_s[...] = jnp.zeros_like(dmn_s)

    def middle():
        loop(0, 6, mid_block)
        transpose_into(nmT_s, lambda b: nm_s[b])

    def turn():
        dmn_s[...] = jnp.zeros_like(dmn_s)
        transpose_into(dmT_s, lambda b: cot_s[b])

    def bo_start(j):
        for c in exchange(1, j):
            c.start()
        if j == 2:
            bo_own.start()

    def ig_start(j):
        for c in exchange(2, j):
            c.start()
        if j == 2:
            ig_own.start()

    def finish():
        for k in range(len(AG_CHUNKS)):
            if AG_CHUNKS[k][0] == 0:
                ag_sent(k)
        for k in range(len(CHUNKS)):
            rs_sent(k)
            home(k).wait()
        for j in range(3):
            for c in exchange(0, j):
                c.wait_send()
            for c in (*exchange(1, j), *exchange(2, j)):
                c.wait()
        bo_own.wait()
        ig_own.wait()
        for i in range(4):
            for c in st_copies(i):
                c.wait_send()

    first_in = {
        4: (qkv_hbm, qkv_ref), 5: (out_hbm, out_ref), 6: (up_hbm, mlp_s.at[pl.ds(0, 96)]),
        7: (down_hbm, mlp_s.at[pl.ds(96, 96)]), 8: (mask_hbm, mask_ref), 9: (norm_hbm, norm_ref),
    }
    loads = {n: pltpu.make_async_copy(src, dst, loc_sem.at[n]) for n, (src, dst) in first_in.items()}
    for copy in (*loads.values(), tok_copy, cot_own):
        copy.start()
    barrier = pltpu.get_barrier_semaphore()
    greet = [device(c=1 - me["c"]), device(y=1 - me["y"]), device(x=1 - me["x"]),
             device(x=1 - me["x"], c=1 - me["c"])]
    greet += [device(z=shifted("z", n)) for n in range(1, Z)]
    for dev in greet:
        pl.semaphore_signal(barrier, inc=1, device_id=dev, device_id_type=MESH_ID)
    here = (me["x"], me["c"], me["z"], me["y"], slice(None))
    loads[4].wait()
    for t in range(3):
        G[(0, *here, pl.ds(t * 128, 128))] = qkv_ref[t, :, 0:128].astype(BF)
    pl.semaphore_wait(barrier, len(greet))

    def rest_of_first():
        last = [qkv_ref[t, :, 128:192] for t in range(3)]
        loads[5].wait()
        out_t = out_ref[...].T
        G[(0, *here, pl.ds(384, 128))] = jnp.concatenate(last[:2], axis=1).astype(BF)
        G[(0, *here, pl.ds(512, 128))] = jnp.concatenate([last[2], out_t[:, 128:192]], axis=1).astype(BF)
        G[(0, *here, pl.ds(640, 128))] = out_t[:, 0:128].astype(BF)

    def rest_of_weights():
        loads[6].wait()
        loads[7].wait()
        G[(1, *here, slice(None))] = mlp_s[0:96, :].astype(BF)
        G[(2, *here, slice(None))] = mlp_s[96:192, :].astype(BF)

    ag_own(0, 'x')
    cot_start(0)
    ag_z(0)
    rest_of_first()
    ag_z(1)
    cot_start(1)
    ag_own(0, 'y')
    rest_of_weights()
    ag_own(1, 'y')
    ag_own(2, 'x')
    setup()
    ag_own(3, 'y')
    ag_pass(0, 'y', 3)
    ag_pass(0, 'x', 2)
    tok_copy.wait()
    loop(0, 2, take_block)
    ag_pass(0, 'x', 3)
    loop(2, 4, take_block)
    ag_pass(0, 'y', 2)
    ag_pass(1, 'x', 1)
    ag_pass(0, 'y', 1)
    ag_core(0, 0)
    ag_pass(1, 'y', 2)
    ag_pass(0, 'x', 1)
    ag_own(1, 'x')
    ag_z(2)
    ag_pass(1, 'x', 3)
    ag_pass(1, 'x', 2)
    ag_pass(1, 'y', 3)
    ag_core(0, 2)
    ag_z(3)
    loop(4, 6, take_block)
    ag_last(0, 'x')
    ag_own(3, 'x')
    ag_pass(1, 'y', 1)
    ag_core(0, 1)
    ag_last(0, 'y')
    turn_in()
    ag_own(4, 'y')
    ag_core(1, 1)
    ag_last(1, 'y')
    ag_own(2, 'y')
    ag_core(1, 0)
    ag_last(1, 'x')
    ag_core(0, 3)
    ag_ready(0)
    ag_pass(2, 'x', 1)
    ag_pass(2, 'x', 2)
    loop(3, 4, qkv_first)
    loop(0, 1, qkv_first)
    ag_core(1, 2)
    ag_z(4)
    ag_pass(2, 'y', 1)
    ag_pass(3, 'x', 1)
    ag_pass(2, 'x', 3)
    loop(1, 2, qkv_first)
    ag_core(1, 3)
    cot_start(2)
    ag_pass(2, 'y', 3)
    loop(2, 4, attend_first)
    ag_core(2, 0)
    ag_ready(1)
    loop(3, 4, qkv_second)
    ag_pass(2, 'y', 2)
    ag_pass(3, 'y', 3)
    loop(1, 2, qkv_second)
    ag_pass(3, 'x', 3)
    loop(2, 3, qkv_first)
    loop(6, 8, attend_first)
    loop(1, 2, attend_second)
    ag_last(2, 'x')
    ag_core(3, 0)
    ag_pass(3, 'y', 1)
    ag_pass(3, 'x', 2)
    loop(0, 2, attend_first)
    loop(2, 3, qkv_second)
    loop(2, 3, attend_second)
    ag_pass(3, 'y', 2)
    loop(0, 1, qkv_second)
    ag_last(2, 'y')
    loop(4, 6, attend_first)
    loop(0, 1, attend_second)
    ag_pass(4, 'x', 3)
    cot_ready()
    loop(0, 2, mid_tile)
    ag_core(2, 2)
    loop(3, 4, attend_second)
    ag_pass(4, 'y', 1)
    loop(2, 3, mid_tile)
    ag_core(2, 1)
    ag_last(3, 'x')
    ag_last(3, 'y')
    loop(3, 4, mid_tile)
    ag_core(2, 3)
    ag_pass(4, 'y', 3)
    ag_pass(4, 'x', 2)
    ag_core(3, 2)
    ag_core(3, 1)
    ag_own(4, 'x')
    middle()
    ag_core(4, 0)
    ag_ready(2)
    ag_pass(4, 'x', 1)
    ag_sent(2)
    loop(0, 1, mlp_pair(0, 256))
    ag_pass(4, 'y', 2)
    ag_core(3, 3)
    loop(1, 2, mlp_pair(0, 256))
    rs_core(2, 1)
    ag_last(4, 'x')
    ag_core(4, 2)
    rs_core(2, 3)
    rs_core(2, 2)
    ag_ready(3)
    rs_core(2, 0)
    ag_last(4, 'y')
    ag_sent(3)
    loop(0, 1, mlp_pair(256, 256))
    ag_core(4, 1)
    rs_add_core(2, 3)
    rs_add_core(2, 2)
    rs_first(2, 'y')
    rs_add_core(2, 1)
    rs_diag_z(2)
    ag_core(4, 3)
    loop(1, 2, mlp_pair(256, 256))
    rs_core(3, 3)
    ag_ready(4)
    rs_core(3, 1)
    rs_side(2, 'y', 1)
    ag_sent(4)
    loop(0, 1, mlp_pair(512, 256))
    rs_add_first(2, 'y')
    rs_side(2, 'x', 2)
    rs_side(2, 'x', 3)
    rs_core(3, 2)
    rs_side(2, 'x', 1)
    rs_add_core(3, 3)
    rs_first(3, 'y')
    rs_side(2, 'y', 2)
    loop(1, 2, mlp_pair(512, 256))
    rs_diag_z(3)
    rs_core(3, 0)
    loop(0, 2, end_block)
    rs_core(4, 3)
    bo_start(0)
    rs_core(4, 2)
    rs_core(4, 1)
    rs_side(2, 'y', 3)
    rs_add_core(2, 0)
    rs_add_core(3, 1)
    rs_add_diag_z(2)
    loop(2, 4, end_block)
    rs_add_first(3, 'y')
    loop(4, 6, end_block)
    rs_side(3, 'x', 1)
    rs_add_side(2, 2)
    rs_add_core(4, 3)
    rs_diag_z(4)
    rs_first(4, 'y')
    rs_add_core(3, 2)
    rs_side(3, 'x', 2)
    bo_start(2)
    loop(0, 1, dctx_tile)
    turn()
    rs_add_core(4, 2)
    rs_add_side(2, 3)
    rs_add_core(3, 0)
    rs_side(3, 'y', 1)
    loop(0, 2, attend_back)
    loop(1, 2, dctx_tile)
    bo_start(1)
    rs_side(3, 'x', 3)
    rs_core(4, 0)
    loop(2, 4, attend_back)
    rs_z(2, 2)
    loop(2, 3, dctx_tile)
    rs_side(4, 'y', 1)
    rs_add_side(2, 1)
    rs_side(3, 'y', 3)
    loop(4, 6, attend_back)
    rs_add_side(3, 1)
    rs_side(4, 'y', 2)
    rs_z(3, 1)
    loop(3, 4, dctx_tile)
    loop(6, 8, attend_back)
    loop(2, 3, grad_a1)
    rs_z(2, 1)
    rs_diag(2)
    rs_add_core(4, 1)
    loop(3, 4, grad_a1)
    loop(1, 2, grad_a1)
    rs_z(2, 3)
    rs_side(4, 'y', 3)
    loop(0, 1, grad_a1)
    rs_core(1, 3)
    rs_add_first(4, 'y')
    rs_side(4, 'x', 2)
    loop(0, 1, grad_a0)
    loop(2, 3, grad_a0)
    rs_add_core(1, 3)
    rs_diag_z(1)
    rs_first(1, 'y')
    rs_core(1, 2)
    rs_side(4, 'x', 1)
    loop(3, 4, grad_a0)
    rs_side(4, 'x', 3)
    rs_add_diag(2)
    rs_core(1, 1)
    loop(1, 2, grad_a0)
    rs_add_side(3, 3)
    rs_z(3, 3)
    rs_core(0, 3)
    rs_add_diag_z(3)
    rs_side(3, 'y', 0)
    rs_core(0, 0)
    rs_add_core(4, 0)
    rs_add_core(1, 1)
    loop(0, 1, in_tile)
    rs_side(2, 'x', 0)
    rs_add_core(0, 3)
    rs_add_side(4, 2)
    rs_diag_z(0)
    rs_add_first(1, 'y')
    rs_first(0, 'y')
    rs_add_core(1, 2)
    rs_core(0, 1)
    rs_diag(3)
    rs_side(1, 'x', 2)
    loop(3, 4, in_tile)
    rs_side(1, 'x', 1)
    loop(2, 3, in_tile)
    rs_side(1, 'x', 3)
    rs_core(1, 0)
    loop(1, 2, in_tile)
    rs_add_side(4, 1)
    rs_z(4, 2)
    rs_side(1, 'y', 1)
    rs_core(0, 2)
    rs_add_core(0, 0)
    rs_add_core(0, 1)
    loop(0, 2, in_block)
    rs_add_first(0, 'y')
    rs_side(0, 'x', 2)
    rs_side(1, 'y', 2)
    loop(2, 6, in_block)
    rs_add_core(0, 2)
    rs_z(4, 1)
    rs_side(0, 'y', 1)
    st_step(0)
    ig_start(2)
    rs_add_side(4, 3)
    st_step(1)
    rs_side(0, 'x', 3)
    rs_add_diag_z(4)
    rs_side(3, 'y', 2)
    rs_side(1, 'y', 3)
    rs_add_core(1, 0)
    rs_add_diag_z(1)
    rs_diag(4)
    rs_side(0, 'y', 2)
    rs_add_side(1, 1)
    rs_z(4, 3)
    st_step(2)
    ig_start(1)
    rs_side(0, 'x', 1)
    rs_add_side(1, 2)
    rs_z(1, 1)
    rs_add_diag(3)
    rs_add_diag_z(0)
    rs_diag(0)
    rs_z(1, 2)
    rs_side(0, 'y', 3)
    rs_diag(1)
    rs_add_diag(4)
    rs_add_side(3, 2)
    st_step(3)
    rs_side(1, 'y', 0)
    rs_side(2, 'y', 0)
    rs_add_side(0, 2)
    rs_side(4, 'x', 0)
    rs_add_diag(0)
    rs_z(3, 2)
    rs_add_diag(1)
    rs_side(1, 'x', 0)
    rs_add_side(1, 3)
    ig_start(0)
    rs_add_side(0, 1)
    rs_add_side(0, 3)
    rs_z(0, 3)
    st_step(4)
    rs_final(2)
    rs_z(1, 3)
    rs_z(0, 1)
    rs_side(3, 'x', 0)
    rs_side(0, 'x', 0)
    rs_side(4, 'y', 0)
    rs_side(0, 'y', 0)
    rs_z(0, 2)
    rs_final(3)
    rs_final(4)
    rs_final(1)
    rs_final(0)
    finish()


def fits_fused(mesh):
    return mesh.shape["dp"] == 8 and mesh.shape["mp"] == 4


def renew_kernel(count, grads, bo, ig, stats, *rest):
    ins, (bo_new, ig_new, rms), news = rest[:15], rest[15:18], rest[18:]

    def rows(t, carry):
        for b in range(bo.shape[1]):
            bo_new[t, b] = bo[t, b].astype(F32)
            ig_new[t, b] = ig[t, b].astype(F32)
        return carry

    lax.fori_loop(0, bo.shape[0], rows, 0)
    size = jnp.sqrt(jnp.sum(stats[...], axis=1, keepdims=True) / count)
    for n in range(3):
        rms[n] = size[4 + n, 0]

    def step(n, at, gradient, rate):
        weight, momentum, average = (ref[at] for ref in ins[3 * n:3 * n + 3])
        for ref, value in zip(news[4 * n:4 * n + 4], renew_weight(weight, momentum, average, gradient, rate)):
            ref[at] = value

    whole = slice(None)
    for t in range(3):
        step(0, (t, whole, pl.ds(0, 128)), grads[0, :, 128 * t:128 * t + 128], MATRIX_RATE)
        step(0, (t, whole, pl.ds(128, 64)), grads[0, :, 384 + 64 * t:448 + 64 * t], MATRIX_RATE)
    step(1, (pl.ds(0, 128), whole), grads[0, :, 640:768].T, OUTPUT_RATE)
    step(1, (pl.ds(128, 64), whole), grads[0, :, 512:640].T[64:], OUTPUT_RATE)
    step(2, (whole, whole), grads[1], MATRIX_RATE)
    step(3, (whole, whole), grads[2], MATRIX_RATE)
    step(4, (whole, whole), stats[0:4], NORM_RATE)


def local_fused(
    tokens,
    visible_mask,
    cotangent,
    qkv_weight,
    qkv_momentum,
    qkv_average,
    out_weight,
    out_momentum,
    out_average,
    up_weight,
    up_momentum,
    up_average,
    down_weight,
    down_momentum,
    down_average,
    norm_params,
    norm_momentum,
    norm_average,
):
    data_size = lax.axis_size("dp")
    model_size = lax.axis_size("mp")
    slots, patches, width = tokens.shape
    quarter = cotangent.shape[1]
    sizes = (model_size // 2, 2, data_size // 2, 2)
    X, C, Z, Y = sizes
    blocks = slots // (4 * model_size)
    group = blocks * 32
    bufs = [pltpu.VMEM(shape, BF) for k in range(len(CHUNKS)) for _, shape in rs_buffers(k)]
    n_chunk = len(CHUNKS)
    rows = blocks * 128
    vmem = pltpu.VMEM
    dma = pltpu.SemaphoreType.DMA
    scratch = [
        vmem((3, X, C, Z, Y, 96, WIDE), BF),
        vmem((1, X, C, Z, Y, 96, WIDE), BF),
        vmem((3, X, 1, Z, Y, 96, WIDE), BF),
        *bufs,
        vmem((24 * patches, WIDE), BF),
        vmem((patches, slots), BF),
        vmem((rows, 128), F32),
        vmem((128, 128), F32),
        vmem((rows, WIDE), BF),
        vmem((rows, WIDE), BF),
        vmem((4, rows, WIDE), BF),
        vmem((4, rows, 256), BF),
        vmem((rows, WIDE), F32),
        vmem((blocks, 128, WIDE), BF),
        vmem((WIDE, rows), BF),
        vmem((WIDE, rows), BF),
        vmem((blocks, 128, WIDE), BF),
        vmem((WIDE, rows), BF),
        vmem((rows, 512), BF),
        vmem((rows, 512), BF),
        vmem((rows, WIDE), F32),
        vmem((rows, WIDE), F32),
        vmem((4, 8, WIDE), F32),
        vmem((6, 8, WIDE), F32),
        vmem((patches, slots), jnp.int32),
        vmem(qkv_weight.shape, F32),
        vmem(out_weight.shape, F32),
        vmem(norm_params.shape, F32),
        vmem((3, 96, WIDE), F32),
        dma((10,)),
        dma((n_chunk,)),
        dma((len(AG_CHUNKS), 21)),
        dma((len(AG_CHUNKS), 21)),
        dma((n_chunk, 21)),
        dma((n_chunk, 21)),
        dma((3, 3, 3)),
        dma((3, 3, 3)),
        dma((6,)),
        dma((6,)),
    ]
    in_vmem = pl.BlockSpec(memory_space=pltpu.VMEM)
    anywhere = pl.BlockSpec(memory_space=pl.ANY)
    grads, bo, ig, stats = pl.pallas_call(
        functools.partial(layer_kernel, sizes),
        out_shape=(
            jax.ShapeDtypeStruct((3, 96, WIDE), F32),
            jax.ShapeDtypeStruct((model_size, blocks, 32, WIDE), BF),
            jax.ShapeDtypeStruct((model_size, blocks, 32, WIDE), BF),
            jax.ShapeDtypeStruct((8, WIDE), F32),
        ),
        in_specs=[anywhere] * 8,
        out_specs=(anywhere, anywhere, anywhere, in_vmem),
        scratch_shapes=scratch,
        compiler_params=pltpu.CompilerParams(
            collective_id=0, has_side_effects=True, vmem_limit_bytes=VMEM_BYTES
        ),
        name="layer",
    )(
        tokens.reshape(slots * patches, width),
        visible_mask.T,
        cotangent.reshape(model_size, blocks, 32, width),
        qkv_weight,
        out_weight,
        up_weight,
        down_weight.T,
        norm_params,
    )
    visible_count = quarter * model_size
    triples = (
        (qkv_weight, qkv_momentum, qkv_average),
        (out_weight, out_momentum, out_average),
        (up_weight, up_momentum, up_average),
        (down_weight.T, down_momentum.T, down_average.T),
        (norm_params, norm_momentum, norm_average),
    )
    shares = jax.ShapeDtypeStruct((model_size, blocks, 32, width), F32)
    news = []
    for weight, _, _ in triples:
        news += [jax.ShapeDtypeStruct(weight.shape, F32)] * 3 + [jax.ShapeDtypeStruct(weight.shape, BF)]
    block_out, input_grad, rms, *new = pl.pallas_call(
        functools.partial(renew_kernel, visible_count * data_size * FLD_DEV * width),
        out_shape=(shares, shares, jax.ShapeDtypeStruct((3,), F32), *news),
        in_specs=[in_vmem] * (4 + 3 * len(triples)),
        out_specs=(in_vmem, in_vmem, pl.BlockSpec(memory_space=pltpu.SMEM)) + (in_vmem,) * len(news),
        compiler_params=pltpu.CompilerParams(vmem_limit_bytes=VMEM_BYTES),
        name="renew",
    )(grads, bo, ig, stats, *(array for triple in triples for array in triple))
    block_out = block_out.reshape(slots, quarter, width)
    input_grad = input_grad.reshape(slots, quarter, width)
    new[12:16] = [array.T for array in new[12:16]]
    return (block_out, input_grad, rms, *new)


def local_general(
    tokens,
    visible_mask,
    cotangent,
    qkv_weight,
    qkv_momentum,
    qkv_average,
    out_weight,
    out_momentum,
    out_average,
    up_weight,
    up_momentum,
    up_average,
    down_weight,
    down_momentum,
    down_average,
    norm_params,
    norm_momentum,
    norm_average,
):
    data_size = lax.axis_size("dp")
    model_size = lax.axis_size("mp")
    data_rank = lax.axis_index("dp")
    model_rank = lax.axis_index("mp")
    slot_count, patch_count, feature_count = tokens.shape
    quarter = cotangent.shape[1]
    visible_count = quarter * model_size
    capacity = (slot_count + data_size - 1) // data_size
    owned_fields = FLD_DEV
    pad_total = data_size * capacity
    per_field = jnp.sum(visible_mask, axis=1)
    field_total = jnp.sum(per_field) // visible_count
    all_fields = lax.all_gather(field_total.reshape(1), "dp", axis=0, tiled=True)
    firsts = jnp.cumsum(all_fields) - all_fields
    my_first = firsts[data_rank]
    patch_ids = jnp.arange(patch_count, dtype=jnp.int32)
    sort_keys = (1 - visible_mask) * patch_count + patch_ids[None, :]
    ranked = jnp.argsort(sort_keys, axis=1)
    my_order = lax.dynamic_slice_in_dim(ranked, model_rank * quarter, quarter, 1)
    visible = jnp.take_along_axis(tokens, my_order[:, :, None], axis=1)
    owner_ids = jnp.arange(data_size, dtype=jnp.int32)[:, None]
    slot_ids = jnp.arange(capacity, dtype=jnp.int32)[None, :]
    source_field = slot_ids * data_size + (owner_ids - my_first) % data_size
    send_live = (source_field < field_total).reshape(-1)[:, None, None]
    source_pick = jnp.minimum(source_field, slot_count - 1).reshape(-1)
    sent_rows = jnp.where(send_live, visible[source_pick], jnp.zeros((), jnp.bfloat16))
    sent_grads = jnp.where(send_live, cotangent[source_pick], jnp.zeros((), jnp.bfloat16))
    got_rows, got_grads = (
        lax.all_to_all(sent_rows, "dp", split_axis=0, concat_axis=0, tiled=True),
        lax.all_to_all(sent_grads, "dp", split_axis=0, concat_axis=0, tiled=True),
    )
    arrive = slot_ids * data_size + (data_rank - firsts[:, None]) % data_size
    flat_live = (arrive < all_fields[:, None]).reshape(-1)
    order_keys = jnp.where(flat_live, 0, pad_total) + jnp.arange(pad_total, dtype=jnp.int32)
    chosen = jnp.argsort(order_keys)[:owned_fields]
    share_rows = owned_fields * quarter
    mine_rows = got_rows[chosen].reshape(share_rows, feature_count)
    mine_grads = got_grads[chosen].reshape(share_rows, feature_count)
    w_qkv, w_out, w_up, w_down = (
        lax.all_gather(qkv_weight.astype(jnp.bfloat16), "dp", axis=1, tiled=True),
        lax.all_gather(out_weight.astype(jnp.bfloat16), "dp", axis=1, tiled=True),
        lax.all_gather(up_weight.astype(jnp.bfloat16), "dp", axis=0, tiled=True),
        lax.all_gather(down_weight.astype(jnp.bfloat16), "dp", axis=1, tiled=True),
    )
    norm_low = lax.optimization_barrier(norm_params.astype(jnp.bfloat16)).astype(jnp.float32)
    total_rows = share_rows * model_size
    local_width = w_qkv.shape[2]
    head_local = local_width // HDIM
    score_scale = HDIM ** (-0.5)
    x_share = mine_rows.astype(jnp.float32)
    normed_share, norm_in_back = jax.vjp(layer_norm, x_share, norm_low[0], norm_low[1])
    normed_all = lax.all_gather(normed_share.astype(jnp.bfloat16), "mp", axis=0, tiled=True)
    qkv_rows = jnp.einsum(
        "rd,tde->tre", normed_all, w_qkv, preferred_element_type=jnp.float32
    ).astype(jnp.bfloat16)
    qkv_six = qkv_rows.reshape(3, model_size, owned_fields, quarter, head_local, HDIM)
    queries = qkv_six[0]
    key_rows = qkv_six[1]
    values = qkv_six[2]
    scores = (
        jnp.einsum("afbhe,cfdhe->fhabcd", queries, key_rows, preferred_element_type=jnp.float32)
        * score_scale
    )
    scores = scores.reshape(owned_fields, head_local, visible_count, visible_count)
    attention = jax.nn.softmax(scores, axis=-1)
    att_six = attention.astype(jnp.bfloat16).reshape(
        owned_fields, head_local, model_size, quarter, model_size, quarter
    )
    context = jnp.einsum("fhabcd,cfdhe->afbhe", att_six, values, preferred_element_type=jnp.float32)
    context = context.astype(jnp.bfloat16).reshape(total_rows, local_width)
    attn_share = lax.psum_scatter(
        jnp.dot(context, w_out, preferred_element_type=jnp.float32).astype(jnp.bfloat16),
        "mp",
        scatter_dimension=0,
        tiled=True,
    ).astype(jnp.float32)
    mid_share = x_share + attn_share
    normed_mid, norm_mid_back = jax.vjp(layer_norm, mid_share, norm_low[2], norm_low[3])
    mid_all, grad_all = (
        lax.all_gather(normed_mid.astype(jnp.bfloat16), "mp", axis=0, tiled=True),
        lax.all_gather(mine_grads, "mp", axis=0, tiled=True),
    )
    pre_act = jnp.dot(mid_all, w_up, preferred_element_type=jnp.float32)
    gelu_float, gelu_back = jax.vjp(gelu_exact, pre_act)
    gelu_out = gelu_float.astype(jnp.bfloat16)
    mlp_share = lax.psum_scatter(
        jnp.dot(gelu_out, w_down, preferred_element_type=jnp.float32).astype(jnp.bfloat16),
        "mp",
        scatter_dimension=0,
        tiled=True,
    ).astype(jnp.float32)
    out_share = mid_share + mlp_share
    squares = jnp.stack(
        [
            jnp.sum(attn_share * attn_share),
            jnp.sum(mlp_share * mlp_share),
            jnp.sum(out_share * out_share),
        ]
    )
    grad_down = jnp.einsum("rf,rd->fd", gelu_out, grad_all, preferred_element_type=jnp.float32)
    d_act = jnp.einsum("rd,fd->rf", grad_all, w_down, preferred_element_type=jnp.float32)
    d_pre = gelu_back(d_act)[0].astype(jnp.bfloat16)
    grad_up = jnp.einsum("rd,rf->df", mid_all, d_pre, preferred_element_type=jnp.float32)
    d_mid_norm = lax.psum_scatter(
        jnp.einsum("rf,df->rd", d_pre, w_up, preferred_element_type=jnp.float32).astype(
            jnp.bfloat16
        ),
        "mp",
        scatter_dimension=0,
        tiled=True,
    ).astype(jnp.float32)
    d_mid_part, grad_gain_mid, grad_shift_mid = norm_mid_back(d_mid_norm)
    d_middle = mine_grads.astype(jnp.float32) + d_mid_part
    d_att_all = lax.all_gather(d_middle.astype(jnp.bfloat16), "mp", axis=0, tiled=True)
    grad_out = jnp.einsum("rc,rd->cd", context, d_att_all, preferred_element_type=jnp.float32)
    d_context = jnp.einsum(
        "rd,cd->rc", d_att_all, w_out, preferred_element_type=jnp.float32
    ).astype(jnp.bfloat16)
    d_ctx_six = d_context.reshape(model_size, owned_fields, quarter, head_local, HDIM)
    d_probs = jnp.einsum(
        "afbhe,cfdhe->fhabcd", d_ctx_six, values, preferred_element_type=jnp.float32
    )
    d_probs = d_probs.reshape(owned_fields, head_local, visible_count, visible_count)
    d_values = jnp.einsum(
        "fhabcd,afbhe->cfdhe", att_six, d_ctx_six, preferred_element_type=jnp.float32
    )
    d_scores = (
        attention * (d_probs - jnp.sum(d_probs * attention, axis=-1, keepdims=True))
    ).astype(jnp.bfloat16)
    d_six = d_scores.reshape(owned_fields, head_local, model_size, quarter, model_size, quarter)
    d_queries = (
        jnp.einsum("fhabcd,cfdhe->afbhe", d_six, key_rows, preferred_element_type=jnp.float32)
        * score_scale
    )
    d_keys = (
        jnp.einsum("fhabcd,afbhe->cfdhe", d_six, queries, preferred_element_type=jnp.float32)
        * score_scale
    )
    d_qkv = (
        jnp.stack([d_queries, d_keys, d_values])
        .astype(jnp.bfloat16)
        .reshape(3, total_rows, local_width)
    )
    grad_qkv = jnp.einsum("rd,tre->tde", normed_all, d_qkv, preferred_element_type=jnp.float32)
    d_in_norm = lax.psum_scatter(
        jnp.einsum("tre,tde->rd", d_qkv, w_qkv, preferred_element_type=jnp.float32).astype(
            jnp.bfloat16
        ),
        "mp",
        scatter_dimension=0,
        tiled=True,
    ).astype(jnp.float32)
    d_in_part, grad_gain_in, grad_shift_in = norm_in_back(d_in_norm)
    d_input = d_middle + d_in_part
    gradients = (grad_qkv, grad_out, grad_up, grad_down)
    summed = lax.psum((gradients[0], gradients[1], gradients[2], gradients[3]), "dp")
    qkv_grad = lax.dynamic_slice_in_dim(
        summed[0], data_rank * qkv_weight.shape[1], qkv_weight.shape[1], 1
    )
    out_grad = lax.dynamic_slice_in_dim(
        summed[1], data_rank * out_weight.shape[1], out_weight.shape[1], 1
    )
    up_grad = lax.dynamic_slice_in_dim(
        summed[2], data_rank * up_weight.shape[0], up_weight.shape[0], 0
    )
    down_grad = lax.dynamic_slice_in_dim(
        summed[3], data_rank * down_weight.shape[1], down_weight.shape[1], 1
    )

    def spread_back(share_block):
        padded = jnp.zeros((pad_total, quarter, feature_count), jnp.float32)
        return padded.at[chosen].set(share_block.reshape(owned_fields, quarter, feature_count))

    back_out, back_grad = (
        lax.all_to_all(
            spread_back(out_share).astype(jnp.bfloat16),
            "dp",
            split_axis=0,
            concat_axis=0,
            tiled=True,
        ).astype(jnp.float32),
        lax.all_to_all(
            spread_back(d_input).astype(jnp.bfloat16), "dp", split_axis=0, concat_axis=0, tiled=True
        ).astype(jnp.float32),
    )
    field_ids = jnp.arange(slot_count, dtype=jnp.int32)
    home_slot = (my_first + field_ids) % data_size * capacity + field_ids // data_size
    field_live = (field_ids < field_total)[:, None, None]
    block_out = jnp.where(field_live, back_out[home_slot], 0.0)
    input_grad = jnp.where(field_live, back_grad[home_slot], 0.0)
    norm_grad = jnp.stack([grad_gain_in, grad_shift_in, grad_gain_mid, grad_shift_mid])
    totals, norm_grad = lax.psum((squares, norm_grad), ("dp", "mp"))
    branch_rms = jnp.sqrt(totals / (visible_count * data_size * FLD_DEV * feature_count))
    qkv_new = renew_weight(qkv_weight, qkv_momentum, qkv_average, qkv_grad, MATRIX_RATE)
    out_new = renew_weight(out_weight, out_momentum, out_average, out_grad, OUTPUT_RATE)
    up_new = renew_weight(up_weight, up_momentum, up_average, up_grad, MATRIX_RATE)
    down_new = renew_weight(down_weight, down_momentum, down_average, down_grad, MATRIX_RATE)
    norm_new = renew_weight(norm_params, norm_momentum, norm_average, norm_grad, NORM_RATE)
    return (
        block_out,
        input_grad,
        branch_rms,
        qkv_new[0],
        qkv_new[1],
        qkv_new[2],
        qkv_new[3],
        out_new[0],
        out_new[1],
        out_new[2],
        out_new[3],
        up_new[0],
        up_new[1],
        up_new[2],
        up_new[3],
        down_new[0],
        down_new[1],
        down_new[2],
        down_new[3],
        norm_new[0],
        norm_new[1],
        norm_new[2],
        norm_new[3],
    )


def solution(mesh):
    in_specs = (
        P("dp", None, None),
        P("dp", None),
        P("dp", "mp", None),
        P(None, "dp", "mp"),
        P(None, "dp", "mp"),
        P(None, "dp", "mp"),
        P("mp", "dp"),
        P("mp", "dp"),
        P("mp", "dp"),
        P("dp", "mp"),
        P("dp", "mp"),
        P("dp", "mp"),
        P("mp", "dp"),
        P("mp", "dp"),
        P("mp", "dp"),
        P(),
        P(),
        P(),
    )
    out_specs = (
        P("dp", "mp", None),
        P("dp", "mp", None),
        P(),
        P(None, "dp", "mp"),
        P(None, "dp", "mp"),
        P(None, "dp", "mp"),
        P(None, "dp", "mp"),
        P("mp", "dp"),
        P("mp", "dp"),
        P("mp", "dp"),
        P("mp", "dp"),
        P("dp", "mp"),
        P("dp", "mp"),
        P("dp", "mp"),
        P("dp", "mp"),
        P("mp", "dp"),
        P("mp", "dp"),
        P("mp", "dp"),
        P("mp", "dp"),
        P(),
        P(),
        P(),
        P(),
    )
    local = local_fused if fits_fused(mesh) else local_general
    return jax.shard_map(local, mesh=mesh, in_specs=in_specs, out_specs=out_specs, check_vma=False)
```
